32 devices in a mesh: user: 8 (over z, x), grp: 4 (over y, core).
Axes of the slice: x: 2, y: 2, z: 4, core: 2. Of those that a mesh axis runs over, the one named last changes fastest.
Arguments:
- user_factors: bfloat16 [32768, 128], P(('user', 'grp')), may hold values from -0.4 to 0.4
- tile_user: int32 [32, 384, 128], P(('user', 'grp')), may hold values from 0 to 1023
- tile_count: int32 [32, 384, 128], P(('user', 'grp')), may hold values from 1 to 8
- tile_valid: int32 [32, 384], P(('user', 'grp')), may hold values from 1 to 128
- tile_item: int32 [32, 384], P(('user', 'grp')), may hold values from 0 to 127, never falling along the last dimension, each value on 1 to 32 neighbouring positions
- prev_items: float32 [128, 128], P(('user', 'grp')), may hold values from -2 to 2
Outputs:
- item_factors: float32 [128, 128], P(('user', 'grp'))
- user_rhs: float32 [32768, 128], P(('user', 'grp'))
The draws below stay inside these ranges and needn't reach their ends.
Inputs may be any that keep to these rules, and one draw needn't show every extreme that they name: `tile_item`: within the tiles of one user block the item ids never fall, and every item has 1 to 32 tiles in every user block.
All inputs are finite; a program needn't handle non-finite values.
Results may differ from the reference program's by a relative error of at most 0.0021.
Values may be sent and summed in bfloat16 or wider, within the bound.
No kernel may reach another device: no remote copies, remote signals or barrier semaphores. Data moves between devices by JAX's collectives and lax.ppermute only.
A program may use at most 128 MiB of HBM per device.

```python
import math
import jax
import jax.numpy as jnp
import numpy as np
from jax import lax

R = 128
TILE = 128
UB = 1024
TILES = 384
ITEMS = 128
MOST = 32
CG_STEPS = 4
USERS = 32768
N_USER = 8
N_GRP = 4
DEVICES = 32


def draw_user_factors(key, part):
    column_scale = jnp.exp(jax.random.uniform(jax.random.fold_in(key, 11), (R,), jnp.float32, math.log(0.004), math.log(0.04)))
    position = jnp.arange(USERS, dtype=jnp.float32) / USERS
    base_draw = jnp.clip(jax.random.normal(jax.random.fold_in(key, 13), (USERS, R), jnp.float32), -5.0, 5.0)
    row_scale = 0.6 + 1.2 * position
    return (base_draw * row_scale[:, None] * column_scale[None, :]).astype(jnp.bfloat16)


def touch_ends(drawn, own_key, smallest, high):
    place = [jax.random.randint(jax.random.fold_in(own_key, axis), (), 0, length) for axis, length in enumerate(drawn.shape)]
    main_axis = drawn.shape.index(max(drawn.shape))
    next_to = place[:main_axis] + [(place[main_axis] + 1) % drawn.shape[main_axis]] + place[main_axis + 1:]
    return drawn.at[tuple(place)].set(smallest).at[tuple(next_to)].set(high)


def block_levels(key, shape, split, smallest, high):
    loudness = 1.0
    for dim, parts in split:
        heights = jax.random.uniform(jax.random.fold_in(jax.random.fold_in(key, 6), dim), (parts,), jnp.float32, smallest / len(split), high / len(split))
        loudness = loudness * jnp.repeat(jnp.exp(heights), shape[dim] // parts).reshape((-1,) + (1,) * (len(shape) - 1 - dim))
    return loudness


def split_up(count, total, limit, skew):
    weights = [(1 << 20) // math.isqrt(rank ** skew) + 1 for rank in range(2, count + 1)]
    surplus, given = total - limit - (count - 1), [1] * (count - 1)
    while surplus > 0:
        movable = [i for i in range(count - 1) if given[i] < limit]
        whole, left = sum([weights[i] for i in movable]), surplus
        for i in movable:
            extra = min(limit - given[i], max(1, left * weights[i] // whole), surplus)
            given[i] = given[i] + extra
            surplus = surplus - extra
    return np.array([limit] + given)


def ragged(stream_key, amount, total, reach, skew):
    if amount == 2:
        one = jax.random.randint(stream_key, (), max(1, total - reach), min(reach, total - 1) + 1)
        return jnp.stack([one, total - one])
    tallies = jnp.asarray(split_up(amount, total, reach, skew), jnp.int32)
    pairs = (amount - 1) // 2
    giver, taker = tallies[1:1 + 2 * pairs:2], tallies[2:2 + 2 * pairs:2]
    room = jnp.minimum(giver - 1, reach - taker)
    passed = jax.random.randint(jax.random.fold_in(stream_key, 1), (pairs,), 0, 1 << 20) % (room + 1)
    tallies = tallies.at[1:1 + 2 * pairs:2].set(giver - passed).at[2:2 + 2 * pairs:2].set(taker + passed)
    return tallies[jax.random.permutation(jax.random.fold_in(stream_key, 2), amount)]


def centred(rng, dims, width, limit, split=(), kind=jnp.bfloat16):
    level = block_levels(rng, dims, split, -0.22, 0.18) if split else 1.0
    values = jax.random.normal(rng, dims, jnp.float32) * width * level
    return jnp.minimum(jnp.maximum(values, -limit), limit).astype(kind)


def setup_inputs(seed: int = 0) -> dict:
    key_of = jax.random.split(jax.random.key(seed), 7)
    user_factors = draw_user_factors(jax.random.fold_in(key_of[6], 71), 0)
    tile_user = touch_ends(jax.random.randint(key_of[1], (DEVICES, TILES, TILE), 0, UB), jax.random.fold_in(key_of[1], 1), 0, UB - 1).astype(jnp.int32)
    tile_count = touch_ends(jax.random.randint(key_of[2], (DEVICES, TILES, TILE), 1, 9), jax.random.fold_in(key_of[2], 1), 1, 8).astype(jnp.int32)
    tile_valid = touch_ends(jax.random.randint(key_of[3], (DEVICES, TILES), 1, TILE + 1), jax.random.fold_in(key_of[3], 1), 1, TILE).astype(jnp.int32)
    tile_item = jax.vmap(lambda own: jnp.searchsorted(jnp.cumsum(ragged(own, ITEMS, TILES, MOST, 2)), jnp.arange(TILES), side="right"))(jax.random.split(key_of[4], DEVICES)).reshape((DEVICES, TILES)).astype(jnp.int32)
    prev_items = centred(key_of[5], (ITEMS, R), 0.3, 2.0, ((0, 32),), jnp.float32)
    return dict(user_factors=user_factors, tile_user=tile_user, tile_count=tile_count, tile_valid=tile_valid, tile_item=tile_item, prev_items=prev_items)


confidence_rate = 0.5
ridge_weight = 1.0


def tile_weights(counts, valid):
    positions = lax.broadcasted_iota(jnp.int32, counts.shape, counts.ndim - 1)
    live_rows = positions < valid[..., None]
    excess = jnp.where(live_rows, confidence_rate * counts.astype(jnp.float32), jnp.float32(0.0))
    confidence = jnp.where(live_rows, 1.0 + excess, jnp.float32(0.0))
    return excess, confidence


def conjugate(system, rhs_total, start):
    def apply_system(vector):
        return jnp.einsum("iab,ib->ia", system, vector, precision=lax.Precision.HIGHEST)

    solution = start
    residual = rhs_total - apply_system(solution)
    direction = residual
    norm_now = jnp.sum(residual * residual, axis=1, keepdims=True)
    for iteration in range(CG_STEPS):
        product_vec = apply_system(direction)
        step_size = norm_now / jnp.sum(direction * product_vec, axis=1, keepdims=True)
        solution = solution + step_size * direction
        residual = residual - step_size * product_vec
        norm_next = jnp.sum(residual * residual, axis=1, keepdims=True)
        direction = residual + (norm_next / norm_now) * direction
        norm_now = norm_next
    return solution


def reference(user_factors, tile_user, tile_count, tile_valid, tile_item, prev_items):
    blocks = N_USER * N_GRP
    own_factors = user_factors.reshape(blocks, UB, R)

    def block_terms(totals, scanned):
        slab_gram, slab_rhs = totals
        factors, users, counts, valid, item_ids = scanned
        excess, confidence = tile_weights(counts, valid)
        gathered = factors[users].astype(jnp.float32)
        weighted = lax.optimization_barrier((excess[..., None] * gathered).astype(jnp.bfloat16)).astype(jnp.float32)
        part_gram = jnp.einsum("tra,trb->tab", gathered, weighted)
        part_rhs = jnp.einsum("tr,tra->ta", confidence, gathered)
        slab_gram = slab_gram + jax.ops.segment_sum(part_gram, item_ids, num_segments=ITEMS)
        slab_rhs = slab_rhs + jax.ops.segment_sum(part_rhs, item_ids, num_segments=ITEMS)
        return (slab_gram, slab_rhs), None

    initial = (jnp.zeros((ITEMS, R, R), jnp.float32), jnp.zeros((ITEMS, R), jnp.float32))
    (slab_gram, slab_rhs), _ = lax.scan(block_terms, initial, (own_factors, tile_user, tile_count, tile_valid, tile_item))
    user_gram = jnp.dot(user_factors.T, user_factors, preferred_element_type=jnp.float32)
    identity = jnp.eye(R, dtype=jnp.float32)
    system = slab_gram + user_gram[None] + ridge_weight * identity[None]
    item_factors = conjugate(system, slab_rhs, prev_items)
    returned = lax.optimization_barrier(item_factors.astype(jnp.bfloat16)).astype(jnp.float32)

    def block_rhs(scanned):
        users, counts, valid, item_ids = scanned
        excess, confidence = tile_weights(counts, valid)
        index = (users * ITEMS + item_ids[:, None]).astype(jnp.int32).reshape(-1)
        weights = jax.ops.segment_sum(confidence.reshape(-1), index, num_segments=UB * ITEMS).reshape(UB, ITEMS)
        return jnp.dot(weights, returned, precision=lax.Precision.HIGHEST)

    user_rhs = lax.map(block_rhs, (tile_user, tile_count, tile_valid, tile_item)).reshape(USERS, R)
    return item_factors, user_rhs
```

```python
import functools

import jax
import jax.numpy as jnp
from jax import lax
from jax.experimental import pallas as pl
from jax.experimental.pallas import tpu as pltpu
from jax.sharding import PartitionSpec as P

CG_STEPS = 4
bf16, f32, i32 = jnp.bfloat16, jnp.float32, jnp.int32
AXES = ("user", "grp")
VMEM = pl.BlockSpec(memory_space=pltpu.VMEM)
SMEM = pl.BlockSpec(memory_space=pltpu.SMEM)
struct = jax.ShapeDtypeStruct

confidence_rate = 0.5
ridge_weight = 1.0


def log2(n):
    k = n.bit_length() - 1
    assert 1 << k == n
    return k


def params(mib):
    return pltpu.CompilerParams(vmem_limit_bytes=mib << 20)


def slot_of(item, me, item_dev, n_grp, n_user):
    rel = (item >> log2(item_dev)) ^ me
    slot = item & (item_dev - 1)
    w = rel >> log2(n_grp)
    per, left = n_user * item_dev, n_user
    k = (rel & (n_grp - 1)) * per
    while left > 4:
        per, left = per // 2, left // 2
        k = k + (w & 1) * per
        w = w >> 1
    return k + w * item_dev + slot


def owner_of(group, item_dev, n_grp, n_user):
    k, w = divmod(group, n_user)
    bits, left, at = 0, n_user, 0
    while left > 4:
        left //= 2
        bits |= (w // left) << at
        w %= left
        at += 1
    return (bits | (w << at)) * n_grp + k


def histogram_kernel(step, item_dev, n_grp, n_user, me_s, valid_s, item_s, users, counts, u, *rest):
    eouts = rest[:n_grp]
    c_hi, c_lo, acc = rest[n_grp:]
    tiles, rows = users.shape[1:]
    num_items = c_hi.shape[0]
    block_users = u.shape[0]
    his = block_users // 128
    me = me_s[0]
    acc[...] = jnp.zeros_like(acc)
    lane = lax.broadcasted_iota(i32, (8, rows), 1)
    sub = lax.broadcasted_iota(i32, (8, rows), 0)
    iota = lax.broadcasted_iota(i32, (128, rows), 0).astype(f32).astype(bf16)
    zero = jnp.zeros((16, rows), bf16)
    one, nil = jnp.ones((128, rows), bf16), jnp.zeros((128, rows), bf16)

    def body(b, _):
        base = pl.multiple_of(b * step, step)
        blk = users[0, pl.ds(base, step), :]
        cnt = counts[0, pl.ds(base, step), :].astype(f32) * confidence_rate
        lo = (blk & 127).astype(f32)
        hi = blk >> 7
        for t in range(0, step, 2):
            oh, lhs = [], []
            for j in (t, t + 1):
                lob = jnp.broadcast_to(lo[j : j + 1], (16, rows)).astype(bf16)
                oh.append(jnp.where(jnp.concatenate([lob] * 8, 0) == iota, one, nil))
                on = (lane < valid_s[0, base + j]) & (jnp.broadcast_to(hi[j : j + 1], (8, rows)) == sub)
                ex = jnp.broadcast_to(cnt[j : j + 1], (8, rows))
                lhs.append(
                    jnp.concatenate([jnp.where(on, ex, 0.0), jnp.where(on, 1.0 + ex, 0.0)], 0).astype(bf16)
                )
            left = jnp.concatenate(
                [jnp.concatenate([lhs[0], zero], 1), jnp.concatenate([zero, lhs[1]], 1)], 0
            )
            out = lax.dot_general(
                left, jnp.concatenate(oh, 1), (((1,), (1,)), ((), ())), preferred_element_type=f32
            )
            for q, j in enumerate((t, t + 1)):
                p = slot_of(item_s[0, base + j], me, item_dev, n_grp, n_user)
                acc[pl.ds(pl.multiple_of(p * 16, 16), 16), :] += out[16 * q : 16 * q + 16]
        return 0

    lax.fori_loop(0, tiles // step, body, 0)
    per = num_items // n_grp
    for h in range(his):
        e = (acc[pl.ds(h, num_items, stride=16), :] + 1.0).astype(bf16)
        for k in range(n_grp):
            eouts[k][:, h * 128 : (h + 1) * 128] = e[k * per : (k + 1) * per]
        c = acc[pl.ds(8 + h, num_items, stride=16), :]
        ch = c.astype(bf16)
        c_hi[:, h * 128 : (h + 1) * 128] = ch
        c_lo[:, h * 128 : (h + 1) * 128] = (c - ch.astype(f32)).astype(bf16)
    uu = u[...]
    r = jnp.dot(c_hi[...], uu, preferred_element_type=f32) + jnp.dot(c_lo[...], uu, preferred_element_type=f32)
    rh = r.astype(bf16)
    rl = (r - rh.astype(f32)).astype(bf16)
    for k in range(n_grp):
        eouts[k][:, block_users : block_users + 128] = rh[k * per : (k + 1) * per]
        eouts[k][:, block_users + 128 :] = rl[k * per : (k + 1) * per]


def histogram(me, valid, item, users, counts, u, num_items, item_dev, n_grp, n_user):
    block_users, rank = u.shape
    step = 16
    return pl.pallas_call(
        functools.partial(histogram_kernel, step, item_dev, n_grp, n_user),
        in_specs=[SMEM, SMEM, SMEM, VMEM, VMEM, VMEM],
        out_specs=[VMEM] * (n_grp + 2),
        out_shape=[struct((num_items // n_grp, block_users + 2 * rank), bf16)] * n_grp
        + [struct((num_items, block_users), bf16)] * 2,
        scratch_shapes=[pltpu.VMEM((num_items * 16, 128), f32)],
        compiler_params=params(32),
        name="histogram",
    )(me, valid, item, users, counts, u)


def transpose_kernel(*refs):
    *us, ut = refs
    block_users = us[0].shape[0]
    for b, u in enumerate(us):
        for c in range(block_users // 128):
            at = b * block_users + c * 128
            ut[:, at : at + 128] = u[c * 128 : (c + 1) * 128, :].T


def transposed(us):
    block_users, rank = us[0].shape
    return pl.pallas_call(
        transpose_kernel,
        in_specs=[VMEM] * len(us),
        out_specs=VMEM,
        out_shape=struct((rank, block_users * len(us)), bf16),
        compiler_params=params(16),
        name="transpose",
    )(*us)


def chunk_rows(item_dev):
    return 64 * item_dev + -(-4 * item_dev // 16) * 16


def systems_kernel(first, n_items, item_dev, keep, n_grp, *refs):
    es, us, ut, out, ef = refs[:n_grp], refs[n_grp : 2 * n_grp], refs[2 * n_grp], refs[2 * n_grp + 1], refs[-1]
    block_users, rank = us[0].shape
    span = slice(first, first + n_items)
    for b in range(n_grp):
        e = es[b][span, :block_users].astype(f32)
        for c in range(n_items // item_dev):
            ef[c, :, b * block_users : (b + 1) * block_users] = e[c * item_dev : (c + 1) * item_dev]
    rhs = jnp.zeros((n_items, rank), f32)
    for b in range(n_grp):
        rhs = rhs + es[b][span, block_users : block_users + rank].astype(f32)
        rhs = rhs + es[b][span, block_users + rank :].astype(f32)
    for c in range(n_items // item_dev):
        ef[c, :, n_grp * block_users :] = rhs[c * item_dev : (c + 1) * item_dev]
    row = lax.broadcasted_iota(i32, (64, rank), 0)
    lane = lax.broadcasted_iota(i32, (64, rank), 1)
    eye = lax.broadcasted_iota(i32, (rank, rank), 0) == lax.broadcasted_iota(i32, (rank, rank), 1)
    above = (lane < 64) & (lane > row)
    base = 64 * item_dev

    def body(c, _):
        total = None
        for b in range(n_grp):
            cols = slice(b * block_users, (b + 1) * block_users)
            w = []
            for j in range(item_dev):
                e = ef[c, j : j + 1, cols]
                e = jnp.broadcast_to(e, (16, block_users)).astype(bf16)
                w.append(jnp.concatenate([e] * (rank // 16), 0) * ut[:, cols])
            g = jnp.dot(jnp.concatenate(w, 0), us[b][...], preferred_element_type=f32)
            total = g if total is None else total + g
        diag = []
        for j in range(item_dev):
            g = total[j * rank : (j + 1) * rank]
            packed = jnp.where(above, pltpu.roll(g[64:], 64, 1), g[:64])
            out[c, 64 * j : 64 * j + 64, :] = packed.astype(out.dtype)
            diag.append(jnp.sum(jnp.where(eye, g, 0.0), axis=0, keepdims=True))
        diag = jnp.concatenate(diag, 0)
        side = ef[c, :, n_grp * block_users :]
        put_extras(lambda a, n, v: out.__setitem__((c, slice(base + a, base + a + n)), v), diag, side, keep, item_dev)
        return 0

    lax.fori_loop(0, n_items // item_dev, body, 0)


def put_extras(put, diag, side, keep, item_dev):
    if keep:
        nil = jnp.zeros_like(diag)
        rows = [diag, nil, side, nil]
    else:
        rows = []
        for v in (diag, side):
            high = v.astype(bf16).astype(f32)
            rows += [high, v - high]
    pad = -4 * item_dev % 16
    if pad:
        rows.append(jnp.zeros((pad, diag.shape[1]), f32))
    value = jnp.concatenate(rows, 0)
    put(0, value.shape[0], value if keep else value.astype(bf16))


def systems(es, us, ut, first, n_items, item_dev, keep):
    n_grp = len(es)
    block_users, rank = us[0].shape
    return pl.pallas_call(
        functools.partial(systems_kernel, first, n_items, item_dev, keep, n_grp),
        in_specs=[VMEM] * (2 * n_grp + 1),
        out_specs=VMEM,
        out_shape=struct((n_items // item_dev, chunk_rows(item_dev), rank), f32 if keep else bf16),
        scratch_shapes=[pltpu.VMEM((n_items // item_dev, item_dev, n_grp * block_users + rank), f32)],
        compiler_params=params(40),
        name="systems",
    )(*es, *us, ut)


def extras(value, item_dev):
    base = 64 * item_dev
    part = [value[base + n * item_dev : base + (n + 1) * item_dev] for n in range(4)]
    return part[0] + part[1], part[2] + part[3]


def merge_kernel(item_dev, n_keep, own, got, kept, *sent):
    base = 64 * item_dev
    for c in range(own.shape[0]):
        value = own[c] + got[c].astype(f32)
        diag, side = extras(value, item_dev)
        if c < n_keep:
            kept[c, :base, :] = value[:base]
            put_extras(lambda a, n, v, c=c: kept.__setitem__((c, slice(base + a, base + a + n)), v), diag, side, True, item_dev)
        else:
            ref = sent[0] if len(sent) == 1 else sent[c - n_keep]
            lead = (c - n_keep,) if len(sent) == 1 else ()
            ref[lead + (slice(0, base),)] = value[:base].astype(bf16)
            put_extras(
                lambda a, n, v, ref=ref, lead=lead: ref.__setitem__(lead + (slice(base + a, base + a + n),), v),
                diag, side, False, item_dev,
            )


def merged(own, got, item_dev, n_keep, apart):
    chunks, rows, rank = own.shape
    n_sent = chunks - n_keep
    shapes = [struct((rows, rank), bf16)] * n_sent if apart else [struct((n_sent, rows, rank), bf16)]
    return pl.pallas_call(
        functools.partial(merge_kernel, item_dev, n_keep),
        in_specs=[VMEM] * 2,
        out_specs=[VMEM] * (1 + len(shapes)),
        out_shape=[struct((n_keep, rows, rank), f32)] + shapes,
        compiler_params=params(16),
        name="merge",
    )(own, got)


def gradients_kernel(item_dev, own, *refs):
    *got, prev, out, half = refs
    value = own[0]
    for g in got:
        value = value + g[...].astype(f32)
    rank = value.shape[1]
    diag, side = extras(value, item_dev)
    row = lax.broadcasted_iota(i32, (64, 64), 0)
    col = lax.broadcasted_iota(i32, (64, 64), 1)
    eye = lax.broadcasted_iota(i32, (rank, rank), 0) == lax.broadcasted_iota(i32, (rank, rank), 1)
    matrices = []
    for j in range(item_dev):
        m = value[64 * j : 64 * j + 64]
        t = m.T
        mix, mix_t = m[:, :64], t[:64]
        a = jnp.where(col < row, mix, mix_t)
        c = jnp.where(col > row, mix, mix_t)
        full = jnp.concatenate(
            [jnp.concatenate([a, m[:, 64:]], 1), jnp.concatenate([t[64:], c], 1)], 0
        )
        matrices.append(jnp.where(eye, diag[j : j + 1] + ridge_weight, full))

    def apply(vector):
        rows = []
        for j in range(item_dev):
            s = jnp.sum(matrices[j] * vector[j : j + 1], axis=1, keepdims=True)
            rows.append(jnp.sum(jnp.where(eye, s, 0.0), axis=0, keepdims=True))
        return jnp.concatenate(rows, 0)

    solution = prev[...]
    residual = side - apply(solution)
    direction = residual
    norm_now = jnp.sum(residual * residual, axis=1, keepdims=True)
    for _ in range(CG_STEPS):
        image = apply(direction)
        step = norm_now / jnp.sum(direction * image, axis=1, keepdims=True)
        solution = solution + step * direction
        residual = residual - step * image
        norm_next = jnp.sum(residual * residual, axis=1, keepdims=True)
        direction = residual + norm_next / norm_now * direction
        norm_now = norm_next
    out[...] = solution
    half[...] = solution.astype(bf16)


def gradients(own, got, prev):
    item_dev, rank = prev.shape
    return pl.pallas_call(
        functools.partial(gradients_kernel, item_dev),
        in_specs=[VMEM] * (2 + len(got)),
        out_specs=[VMEM] * 2,
        out_shape=[struct(prev.shape, f32), struct(prev.shape, bf16)],
        compiler_params=params(16),
        name="gradients",
    )(own, *got, prev)


def user_side_kernel(item_dev, n_grp, n_user, me_s, returned, c_hi, c_lo, out, rows, order):
    num_items = returned.shape[0]
    rows[...] = returned[...].astype(f32)
    me = me_s[0]
    for group in range(num_items // item_dev):
        owner = owner_of(group, item_dev, n_grp, n_user) ^ me
        order[group * item_dev : (group + 1) * item_dev, :] = rows[pl.ds(owner * item_dev, item_dev), :]
    ret = order[...].astype(bf16)
    dims = (((0,), (0,)), ((), ()))
    out[...] = lax.dot_general(c_hi[...], ret, dims, preferred_element_type=f32) + lax.dot_general(
        c_lo[...], ret, dims, preferred_element_type=f32
    )


def user_side(me, returned, c_hi, c_lo, item_dev, n_grp, n_user):
    num_items, rank = returned.shape
    return pl.pallas_call(
        functools.partial(user_side_kernel, item_dev, n_grp, n_user),
        in_specs=[SMEM, VMEM, VMEM, VMEM],
        out_specs=VMEM,
        out_shape=struct((c_hi.shape[1], rank), f32),
        scratch_shapes=[pltpu.VMEM((num_items, rank), f32)] * 2,
        compiler_params=params(16),
        name="user_side",
    )(me, returned, c_hi, c_lo)


def shards(user_factors, tile_user, tile_count, tile_valid, tile_item, prev_items):
    n_user = lax.axis_size("user")
    n_grp = lax.axis_size("grp")
    devices = n_user * n_grp
    item_dev, rank = prev_items.shape
    num_items = item_dev * devices
    assert n_grp == 4 and n_user >= 4 and rank == 128 and user_factors.shape[0] == 1024
    me = lax.axis_index(AXES).astype(i32).reshape(1)

    def swap(value, bit):
        return lax.ppermute(value, AXES, [(d, d ^ bit) for d in range(devices)])

    u0 = user_factors
    u2 = swap(u0, 2)
    u1 = swap(u0, 1)
    *es, c_hi, c_lo = histogram(
        me, tile_valid, tile_item, tile_user, tile_count, u0, num_items, item_dev, n_grp, n_user
    )
    u3 = swap(u2, 1)
    got = [es[0], swap(es[1], 1), swap(es[2], 2), swap(es[3], 3)]
    us = [u0, u1, u2, u3]
    ut = transposed(us)
    n_items = num_items // n_grp
    left, bit = n_user, n_grp
    n_half = n_items // 2
    sent = systems(got, us, ut, n_half, n_half, item_dev, False)
    other = swap(sent, bit)
    own = systems(got, us, ut, 0, n_half, item_dev, True)
    left, bit = left // 2, bit * 2
    while left > 4:
        own, sent = merged(own, other, item_dev, left // 2, False)
        other = swap(sent, bit)
        left, bit = left // 2, bit * 2
    own, *sent = merged(own, other, item_dev, 1, True)
    parts = [swap(value, bit * (n + 1)) for n, value in enumerate(sent)]
    solved, half = gradients(own, parts, prev_items)
    spread = jnp.broadcast_to(half[None], (devices, item_dev, rank))
    returned = lax.all_to_all(spread, AXES, 0, 0, tiled=True).reshape(num_items, rank)
    return solved, user_side(me, returned, c_hi, c_lo, item_dev, n_grp, n_user)


def solution(mesh):
    return jax.shard_map(
        shards,
        mesh=mesh,
        in_specs=(
            P(AXES, None),
            P(AXES, None, None),
            P(AXES, None, None),
            P(AXES, None),
            P(AXES, None),
            P(AXES, None),
        ),
        out_specs=(P(AXES, None), P(AXES, None)),
        check_vma=False,
    )
```

```python
import functools

import jax
import jax.numpy as jnp
from jax import lax
from jax.experimental import pallas as pl
from jax.experimental.pallas import tpu as pltpu
from jax.sharding import PartitionSpec as P

CG_STEPS = 4
bf16, f32, i32 = jnp.bfloat16, jnp.float32, jnp.int32
AXES = ("user", "grp")
VMEM = pl.BlockSpec(memory_space=pltpu.VMEM)
SMEM = pl.BlockSpec(memory_space=pltpu.SMEM)
struct = jax.ShapeDtypeStruct

confidence_rate = 0.5
ridge_weight = 1.0


def log2(n):
    k = n.bit_length() - 1
    assert 1 << k == n
    return k


def cost(us):
    return pl.CostEstimate(flops=int(us * 1e9), bytes_accessed=int(us * 3e6), transcendentals=0)


def params(mib):
    return pltpu.CompilerParams(vmem_limit_bytes=mib << 20)


def slot_of(item, me, item_dev, n_grp, n_user):
    rel = (item >> log2(item_dev)) ^ me
    slot = item & (item_dev - 1)
    w = rel >> log2(n_grp)
    per, left = n_user * item_dev, n_user
    k = (rel & (n_grp - 1)) * per
    while left > 4:
        per, left = per // 2, left // 2
        k = k + (w & 1) * per
        w = w >> 1
    return k + w * item_dev + slot


def owner_of(group, item_dev, n_grp, n_user):
    k, w = divmod(group, n_user)
    bits, left, at = 0, n_user, 0
    while left > 4:
        left //= 2
        bits |= (w // left) << at
        w %= left
        at += 1
    return (bits | (w << at)) * n_grp + k


def histogram_kernel(step, item_dev, n_grp, n_user, me_s, *refs):
    sources, rest = refs[:5], refs[5:]
    eouts = rest[:n_grp]
    c_hi, c_lo, acc, *here, sem = rest[n_grp:]
    copies = [pltpu.make_async_copy(a, b, sem.at[n]) for n, (a, b) in enumerate(zip(sources, here))]
    for copy in copies:
        copy.start()
    valid_s, item_s, users, counts, u = here
    tiles, rows = users.shape[1:]
    num_items = c_hi.shape[0]
    block_users = u.shape[0]
    his = block_users // 128
    me = me_s[0]
    acc[...] = jnp.zeros_like(acc)
    for copy in copies[:4]:
        copy.wait()
    lane = lax.broadcasted_iota(i32, (8, rows), 1)
    sub = lax.broadcasted_iota(i32, (8, rows), 0)
    iota = lax.broadcasted_iota(i32, (128, rows), 0).astype(f32).astype(bf16)
    zero = jnp.zeros((16, rows), bf16)
    one, nil = jnp.ones((128, rows), bf16), jnp.zeros((128, rows), bf16)

    def body(b, _):
        base = pl.multiple_of(b * step, step)
        blk = users[0, pl.ds(base, step), :]
        cnt = counts[0, pl.ds(base, step), :].astype(f32) * confidence_rate
        lo = (blk & 127).astype(f32)
        hi = blk >> 7
        for t in range(0, step, 2):
            oh, lhs = [], []
            for j in (t, t + 1):
                lob = jnp.broadcast_to(lo[j : j + 1], (16, rows)).astype(bf16)
                oh.append(jnp.where(jnp.concatenate([lob] * 8, 0) == iota, one, nil))
                on = (lane < valid_s[0, base + j]) & (jnp.broadcast_to(hi[j : j + 1], (8, rows)) == sub)
                ex = jnp.broadcast_to(cnt[j : j + 1], (8, rows))
                lhs.append(
                    jnp.concatenate([jnp.where(on, ex, 0.0), jnp.where(on, 1.0 + ex, 0.0)], 0).astype(bf16)
                )
            left = jnp.concatenate(
                [jnp.concatenate([lhs[0], zero], 1), jnp.concatenate([zero, lhs[1]], 1)], 0
            )
            out = lax.dot_general(
                left, jnp.concatenate(oh, 1), (((1,), (1,)), ((), ())), preferred_element_type=f32
            )
            for q, j in enumerate((t, t + 1)):
                p = slot_of(item_s[0, base + j], me, item_dev, n_grp, n_user)
                acc[pl.ds(pl.multiple_of(p * 16, 16), 16), :] += out[16 * q : 16 * q + 16]
        return 0

    lax.fori_loop(0, tiles // step, body, 0)
    copies[4].wait()
    per = num_items // n_grp
    for h in range(his):
        e = (acc[pl.ds(h, num_items, stride=16), :] + 1.0).astype(bf16)
        for k in range(n_grp):
            eouts[k][:, h * 128 : (h + 1) * 128] = e[k * per : (k + 1) * per]
        c = acc[pl.ds(8 + h, num_items, stride=16), :]
        ch = c.astype(bf16)
        c_hi[:, h * 128 : (h + 1) * 128] = ch
        c_lo[:, h * 128 : (h + 1) * 128] = (c - ch.astype(f32)).astype(bf16)
    uu = u[...]
    r = jnp.dot(c_hi[...], uu, preferred_element_type=f32) + jnp.dot(c_lo[...], uu, preferred_element_type=f32)
    rh = r.astype(bf16)
    rl = (r - rh.astype(f32)).astype(bf16)
    for k in range(n_grp):
        eouts[k][:, block_users : block_users + 128] = rh[k * per : (k + 1) * per]
        eouts[k][:, block_users + 128 :] = rl[k * per : (k + 1) * per]


def histogram(me, valid, item, users, counts, u, num_items, item_dev, n_grp, n_user):
    block_users, rank = u.shape
    step = 64
    return pl.pallas_call(
        functools.partial(histogram_kernel, step, item_dev, n_grp, n_user),
        in_specs=[SMEM] + [pl.BlockSpec(memory_space=pl.ANY)] * 5,
        out_specs=[VMEM] * (n_grp + 2),
        out_shape=[struct((num_items // n_grp, block_users + 2 * rank), bf16)] * n_grp
        + [struct((num_items, block_users), bf16)] * 2,
        scratch_shapes=[
            pltpu.VMEM((num_items * 16, 128), f32),
            pltpu.SMEM(valid.shape, i32),
            pltpu.SMEM(item.shape, i32),
            pltpu.VMEM(users.shape, i32),
            pltpu.VMEM(counts.shape, i32),
            pltpu.VMEM(u.shape, bf16),
            pltpu.SemaphoreType.DMA((5,)),
        ],
        compiler_params=params(32),
        cost_estimate=cost(7),
        name="histogram",
    )(me, valid, item, users, counts, u)


def transpose_kernel(*refs):
    *us, ut = refs
    block_users = us[0].shape[0]
    for b, u in enumerate(us):
        for c in range(block_users // 128):
            at = b * block_users + c * 128
            ut[:, at : at + 128] = u[c * 128 : (c + 1) * 128, :].T


def transposed(us):
    block_users, rank = us[0].shape
    return pl.pallas_call(
        transpose_kernel,
        in_specs=[VMEM] * len(us),
        out_specs=VMEM,
        out_shape=struct((rank, block_users * len(us)), bf16),
        compiler_params=params(16),
        cost_estimate=cost(0.2),
        name="transpose",
    )(*us)


def chunk_rows(item_dev):
    return 64 * item_dev + -(-4 * item_dev // 16) * 16


def partial_systems(ef, ut, us, c, item_dev, at):
    total = None
    for b, u in enumerate(us):
        block_users, rank = u.shape
        cols = slice(b * block_users, (b + 1) * block_users)
        w = []
        for j in range(item_dev):
            e = jnp.broadcast_to(ef[c, j : j + 1, cols], (16, block_users)).astype(bf16)
            w.append(jnp.concatenate([e] * (rank // 16), 0) * ut[:, at + cols.start : at + cols.stop])
        g = jnp.dot(jnp.concatenate(w, 0), u[...], preferred_element_type=f32)
        total = g if total is None else total + g
    return total


def spread_rows(ef, es, first, n_items, item_dev, block_users):
    for b, e in enumerate(es):
        value = e[first : first + n_items, :block_users].astype(f32)
        for c in range(n_items // item_dev):
            ef[c, :, b * block_users : (b + 1) * block_users] = value[c * item_dev : (c + 1) * item_dev]


def begun_kernel(first, n_items, item_dev, n, *refs):
    es, us, ut, out, ef = refs[:n], refs[n : 2 * n], refs[2 * n], refs[2 * n + 1], refs[2 * n + 2]
    spread_rows(ef, es, first, n_items, item_dev, us[0].shape[0])

    def body(c, _):
        out[c] = partial_systems(ef, ut, us, c, item_dev, 0)
        return 0

    lax.fori_loop(0, n_items // item_dev, body, 0)


def begun(es, us, ut, first, n_items, item_dev):
    n = len(es)
    block_users, rank = us[0].shape
    return pl.pallas_call(
        functools.partial(begun_kernel, first, n_items, item_dev, n),
        in_specs=[VMEM] * (2 * n + 1),
        out_specs=VMEM,
        out_shape=struct((n_items // item_dev, item_dev * rank, rank), f32),
        scratch_shapes=[pltpu.VMEM((n_items // item_dev, item_dev, n * block_users), f32)],
        compiler_params=params(32),
        cost_estimate=cost(2.6),
        name="begun",
    )(*es, *us, ut)


def systems_kernel(first, n_items, item_dev, keep, n, done, *refs):
    es, us, ut = refs[:n], refs[n : 2 * n - done], refs[2 * n - done]
    start = refs[2 * n - done + 1] if done else None
    out, ef = refs[-2:]
    block_users, rank = us[0].shape
    span = slice(first, first + n_items)
    wide = (n - done) * block_users
    spread_rows(ef, es[done:], first, n_items, item_dev, block_users)
    rhs = jnp.zeros((n_items, rank), f32)
    for e in es:
        rhs = rhs + e[span, block_users : block_users + rank].astype(f32)
        rhs = rhs + e[span, block_users + rank :].astype(f32)
    for c in range(n_items // item_dev):
        ef[c, :, wide:] = rhs[c * item_dev : (c + 1) * item_dev]
    row = lax.broadcasted_iota(i32, (64, rank), 0)
    lane = lax.broadcasted_iota(i32, (64, rank), 1)
    eye = lax.broadcasted_iota(i32, (rank, rank), 0) == lax.broadcasted_iota(i32, (rank, rank), 1)
    above = (lane < 64) & (lane > row)
    base = 64 * item_dev

    def body(c, _):
        total = partial_systems(ef, ut, us, c, item_dev, done * block_users)
        if done:
            total = total + start[c]
        diag = []
        for j in range(item_dev):
            g = total[j * rank : (j + 1) * rank]
            packed = jnp.where(above, pltpu.roll(g[64:], 64, 1), g[:64])
            out[c, 64 * j : 64 * j + 64, :] = packed.astype(out.dtype)
            diag.append(jnp.sum(jnp.where(eye, g, 0.0), axis=0, keepdims=True))
        diag = jnp.concatenate(diag, 0)
        side = ef[c, :, wide:]
        put_extras(lambda a, n, v: out.__setitem__((c, slice(base + a, base + a + n)), v), diag, side, keep, item_dev)
        return 0

    lax.fori_loop(0, n_items // item_dev, body, 0)


def put_extras(put, diag, side, keep, item_dev):
    if keep:
        nil = jnp.zeros_like(diag)
        rows = [diag, nil, side, nil]
    else:
        rows = []
        for v in (diag, side):
            high = v.astype(bf16).astype(f32)
            rows += [high, v - high]
    pad = -4 * item_dev % 16
    if pad:
        rows.append(jnp.zeros((pad, diag.shape[1]), f32))
    value = jnp.concatenate(rows, 0)
    put(0, value.shape[0], value if keep else value.astype(bf16))


def systems(es, us, ut, first, n_items, item_dev, keep, start=None, done=0):
    n = len(es)
    block_users, rank = us[0].shape
    more = [] if start is None else [start]
    return pl.pallas_call(
        functools.partial(systems_kernel, first, n_items, item_dev, keep, n, done),
        in_specs=[VMEM] * (2 * n - done + 1 + len(more)),
        out_specs=VMEM,
        out_shape=struct((n_items // item_dev, chunk_rows(item_dev), rank), f32 if keep else bf16),
        scratch_shapes=[pltpu.VMEM((n_items // item_dev, item_dev, (n - done) * block_users + rank), f32)],
        compiler_params=params(40),
        cost_estimate=cost(1.3 * (n - done)),
        name="systems",
    )(*es, *us[done:], ut, *more)


def extras(value, item_dev):
    base = 64 * item_dev
    part = [value[base + n * item_dev : base + (n + 1) * item_dev] for n in range(4)]
    return part[0] + part[1], part[2] + part[3]


def merge_kernel(item_dev, n_keep, own, got, kept, *sent):
    base = 64 * item_dev
    for c in range(own.shape[0]):
        value = own[c] + got[c].astype(f32)
        diag, side = extras(value, item_dev)
        if c < n_keep:
            kept[c, :base, :] = value[:base]
            put_extras(lambda a, n, v, c=c: kept.__setitem__((c, slice(base + a, base + a + n)), v), diag, side, True, item_dev)
        else:
            ref = sent[0] if len(sent) == 1 else sent[c - n_keep]
            lead = (c - n_keep,) if len(sent) == 1 else ()
            ref[lead + (slice(0, base),)] = value[:base].astype(bf16)
            put_extras(
                lambda a, n, v, ref=ref, lead=lead: ref.__setitem__(lead + (slice(base + a, base + a + n),), v),
                diag, side, False, item_dev,
            )


def merged(own, got, item_dev, n_keep, apart):
    chunks, rows, rank = own.shape
    n_sent = chunks - n_keep
    shapes = [struct((rows, rank), bf16)] * n_sent if apart else [struct((n_sent, rows, rank), bf16)]
    return pl.pallas_call(
        functools.partial(merge_kernel, item_dev, n_keep),
        in_specs=[VMEM] * 2,
        out_specs=[VMEM] * (1 + len(shapes)),
        out_shape=[struct((n_keep, rows, rank), f32)] + shapes,
        compiler_params=params(16),
        name="merge",
    )(own, got)


def gradients_kernel(item_dev, own, *refs):
    *got, prev, out, half = refs
    value = own[0]
    for g in got:
        value = value + g[...].astype(f32)
    rank = value.shape[1]
    diag, side = extras(value, item_dev)
    row = lax.broadcasted_iota(i32, (64, 64), 0)
    col = lax.broadcasted_iota(i32, (64, 64), 1)
    eye = lax.broadcasted_iota(i32, (rank, rank), 0) == lax.broadcasted_iota(i32, (rank, rank), 1)
    matrices = []
    for j in range(item_dev):
        m = value[64 * j : 64 * j + 64]
        t = m.T
        mix, mix_t = m[:, :64], t[:64]
        a = jnp.where(col < row, mix, mix_t)
        c = jnp.where(col > row, mix, mix_t)
        full = jnp.concatenate(
            [jnp.concatenate([a, m[:, 64:]], 1), jnp.concatenate([t[64:], c], 1)], 0
        )
        matrices.append(jnp.where(eye, diag[j : j + 1] + ridge_weight, full))

    def apply(vector):
        rows = []
        for j in range(item_dev):
            s = jnp.sum(matrices[j] * vector[j : j + 1], axis=1, keepdims=True)
            rows.append(jnp.sum(jnp.where(eye, s, 0.0), axis=0, keepdims=True))
        return jnp.concatenate(rows, 0)

    solution = prev[...]
    residual = side - apply(solution)
    direction = residual
    norm_now = jnp.sum(residual * residual, axis=1, keepdims=True)
    for _ in range(CG_STEPS):
        image = apply(direction)
        step = norm_now / jnp.sum(direction * image, axis=1, keepdims=True)
        solution = solution + step * direction
        residual = residual - step * image
        norm_next = jnp.sum(residual * residual, axis=1, keepdims=True)
        direction = residual + norm_next / norm_now * direction
        norm_now = norm_next
    out[...] = solution
    half[...] = solution.astype(bf16)


def gradients(own, got, prev):
    item_dev, rank = prev.shape
    return pl.pallas_call(
        functools.partial(gradients_kernel, item_dev),
        in_specs=[VMEM] * (2 + len(got)),
        out_specs=[VMEM] * 2,
        out_shape=[struct(prev.shape, f32), struct(prev.shape, bf16)],
        compiler_params=params(16),
        cost_estimate=cost(2),
        name="gradients",
    )(own, *got, prev)


def user_side_kernel(item_dev, n_grp, n_user, me_s, returned, c_hi, c_lo, out, rows, order):
    num_items = returned.shape[0]
    rows[...] = returned[...].astype(f32)
    me = me_s[0]
    for group in range(num_items // item_dev):
        owner = owner_of(group, item_dev, n_grp, n_user) ^ me
        order[group * item_dev : (group + 1) * item_dev, :] = rows[pl.ds(owner * item_dev, item_dev), :]
    ret = order[...].astype(bf16)
    out[...] = jnp.dot(c_hi[...], ret, preferred_element_type=f32) + jnp.dot(
        c_lo[...], ret, preferred_element_type=f32
    )


def user_side(me, returned, c_hi, c_lo, item_dev, n_grp, n_user):
    num_items, rank = returned.shape
    return pl.pallas_call(
        functools.partial(user_side_kernel, item_dev, n_grp, n_user),
        in_specs=[SMEM, VMEM, VMEM, VMEM],
        out_specs=VMEM,
        out_shape=struct((c_hi.shape[0], rank), f32),
        scratch_shapes=[pltpu.VMEM((num_items, rank), f32)] * 2,
        compiler_params=params(16),
        cost_estimate=cost(1),
        name="user_side",
    )(me, returned, c_hi, c_lo)


def flip_kernel(*refs):
    n = len(refs) // 2
    for a, b in zip(refs[:n], refs[n:]):
        for c in range(a.shape[1] // 128):
            b[c * 128 : (c + 1) * 128, :] = a[:, c * 128 : (c + 1) * 128].T


def flipped(*values):
    return pl.pallas_call(
        flip_kernel,
        in_specs=[VMEM] * len(values),
        out_specs=[VMEM] * len(values),
        out_shape=[struct(v.shape[::-1], v.dtype) for v in values],
        compiler_params=params(16),
        cost_estimate=cost(0.6),
        name="flip",
    )(*values)


def shards(user_factors, tile_user, tile_count, tile_valid, tile_item, prev_items):
    n_user = lax.axis_size("user")
    n_grp = lax.axis_size("grp")
    devices = n_user * n_grp
    item_dev, rank = prev_items.shape
    num_items = item_dev * devices
    assert n_grp == 4 and n_user >= 4 and rank == 128 and user_factors.shape[0] == 1024
    me = lax.axis_index(AXES).astype(i32).reshape(1)

    def swap(value, bit):
        return lax.ppermute(value, AXES, [(d, d ^ bit) for d in range(devices)])

    u0 = user_factors
    u2 = swap(u0, 2)
    u1 = swap(u0, 1)
    *es, c_hi, c_lo = histogram(
        me, tile_valid, tile_item, tile_user, tile_count, u0, num_items, item_dev, n_grp, n_user
    )
    u2, es[0] = lax.optimization_barrier((u2, es[0]))
    u3 = swap(u2, 1)
    got = [es[0], swap(es[1], 1), swap(es[2], 2), swap(es[3], 3)]
    us = [u0, u1, u2, u3]
    ut = transposed(us)
    n_items = num_items // n_grp
    left, bit = n_user, n_grp
    n_half = n_items // 2
    start = begun(got[:2], us[:2], transposed(us[:2]), n_half, n_half, item_dev)
    sent = systems(got, us, ut, n_half, n_half, item_dev, False, start, 2)
    other = swap(sent, bit)
    own = systems(got, us, ut, 0, n_half, item_dev, True)
    left, bit = left // 2, bit * 2
    while left > 4:
        own, sent = merged(own, other, item_dev, left // 2, False)
        other = swap(sent, bit)
        left, bit = left // 2, bit * 2
    own, *sent = merged(own, other, item_dev, 1, True)
    parts = [swap(value, bit * (n + 1)) for n, value in enumerate(sent)]
    c_hi, c_lo, _ = lax.optimization_barrier((c_hi, c_lo, sent[0]))
    c_hi, c_lo = flipped(c_hi, c_lo)
    solved, half = gradients(own, parts, prev_items)
    spread = jnp.broadcast_to(half[None], (devices, item_dev, rank))
    returned = lax.all_to_all(spread, AXES, 0, 0, tiled=True).reshape(num_items, rank)
    return solved, user_side(me, returned, c_hi, c_lo, item_dev, n_grp, n_user)


def solution(mesh):
    return jax.shard_map(
        shards,
        mesh=mesh,
        in_specs=(
            P(AXES, None),
            P(AXES, None, None),
            P(AXES, None, None),
            P(AXES, None),
            P(AXES, None),
            P(AXES, None),
        ),
        out_specs=(P(AXES, None), P(AXES, None)),
        check_vma=False,
    )
```

```python
import functools

import jax
import jax.numpy as jnp
from jax import lax
from jax.experimental import pallas as pl
from jax.experimental.pallas import tpu as pltpu
from jax.sharding import PartitionSpec as P

CG_STEPS = 4
bf16, f32, i32 = jnp.bfloat16, jnp.float32, jnp.int32
AXES = ("user", "grp")
VMEM = pl.BlockSpec(memory_space=pltpu.VMEM)
SMEM = pl.BlockSpec(memory_space=pltpu.SMEM)
struct = jax.ShapeDtypeStruct

confidence_rate = 0.5
ridge_weight = 1.0


def log2(n):
    k = n.bit_length() - 1
    assert 1 << k == n
    return k


def cost(us):
    return pl.CostEstimate(flops=int(us * 1e9), bytes_accessed=int(us * 3e6), transcendentals=0)


def params(mib):
    return pltpu.CompilerParams(vmem_limit_bytes=mib << 20)


def slot_of(item, me, item_dev, n_grp, n_user):
    rel = (item >> log2(item_dev)) ^ me
    slot = item & (item_dev - 1)
    w = rel >> log2(n_grp)
    per, left = n_user * item_dev, n_user
    k = (rel & (n_grp - 1)) * per
    while left > 4:
        per, left = per // 2, left // 2
        k = k + (w & 1) * per
        w = w >> 1
    return k + w * item_dev + slot


def owner_of(group, item_dev, n_grp, n_user):
    k, w = divmod(group, n_user)
    bits, left, at = 0, n_user, 0
    while left > 4:
        left //= 2
        bits |= (w // left) << at
        w %= left
        at += 1
    return (bits | (w << at)) * n_grp + k


def histogram_kernel(step, low_part, item_dev, n_grp, n_user, me_s, *refs):
    sources, rest = refs[:5], refs[5:]
    eouts = rest[:n_grp]
    c_hi, c_lo, acc, *here, sem = rest[n_grp:]
    copies = [pltpu.make_async_copy(a, b, sem.at[n]) for n, (a, b) in enumerate(zip(sources, here))]
    for copy in copies:
        copy.start()
    valid_s, item_s, users, counts, u = here
    tiles, rows = users.shape[1:]
    num_items = c_hi.shape[0]
    block_users = u.shape[0]
    his = block_users // low_part
    kinds = 2 * his
    me = me_s[0]
    acc[...] = jnp.zeros_like(acc)
    for copy in copies[:4]:
        copy.wait()
    lane = lax.broadcasted_iota(i32, (his, rows), 1)
    sub = lax.broadcasted_iota(i32, (his, rows), 0)
    iota = lax.broadcasted_iota(i32, (low_part, rows), 0).astype(f32).astype(bf16)
    zero = jnp.zeros((kinds, rows), bf16)
    one, nil = jnp.ones((low_part, rows), bf16), jnp.zeros((low_part, rows), bf16)

    def body(b, _):
        base = pl.multiple_of(b * step, step)
        blk = users[0, pl.ds(base, step), :]
        cnt = counts[0, pl.ds(base, step), :].astype(f32) * confidence_rate
        lo = (blk & (low_part - 1)).astype(f32)
        hi = blk >> log2(low_part)
        for t in range(0, step, 2):
            oh, lhs = [], []
            for j in (t, t + 1):
                lob = jnp.broadcast_to(lo[j : j + 1], (16, rows)).astype(bf16)
                oh.append(jnp.where(jnp.concatenate([lob] * (low_part // 16), 0) == iota, one, nil))
                on = (lane < valid_s[0, base + j]) & (jnp.broadcast_to(hi[j : j + 1], (his, rows)) == sub)
                ex = jnp.broadcast_to(cnt[j : j + 1], (his, rows))
                lhs.append(
                    jnp.concatenate([jnp.where(on, ex, 0.0), jnp.where(on, 1.0 + ex, 0.0)], 0).astype(bf16)
                )
            left = jnp.concatenate(
                [jnp.concatenate([lhs[0], zero], 1), jnp.concatenate([zero, lhs[1]], 1)], 0
            )
            out = lax.dot_general(
                left, jnp.concatenate(oh, 1), (((1,), (1,)), ((), ())), preferred_element_type=f32
            )
            for q, j in enumerate((t, t + 1)):
                p = slot_of(item_s[0, base + j], me, item_dev, n_grp, n_user)
                acc[pl.ds(pl.multiple_of(p * kinds, kinds), kinds), :] += out[kinds * q : kinds * (q + 1)]
        return 0

    lax.fori_loop(0, tiles // step, body, 0)
    copies[4].wait()
    per = num_items // n_grp
    wide = 128 // low_part

    def row(h):
        parts = [acc[pl.ds(h * wide + n, num_items, stride=kinds), :] for n in range(wide)]
        return jnp.concatenate(parts, 1)

    for h in range(block_users // 128):
        e = (row(h) + 1.0).astype(bf16)
        for k in range(n_grp):
            eouts[k][:, h * 128 : (h + 1) * 128] = e[k * per : (k + 1) * per]
        c = row(his // wide + h)
        ch = c.astype(bf16)
        c_hi[:, h * 128 : (h + 1) * 128] = ch
        c_lo[:, h * 128 : (h + 1) * 128] = (c - ch.astype(f32)).astype(bf16)
    uu = u[...]
    r = jnp.dot(c_hi[...], uu, preferred_element_type=f32) + jnp.dot(c_lo[...], uu, preferred_element_type=f32)
    rh = r.astype(bf16)
    rl = (r - rh.astype(f32)).astype(bf16)
    for k in range(n_grp):
        eouts[k][:, block_users : block_users + 128] = rh[k * per : (k + 1) * per]
        eouts[k][:, block_users + 128 :] = rl[k * per : (k + 1) * per]


def histogram(me, valid, item, users, counts, u, num_items, item_dev, n_grp, n_user):
    block_users, rank = u.shape
    step, low_part = 128, 64
    return pl.pallas_call(
        functools.partial(histogram_kernel, step, low_part, item_dev, n_grp, n_user),
        in_specs=[SMEM] + [pl.BlockSpec(memory_space=pltpu.HBM)] * 5,
        out_specs=[VMEM] * (n_grp + 2),
        out_shape=[struct((num_items // n_grp, block_users + 2 * rank), bf16)] * n_grp
        + [struct((num_items, block_users), bf16)] * 2,
        scratch_shapes=[
            pltpu.VMEM((num_items * 2 * block_users // low_part, low_part), f32),
            pltpu.SMEM(valid.shape, i32),
            pltpu.SMEM(item.shape, i32),
            pltpu.VMEM(users.shape, i32),
            pltpu.VMEM(counts.shape, i32),
            pltpu.VMEM(u.shape, bf16),
            pltpu.SemaphoreType.DMA((5,)),
        ],
        compiler_params=params(32),
        cost_estimate=cost(7),
        name="histogram",
    )(me, *[pltpu.with_memory_space_constraint(v, pltpu.HBM) for v in (valid, item, users, counts, u)])


def transpose_kernel(*refs):
    *us, ut = refs
    block_users = us[0].shape[0]
    for b, u in enumerate(us):
        for c in range(block_users // 128):
            at = b * block_users + c * 128
            ut[:, at : at + 128] = u[c * 128 : (c + 1) * 128, :].T


def transposed(us):
    block_users, rank = us[0].shape
    return pl.pallas_call(
        transpose_kernel,
        in_specs=[VMEM] * len(us),
        out_specs=VMEM,
        out_shape=struct((rank, block_users * len(us)), bf16),
        compiler_params=params(16),
        cost_estimate=cost(0.2),
        name="transpose",
    )(*us)


def chunk_rows(item_dev):
    return 64 * item_dev + -(-4 * item_dev // 16) * 16


def partial_systems(ef, ut, us, c, item_dev, at):
    total = None
    for b, u in enumerate(us):
        block_users, rank = u.shape
        cols = slice(b * block_users, (b + 1) * block_users)
        w = []
        for j in range(item_dev):
            e = jnp.broadcast_to(ef[c, j : j + 1, cols], (16, block_users)).astype(bf16)
            w.append(jnp.concatenate([e] * (rank // 16), 0) * ut[:, at + cols.start : at + cols.stop])
        g = jnp.dot(jnp.concatenate(w, 0), u[...], preferred_element_type=f32)
        total = g if total is None else total + g
    return total


def some_rows(ref, first, n, cols):
    low, high = first // 16 * 16, -(-(first + n) // 16) * 16
    return ref[low:high, cols].astype(f32)[first - low : first - low + n]


def spread_rows(ef, es, first, n_items, item_dev, block_users):
    for b, e in enumerate(es):
        value = some_rows(e, first, n_items, slice(0, block_users))
        for c in range(n_items // item_dev):
            ef[c, :, b * block_users : (b + 1) * block_users] = value[c * item_dev : (c + 1) * item_dev]


def begun_kernel(first, n_items, item_dev, n, *refs):
    es, us, ut, out, ef = refs[:n], refs[n : 2 * n], refs[2 * n], refs[2 * n + 1], refs[2 * n + 2]
    spread_rows(ef, es, first, n_items, item_dev, us[0].shape[0])

    def body(c, _):
        out[c] = partial_systems(ef, ut, us, c, item_dev, 0)
        return 0

    lax.fori_loop(0, n_items // item_dev, body, 0)


def begun(es, us, ut, first, n_items, item_dev):
    n = len(es)
    block_users, rank = us[0].shape
    return pl.pallas_call(
        functools.partial(begun_kernel, first, n_items, item_dev, n),
        in_specs=[VMEM] * (2 * n + 1),
        out_specs=VMEM,
        out_shape=struct((n_items // item_dev, item_dev * rank, rank), f32),
        scratch_shapes=[pltpu.VMEM((n_items // item_dev, item_dev, n * block_users), f32)],
        compiler_params=params(32),
        cost_estimate=cost(2.6),
        name="begun",
    )(*es, *us, ut)


def systems_kernel(first, n_items, item_dev, keep, n, done, at, *refs):
    es, us, ut = refs[:n], refs[n : 2 * n - done], refs[2 * n - done]
    start = refs[2 * n - done + 1] if done else None
    out, ef = refs[-2:]
    block_users, rank = us[0].shape
    wide = (n - done) * block_users
    spread_rows(ef, es[done:], first, n_items, item_dev, block_users)
    rhs = jnp.zeros((n_items, rank), f32)
    for e in es:
        rhs = rhs + some_rows(e, first, n_items, slice(block_users, block_users + rank))
        rhs = rhs + some_rows(e, first, n_items, slice(block_users + rank, block_users + 2 * rank))
    for c in range(n_items // item_dev):
        ef[c, :, wide:] = rhs[c * item_dev : (c + 1) * item_dev]
    row = lax.broadcasted_iota(i32, (64, rank), 0)
    lane = lax.broadcasted_iota(i32, (64, rank), 1)
    eye = lax.broadcasted_iota(i32, (rank, rank), 0) == lax.broadcasted_iota(i32, (rank, rank), 1)
    above = (lane < 64) & (lane > row)
    base = 64 * item_dev

    def body(c, _):
        total = partial_systems(ef, ut, us, c, item_dev, done * block_users)
        if done:
            total = total + start[at + c]
        diag = []
        for j in range(item_dev):
            g = total[j * rank : (j + 1) * rank]
            packed = jnp.where(above, pltpu.roll(g[64:], 64, 1), g[:64])
            out[c, 64 * j : 64 * j + 64, :] = packed.astype(out.dtype)
            diag.append(jnp.sum(jnp.where(eye, g, 0.0), axis=0, keepdims=True))
        diag = jnp.concatenate(diag, 0)
        side = ef[c, :, wide:]
        put_extras(lambda a, n, v: out.__setitem__((c, slice(base + a, base + a + n)), v), diag, side, keep, item_dev)
        return 0

    lax.fori_loop(0, n_items // item_dev, body, 0)


def put_extras(put, diag, side, keep, item_dev):
    if keep:
        nil = jnp.zeros_like(diag)
        rows = [diag, nil, side, nil]
    else:
        rows = []
        for v in (diag, side):
            high = v.astype(bf16).astype(f32)
            rows += [high, v - high]
    pad = -4 * item_dev % 16
    if pad:
        rows.append(jnp.zeros((pad, diag.shape[1]), f32))
    value = jnp.concatenate(rows, 0)
    put(0, value.shape[0], value if keep else value.astype(bf16))


def systems(es, us, ut, first, n_items, item_dev, keep, start=None, done=0, at=0, us_cost=None):
    n = len(es)
    block_users, rank = us[0].shape
    more = [] if start is None else [start]
    return pl.pallas_call(
        functools.partial(systems_kernel, first, n_items, item_dev, keep, n, done, at),
        in_specs=[VMEM] * (2 * n - done + 1 + len(more)),
        out_specs=VMEM,
        out_shape=struct((n_items // item_dev, chunk_rows(item_dev), rank), f32 if keep else bf16),
        scratch_shapes=[pltpu.VMEM((n_items // item_dev, item_dev, (n - done) * block_users + rank), f32)],
        compiler_params=params(40),
        cost_estimate=cost(0.082 * (n - done) * n_items if us_cost is None else us_cost),
        name="systems",
    )(*es, *us[done:], ut, *more)


def extras(value, item_dev):
    base = 64 * item_dev
    part = [value[base + n * item_dev : base + (n + 1) * item_dev] for n in range(4)]
    return part[0] + part[1], part[2] + part[3]


def merge_kernel(item_dev, n_keep, apart, own, got, *outs):
    kept, sent = outs[0], outs[bool(n_keep) :]
    base = 64 * item_dev
    for c in range(own.shape[0]):
        value = own[c] + got[c].astype(f32)
        diag, side = extras(value, item_dev)
        if c < n_keep:
            kept[c, :base, :] = value[:base]
            put_extras(lambda a, n, v, c=c: kept.__setitem__((c, slice(base + a, base + a + n)), v), diag, side, True, item_dev)
        else:
            ref = sent[c - n_keep] if apart else sent[0]
            lead = () if apart else (c - n_keep,)
            ref[lead + (slice(0, base),)] = value[:base].astype(bf16)
            put_extras(
                lambda a, n, v, ref=ref, lead=lead: ref.__setitem__(lead + (slice(base + a, base + a + n),), v),
                diag, side, False, item_dev,
            )


def merged(own, got, item_dev, n_keep, apart):
    chunks, rows, rank = own.shape
    n_sent = chunks - n_keep
    shapes = [struct((rows, rank), bf16)] * n_sent if apart else [struct((n_sent, rows, rank), bf16)]
    shapes = ([struct((n_keep, rows, rank), f32)] if n_keep else []) + shapes
    return pl.pallas_call(
        functools.partial(merge_kernel, item_dev, n_keep, apart),
        in_specs=[VMEM] * 2,
        out_specs=[VMEM] * len(shapes),
        out_shape=shapes,
        compiler_params=params(16),
        name="merge",
    )(own, got)


def gradients_kernel(item_dev, own, *refs):
    *got, prev, out, half = refs
    value = own[0]
    for g in got:
        value = value + g[...].astype(f32)
    rank = value.shape[1]
    diag, side = extras(value, item_dev)
    row = lax.broadcasted_iota(i32, (64, 64), 0)
    col = lax.broadcasted_iota(i32, (64, 64), 1)
    eye = lax.broadcasted_iota(i32, (rank, rank), 0) == lax.broadcasted_iota(i32, (rank, rank), 1)
    matrices = []
    for j in range(item_dev):
        m = value[64 * j : 64 * j + 64]
        t = m.T
        mix, mix_t = m[:, :64], t[:64]
        a = jnp.where(col < row, mix, mix_t)
        c = jnp.where(col > row, mix, mix_t)
        full = jnp.concatenate(
            [jnp.concatenate([a, m[:, 64:]], 1), jnp.concatenate([t[64:], c], 1)], 0
        )
        matrices.append(jnp.where(eye, diag[j : j + 1] + ridge_weight, full))

    def apply(vector):
        rows = []
        for j in range(item_dev):
            s = jnp.sum(matrices[j] * vector[j : j + 1], axis=1, keepdims=True)
            rows.append(jnp.sum(jnp.where(eye, s, 0.0), axis=0, keepdims=True))
        return jnp.concatenate(rows, 0)

    solution = prev[...]
    residual = side - apply(solution)
    direction = residual
    norm_now = jnp.sum(residual * residual, axis=1, keepdims=True)
    for _ in range(CG_STEPS):
        image = apply(direction)
        step = norm_now / jnp.sum(direction * image, axis=1, keepdims=True)
        solution = solution + step * direction
        residual = residual - step * image
        norm_next = jnp.sum(residual * residual, axis=1, keepdims=True)
        direction = residual + norm_next / norm_now * direction
        norm_now = norm_next
    out[...] = solution
    short = solution.astype(bf16)
    for d in range(half.shape[0]):
        half[d] = short


def gradients(own, got, prev, devices):
    item_dev, rank = prev.shape
    return pl.pallas_call(
        functools.partial(gradients_kernel, item_dev),
        in_specs=[VMEM] * (2 + len(got)),
        out_specs=[VMEM] * 2,
        out_shape=[struct(prev.shape, f32), struct((devices,) + prev.shape, bf16)],
        compiler_params=params(16),
        cost_estimate=cost(2),
        name="gradients",
    )(own, *got, prev)


def user_side_kernel(item_dev, n_grp, n_user, me_s, returned, c_hi, c_lo, out, rows, order):
    num_items = returned.shape[0]
    rows[...] = returned[...].astype(f32)
    me = me_s[0]
    for group in range(num_items // item_dev):
        owner = owner_of(group, item_dev, n_grp, n_user) ^ me
        order[group * item_dev : (group + 1) * item_dev, :] = rows[pl.ds(owner * item_dev, item_dev), :]
    ret = order[...].astype(bf16)
    out[...] = jnp.dot(c_hi[...], ret, preferred_element_type=f32) + jnp.dot(
        c_lo[...], ret, preferred_element_type=f32
    )


def user_side(me, returned, c_hi, c_lo, item_dev, n_grp, n_user):
    num_items, rank = returned.shape
    return pl.pallas_call(
        functools.partial(user_side_kernel, item_dev, n_grp, n_user),
        in_specs=[SMEM, VMEM, VMEM, VMEM],
        out_specs=VMEM,
        out_shape=struct((c_hi.shape[0], rank), f32),
        scratch_shapes=[pltpu.VMEM((num_items, rank), f32)] * 2,
        compiler_params=params(16),
        cost_estimate=cost(1),
        name="user_side",
    )(me, returned, c_hi, c_lo)


def flip_kernel(*refs):
    n = len(refs) // 2
    for a, b in zip(refs[:n], refs[n:]):
        for c in range(a.shape[1] // 128):
            b[c * 128 : (c + 1) * 128, :] = a[:, c * 128 : (c + 1) * 128].T


def flipped(*values):
    return pl.pallas_call(
        flip_kernel,
        in_specs=[VMEM] * len(values),
        out_specs=[VMEM] * len(values),
        out_shape=[struct(v.shape[::-1], v.dtype) for v in values],
        compiler_params=params(16),
        cost_estimate=cost(8),
        name="flip",
    )(*values)


def shards(user_factors, tile_user, tile_count, tile_valid, tile_item, prev_items):
    n_user = lax.axis_size("user")
    n_grp = lax.axis_size("grp")
    devices = n_user * n_grp
    item_dev, rank = prev_items.shape
    num_items = item_dev * devices
    assert n_grp == 4 and n_user >= 4 and rank == 128 and user_factors.shape[0] == 1024
    me = lax.axis_index(AXES).astype(i32).reshape(1)

    def swap(value, bit):
        return lax.ppermute(value, AXES, [(d, d ^ bit) for d in range(devices)])

    u0 = user_factors
    u2 = swap(u0, 2)
    u1 = swap(u0, 1)
    *es, c_hi, c_lo = histogram(
        me, tile_valid, tile_item, tile_user, tile_count, u0, num_items, item_dev, n_grp, n_user
    )
    u2, es[0] = lax.optimization_barrier((u2, es[0]))
    u3 = swap(u2, 1)
    got = [es[0], swap(es[1], 1), swap(es[2], 2), swap(es[3], 3)]
    us = [u0, u1, u2, u3]
    ut = transposed(us)
    n_items = num_items // n_grp
    n_half = n_items // 2
    start = begun(got[:2], us[:2], transposed(us[:2]), n_half, n_half, item_dev)
    if n_user == 8:
        n_far = n_half // 2
        chunks = n_far // item_dev
        sent = systems(got, us, ut, n_half + n_far, n_far, item_dev, False, start, 2, chunks)
        far_other = swap(sent, n_grp)
        ut, _ = lax.optimization_barrier((ut, sent))
        sent = systems(got, us, ut, n_half, n_far, item_dev, False, start, 2, 0)
        near_other = swap(sent, n_grp)
        ut, _ = lax.optimization_barrier((ut, sent))
        own = systems(got, us, ut, n_far, n_far, item_dev, True, us_cost=0.01)
        far = merged(own, far_other, item_dev, 0, True)
        parts = [swap(value, n_grp * 2 * (chunks + n)) for n, value in reversed(list(enumerate(far)))]
        ut, _ = lax.optimization_barrier((ut, far[0]))
        own = systems(got, us, ut, 0, n_far, item_dev, True)
        own, *near = merged(own, near_other, item_dev, 1, True)
        parts += [swap(value, n_grp * 2 * (n + 1)) for n, value in enumerate(near)]
    else:
        left, bit = n_user, n_grp
        sent = systems(got, us, ut, n_half, n_half, item_dev, False, start, 2)
        other = swap(sent, bit)
        own = systems(got, us, ut, 0, n_half, item_dev, True)
        left, bit = left // 2, bit * 2
        while left > 4:
            own, sent = merged(own, other, item_dev, left // 2, False)
            other = swap(sent, bit)
            left, bit = left // 2, bit * 2
        own, *sent = merged(own, other, item_dev, 1, True)
        parts = [swap(value, bit * (n + 1)) for n, value in enumerate(sent)]
    c_hi, c_lo, own, *parts[:2] = lax.optimization_barrier((c_hi, c_lo, own, *parts[:2]))
    c_hi, c_lo = flipped(c_hi, c_lo)
    own, c_hi = lax.optimization_barrier((own, c_hi))
    solved, spread = gradients(own, parts, prev_items, devices)
    returned = lax.all_to_all(spread, AXES, 0, 0, tiled=True).reshape(num_items, rank)
    return solved, user_side(me, returned, c_hi, c_lo, item_dev, n_grp, n_user)


def solution(mesh):
    return jax.shard_map(
        shards,
        mesh=mesh,
        in_specs=(
            P(AXES, None),
            P(AXES, None, None),
            P(AXES, None, None),
            P(AXES, None),
            P(AXES, None),
            P(AXES, None),
        ),
        out_specs=(P(AXES, None), P(AXES, None)),
        check_vma=False,
    )
```

```python
import functools

import jax
import jax.numpy as jnp
from jax import lax
from jax.experimental import pallas as pl
from jax.experimental.pallas import tpu as pltpu
from jax.sharding import PartitionSpec as P

CG_STEPS = 4
bf16, f32, i32 = jnp.bfloat16, jnp.float32, jnp.int32
AXES = ("user", "grp")
VMEM = pl.BlockSpec(memory_space=pltpu.VMEM)
SMEM = pl.BlockSpec(memory_space=pltpu.SMEM)
struct = jax.ShapeDtypeStruct

confidence_rate = 0.5
ridge_weight = 1.0


def log2(n):
    k = n.bit_length() - 1
    assert 1 << k == n
    return k


def cost(us):
    return pl.CostEstimate(flops=int(us * 1e9), bytes_accessed=int(us * 3e6), transcendentals=0)


def params(mib):
    return pltpu.CompilerParams(vmem_limit_bytes=mib << 20)


def slot_of(item, me, item_dev, n_grp, n_user):
    rel = (item >> log2(item_dev)) ^ me
    slot = item & (item_dev - 1)
    w = rel >> log2(n_grp)
    per, left = n_user * item_dev, n_user
    k = (rel & (n_grp - 1)) * per
    while left > 4:
        per, left = per // 2, left // 2
        k = k + (w & 1) * per
        w = w >> 1
    return k + w * item_dev + slot


def owner_of(group, item_dev, n_grp, n_user):
    k, w = divmod(group, n_user)
    bits, left, at = 0, n_user, 0
    while left > 4:
        left //= 2
        bits |= (w // left) << at
        w %= left
        at += 1
    return (bits | (w << at)) * n_grp + k


def histogram_kernel(step, low_part, item_dev, n_grp, n_user, me_s, *refs):
    sources, rest = refs[:5], refs[5:]
    eouts = rest[:n_grp]
    c_hi, c_lo, acc, *here, sem = rest[n_grp:]
    copies = [pltpu.make_async_copy(a, b, sem.at[n]) for n, (a, b) in enumerate(zip(sources, here))]
    for copy in copies:
        copy.start()
    valid_s, item_s, users, counts, u = here
    tiles, rows = users.shape[1:]
    num_items = c_hi.shape[0]
    block_users = u.shape[0]
    his = block_users // low_part
    kinds = 2 * his
    me = me_s[0]
    acc[...] = jnp.zeros_like(acc)
    for copy in copies[:4]:
        copy.wait()
    lane = lax.broadcasted_iota(i32, (his, rows), 1)
    sub = lax.broadcasted_iota(i32, (his, rows), 0)
    iota = lax.broadcasted_iota(i32, (low_part, rows), 0).astype(f32).astype(bf16)
    zero = jnp.zeros((kinds, rows), bf16)
    one, nil = jnp.ones((low_part, rows), bf16), jnp.zeros((low_part, rows), bf16)

    def body(b, _):
        base = pl.multiple_of(b * step, step)
        blk = users[0, pl.ds(base, step), :]
        cnt = counts[0, pl.ds(base, step), :].astype(f32) * confidence_rate
        lo = (blk & (low_part - 1)).astype(f32)
        hi = blk >> log2(low_part)
        for t in range(0, step, 2):
            oh, lhs = [], []
            for j in (t, t + 1):
                lob = jnp.broadcast_to(lo[j : j + 1], (16, rows)).astype(bf16)
                oh.append(jnp.where(jnp.concatenate([lob] * (low_part // 16), 0) == iota, one, nil))
                on = (lane < valid_s[0, base + j]) & (jnp.broadcast_to(hi[j : j + 1], (his, rows)) == sub)
                ex = jnp.broadcast_to(cnt[j : j + 1], (his, rows))
                lhs.append(
                    jnp.concatenate([jnp.where(on, ex, 0.0), jnp.where(on, 1.0 + ex, 0.0)], 0).astype(bf16)
                )
            left = jnp.concatenate(
                [jnp.concatenate([lhs[0], zero], 1), jnp.concatenate([zero, lhs[1]], 1)], 0
            )
            out = lax.dot_general(
                left, jnp.concatenate(oh, 1), (((1,), (1,)), ((), ())), preferred_element_type=f32
            )
            for q, j in enumerate((t, t + 1)):
                p = slot_of(item_s[0, base + j], me, item_dev, n_grp, n_user)
                acc[pl.ds(pl.multiple_of(p * kinds, kinds), kinds), :] += out[kinds * q : kinds * (q + 1)]
        return 0

    lax.fori_loop(0, tiles // step, body, 0)
    copies[4].wait()
    per = num_items // n_grp
    wide = 128 // low_part

    def row(h):
        parts = [acc[pl.ds(h * wide + n, num_items, stride=kinds), :] for n in range(wide)]
        return jnp.concatenate(parts, 1)

    for h in range(block_users // 128):
        e = (row(h) + 1.0).astype(bf16)
        for k in range(n_grp):
            eouts[k][:, h * 128 : (h + 1) * 128] = e[k * per : (k + 1) * per]
        c = row(his // wide + h)
        ch = c.astype(bf16)
        c_hi[:, h * 128 : (h + 1) * 128] = ch
        c_lo[:, h * 128 : (h + 1) * 128] = (c - ch.astype(f32)).astype(bf16)
    uu = u[...]
    r = jnp.dot(c_hi[...], uu, preferred_element_type=f32) + jnp.dot(c_lo[...], uu, preferred_element_type=f32)
    rh = r.astype(bf16)
    rl = (r - rh.astype(f32)).astype(bf16)
    for k in range(n_grp):
        eouts[k][:, block_users : block_users + 128] = rh[k * per : (k + 1) * per]
        eouts[k][:, block_users + 128 :] = rl[k * per : (k + 1) * per]


def histogram(me, valid, item, users, counts, u, num_items, item_dev, n_grp, n_user):
    block_users, rank = u.shape
    step, low_part = 128, 64
    return pl.pallas_call(
        functools.partial(histogram_kernel, step, low_part, item_dev, n_grp, n_user),
        in_specs=[SMEM] + [pl.BlockSpec(memory_space=pltpu.HBM)] * 5,
        out_specs=[VMEM] * (n_grp + 2),
        out_shape=[struct((num_items // n_grp, block_users + 2 * rank), bf16)] * n_grp
        + [struct((num_items, block_users), bf16)] * 2,
        scratch_shapes=[
            pltpu.VMEM((num_items * 2 * block_users // low_part, low_part), f32),
            pltpu.SMEM(valid.shape, i32),
            pltpu.SMEM(item.shape, i32),
            pltpu.VMEM(users.shape, i32),
            pltpu.VMEM(counts.shape, i32),
            pltpu.VMEM(u.shape, bf16),
            pltpu.SemaphoreType.DMA((5,)),
        ],
        compiler_params=params(32),
        cost_estimate=cost(7),
        name="histogram",
    )(me, *[pltpu.with_memory_space_constraint(v, pltpu.HBM) for v in (valid, item, users, counts, u)])


def transpose_kernel(*refs):
    *us, ut = refs
    block_users = us[0].shape[0]
    for b, u in enumerate(us):
        for c in range(block_users // 128):
            at = b * block_users + c * 128
            ut[:, at : at + 128] = u[c * 128 : (c + 1) * 128, :].T


def transposed(us):
    block_users, rank = us[0].shape
    return pl.pallas_call(
        transpose_kernel,
        in_specs=[VMEM] * len(us),
        out_specs=VMEM,
        out_shape=struct((rank, block_users * len(us)), bf16),
        compiler_params=params(16),
        cost_estimate=cost(0.2),
        name="transpose",
    )(*us)


def chunk_rows(item_dev):
    return 64 * item_dev + -(-4 * item_dev // 16) * 16


def partial_systems(rows, ut, us, c, item_dev, at):
    rank = ut.shape[0]
    w = []
    for j in range(item_dev):
        one = c * item_dev + j
        e = jnp.concatenate([r[one : one + 1] for r in rows], 1)
        e = jnp.broadcast_to(e, (16, e.shape[1])).astype(bf16)
        w.append(jnp.concatenate([e] * (rank // 16), 0) * ut[:, at : at + e.shape[1]])
    return jnp.dot(jnp.concatenate(w, 0), jnp.concatenate([u[...] for u in us], 0), preferred_element_type=f32)


def some_rows(ref, first, n, cols):
    low, high = first // 16 * 16, -(-(first + n) // 16) * 16
    return ref[low:high, cols].astype(f32)[first - low : first - low + n]


def begun_kernel(first, n_items, item_dev, n, *refs):
    es, us, ut, out = refs[:n], refs[n : 2 * n], refs[2 * n], refs[2 * n + 1]
    rows = [some_rows(e, first, n_items, slice(0, us[0].shape[0])) for e in es]
    for c in range(n_items // item_dev):
        out[c] = partial_systems(rows, ut, us, c, item_dev, 0)


def begun(es, us, ut, first, n_items, item_dev):
    n = len(es)
    block_users, rank = us[0].shape
    return pl.pallas_call(
        functools.partial(begun_kernel, first, n_items, item_dev, n),
        in_specs=[VMEM] * (2 * n + 1),
        out_specs=VMEM,
        out_shape=struct((n_items // item_dev, item_dev * rank, rank), f32),
        compiler_params=params(32),
        cost_estimate=cost(2.6),
        name="begun",
    )(*es, *us, ut)


def systems_kernel(first, n_items, item_dev, keep, n, done, at, *refs):
    es, us, ut = refs[:n], refs[n : 2 * n - done], refs[2 * n - done]
    start = refs[2 * n - done + 1] if done else None
    out = refs[-1]
    block_users, rank = us[0].shape
    rows = [some_rows(e, first, n_items, slice(0, block_users)) for e in es[done:]]
    rhs = jnp.zeros((n_items, rank), f32)
    for e in es:
        rhs = rhs + some_rows(e, first, n_items, slice(block_users, block_users + rank))
        rhs = rhs + some_rows(e, first, n_items, slice(block_users + rank, block_users + 2 * rank))
    row = lax.broadcasted_iota(i32, (64, rank), 0)
    lane = lax.broadcasted_iota(i32, (64, rank), 1)
    eye = lax.broadcasted_iota(i32, (rank, rank), 0) == lax.broadcasted_iota(i32, (rank, rank), 1)
    above = (lane < 64) & (lane > row)
    base = 64 * item_dev

    for c in range(n_items // item_dev):
        total = partial_systems(rows, ut, us, c, item_dev, done * block_users)
        if done:
            total = total + start[at + c]
        diag = []
        for j in range(item_dev):
            g = total[j * rank : (j + 1) * rank]
            packed = jnp.where(above, pltpu.roll(g[64:], 64, 1), g[:64])
            out[c, 64 * j : 64 * j + 64, :] = packed.astype(out.dtype)
            diag.append(jnp.sum(jnp.where(eye, g, 0.0), axis=0, keepdims=True))
        diag = jnp.concatenate(diag, 0)
        side = rhs[c * item_dev : (c + 1) * item_dev]
        put_extras(
            lambda a, n, v, c=c: out.__setitem__((c, slice(base + a, base + a + n)), v), diag, side, keep, item_dev
        )


def put_extras(put, diag, side, keep, item_dev):
    if keep:
        nil = jnp.zeros_like(diag)
        rows = [diag, nil, side, nil]
    else:
        rows = []
        for v in (diag, side):
            high = v.astype(bf16).astype(f32)
            rows += [high, v - high]
    pad = -4 * item_dev % 16
    if pad:
        rows.append(jnp.zeros((pad, diag.shape[1]), f32))
    value = jnp.concatenate(rows, 0)
    put(0, value.shape[0], value if keep else value.astype(bf16))


def systems(es, us, ut, first, n_items, item_dev, keep, start=None, done=0, at=0, us_cost=None):
    n = len(es)
    block_users, rank = us[0].shape
    more = [] if start is None else [start]
    return pl.pallas_call(
        functools.partial(systems_kernel, first, n_items, item_dev, keep, n, done, at),
        in_specs=[VMEM] * (2 * n - done + 1 + len(more)),
        out_specs=VMEM,
        out_shape=struct((n_items // item_dev, chunk_rows(item_dev), rank), f32 if keep else bf16),
        compiler_params=params(40),
        cost_estimate=cost(0.082 * (n - done) * n_items if us_cost is None else us_cost),
        name="systems",
    )(*es, *us[done:], ut, *more)


def extras(value, item_dev):
    base = 64 * item_dev
    part = [value[base + n * item_dev : base + (n + 1) * item_dev] for n in range(4)]
    return part[0] + part[1], part[2] + part[3]


def merge_kernel(item_dev, n_keep, apart, skip, own, got, *outs):
    kept, sent = outs[0], outs[bool(n_keep) :]
    base = 64 * item_dev
    for c in range(own.shape[0]):
        value = own[c] + got[c + skip].astype(f32)
        diag, side = extras(value, item_dev)
        if c < n_keep:
            kept[c, :base, :] = value[:base]
            put_extras(lambda a, n, v, c=c: kept.__setitem__((c, slice(base + a, base + a + n)), v), diag, side, True, item_dev)
        else:
            ref = sent[c - n_keep] if apart else sent[0]
            lead = () if apart else (c - n_keep,)
            ref[lead + (slice(0, base),)] = value[:base].astype(bf16)
            put_extras(
                lambda a, n, v, ref=ref, lead=lead: ref.__setitem__(lead + (slice(base + a, base + a + n),), v),
                diag, side, False, item_dev,
            )


def merged(own, got, item_dev, n_keep, apart, skip=0):
    chunks, rows, rank = own.shape
    n_sent = chunks - n_keep
    shapes = [struct((rows, rank), bf16)] * n_sent if apart else [struct((n_sent, rows, rank), bf16)]
    shapes = ([struct((n_keep, rows, rank), f32)] if n_keep else []) + shapes
    return pl.pallas_call(
        functools.partial(merge_kernel, item_dev, n_keep, apart, skip),
        in_specs=[VMEM] * 2,
        out_specs=[VMEM] * len(shapes),
        out_shape=shapes,
        compiler_params=params(16),
        name="merge",
    )(own, got)


def gradients_kernel(item_dev, own, *refs):
    *got, prev_far, out, half, prev, sem = refs
    fetch = pltpu.make_async_copy(prev_far, prev, sem)
    fetch.start()
    value = own[0]
    for g in got:
        value = value + (g[...] if len(g.shape) == 2 else g[0]).astype(f32)
    rank = value.shape[1]
    diag, side = extras(value, item_dev)
    row = lax.broadcasted_iota(i32, (64, 64), 0)
    col = lax.broadcasted_iota(i32, (64, 64), 1)
    eye = lax.broadcasted_iota(i32, (rank, rank), 0) == lax.broadcasted_iota(i32, (rank, rank), 1)
    matrices = []
    for j in range(item_dev):
        m = value[64 * j : 64 * j + 64]
        t = m.T
        mix, mix_t = m[:, :64], t[:64]
        a = jnp.where(col < row, mix, mix_t)
        c = jnp.where(col > row, mix, mix_t)
        full = jnp.concatenate(
            [jnp.concatenate([a, m[:, 64:]], 1), jnp.concatenate([t[64:], c], 1)], 0
        )
        matrices.append(jnp.where(eye, diag[j : j + 1] + ridge_weight, full))

    def apply(vector):
        rows = []
        for j in range(item_dev):
            s = jnp.sum(matrices[j] * vector[j : j + 1], axis=1, keepdims=True)
            rows.append(jnp.sum(jnp.where(eye, s, 0.0), axis=0, keepdims=True))
        return jnp.concatenate(rows, 0)

    fetch.wait()
    solution = prev[...]
    residual = side - apply(solution)
    direction = residual
    norm_now = jnp.sum(residual * residual, axis=1, keepdims=True)
    for _ in range(CG_STEPS):
        image = apply(direction)
        step = norm_now / jnp.sum(direction * image, axis=1, keepdims=True)
        solution = solution + step * direction
        residual = residual - step * image
        norm_next = jnp.sum(residual * residual, axis=1, keepdims=True)
        direction = residual + norm_next / norm_now * direction
        norm_now = norm_next
    out[...] = solution
    short = solution.astype(bf16)
    for d in range(half.shape[0]):
        half[d] = short


def gradients(own, got, prev, devices):
    item_dev, rank = prev.shape
    return pl.pallas_call(
        functools.partial(gradients_kernel, item_dev),
        in_specs=[VMEM] * (1 + len(got)) + [pl.BlockSpec(memory_space=pltpu.HBM)],
        out_specs=[VMEM] * 2,
        out_shape=[struct(prev.shape, f32), struct((devices,) + prev.shape, bf16)],
        scratch_shapes=[pltpu.VMEM(prev.shape, f32), pltpu.SemaphoreType.DMA(())],
        compiler_params=params(16),
        cost_estimate=cost(2),
        name="gradients",
    )(own, *got, pltpu.with_memory_space_constraint(prev, pltpu.HBM))


def user_side_kernel(item_dev, n_grp, n_user, me_s, returned, c_hi, c_lo, out, rows, order, made, sem):
    num_items = returned.shape[0]
    rows[...] = returned[...].astype(f32)
    me = me_s[0]
    for group in range(num_items // item_dev):
        owner = owner_of(group, item_dev, n_grp, n_user) ^ me
        order[group * item_dev : (group + 1) * item_dev, :] = rows[pl.ds(owner * item_dev, item_dev), :]
    ret = order[...].astype(bf16)
    copies = []
    for c in range(made.shape[0]):
        rows_c = slice(c * made.shape[1], (c + 1) * made.shape[1])
        made[c] = jnp.dot(c_hi[rows_c], ret, preferred_element_type=f32) + jnp.dot(
            c_lo[rows_c], ret, preferred_element_type=f32
        )
        copies.append(pltpu.make_async_copy(made.at[c], out.at[rows_c], sem.at[c]))
        copies[-1].start()
    for copy in copies:
        copy.wait()


def user_side(me, returned, c_hi, c_lo, item_dev, n_grp, n_user):
    num_items, rank = returned.shape
    pieces = 4
    return pl.pallas_call(
        functools.partial(user_side_kernel, item_dev, n_grp, n_user),
        in_specs=[SMEM, VMEM, VMEM, VMEM],
        out_specs=pl.BlockSpec(memory_space=pltpu.HBM),
        out_shape=struct((c_hi.shape[0], rank), f32),
        scratch_shapes=[pltpu.VMEM((num_items, rank), f32)] * 2
        + [pltpu.VMEM((pieces, c_hi.shape[0] // pieces, rank), f32), pltpu.SemaphoreType.DMA((pieces,))],
        compiler_params=params(16),
        cost_estimate=cost(1),
        name="user_side",
    )(me, returned, c_hi, c_lo)


def flip_kernel(*refs):
    n = len(refs) // 2
    for a, b in zip(refs[:n], refs[n:]):
        for c in range(a.shape[1] // 128):
            b[c * 128 : (c + 1) * 128, :] = a[:, c * 128 : (c + 1) * 128].T


def flipped(*values):
    return pl.pallas_call(
        flip_kernel,
        in_specs=[VMEM] * len(values),
        out_specs=[VMEM] * len(values),
        out_shape=[struct(v.shape[::-1], v.dtype) for v in values],
        compiler_params=params(16),
        cost_estimate=cost(8),
        name="flip",
    )(*values)


def shards(user_factors, tile_user, tile_count, tile_valid, tile_item, prev_items):
    n_user = lax.axis_size("user")
    n_grp = lax.axis_size("grp")
    devices = n_user * n_grp
    item_dev, rank = prev_items.shape
    num_items = item_dev * devices
    assert n_grp == 4 and n_user >= 4 and rank == 128 and user_factors.shape[0] == 1024
    me = lax.axis_index(AXES).astype(i32).reshape(1)

    def swap(value, bit):
        return lax.ppermute(value, AXES, [(d, d ^ bit) for d in range(devices)])

    u0 = user_factors
    u2 = swap(u0, 2)
    u1 = swap(u0, 1)
    *es, c_hi, c_lo = histogram(
        me, tile_valid, tile_item, tile_user, tile_count, u0, num_items, item_dev, n_grp, n_user
    )
    u2, es[0] = lax.optimization_barrier((u2, es[0]))
    u3 = swap(u2, 1)
    got = [es[0], swap(es[1], 1), swap(es[2], 2), swap(es[3], 3)]
    us = [u0, u1, u2, u3]
    ut = transposed(us)
    n_items = num_items // n_grp
    n_half = n_items // 2
    start = begun(got[:2], us[:2], transposed(us[:2]), n_half, n_half, item_dev)
    if n_user == 8:
        n_far = n_half // 2
        chunks = n_far // item_dev
        sent = systems(got, us, ut, n_half + n_far, n_far, item_dev, False, start, 2, chunks)
        far_other = swap(sent, n_grp)
        ut, _ = lax.optimization_barrier((ut, sent))
        sent = systems(got, us, ut, n_half, n_far, item_dev, False, start, 2, 0)
        near_other = swap(sent, n_grp)
        ut, _ = lax.optimization_barrier((ut, sent))
        own = systems(got, us, ut, n_far, n_far, item_dev, True, us_cost=0.01)
        far = merged(own, far_other, item_dev, 0, True)
        parts = [swap(value, n_grp * 2 * (chunks + n)) for n, value in reversed(list(enumerate(far)))]
        ut, _ = lax.optimization_barrier((ut, far[0]))
        own = systems(got, us, ut, item_dev, n_far - item_dev, item_dev, True)
        near = merged(own, near_other, item_dev, 0, True, 1)
        parts += [swap(value, n_grp * 2 * (n + 1)) for n, value in enumerate(near)]
        ut, _ = lax.optimization_barrier((ut, own))
        own = systems(got, us, ut, 0, item_dev, item_dev, True)
        parts.append(near_other)
    else:
        left, bit = n_user, n_grp
        sent = systems(got, us, ut, n_half, n_half, item_dev, False, start, 2)
        other = swap(sent, bit)
        own = systems(got, us, ut, 0, n_half, item_dev, True)
        left, bit = left // 2, bit * 2
        while left > 4:
            own, sent = merged(own, other, item_dev, left // 2, False)
            other = swap(sent, bit)
            left, bit = left // 2, bit * 2
        own, *sent = merged(own, other, item_dev, 1, True)
        parts = [swap(value, bit * (n + 1)) for n, value in enumerate(sent)]
    c_hi, c_lo, own, *parts[:2] = lax.optimization_barrier((c_hi, c_lo, own, *parts[:2]))
    c_hi, c_lo = flipped(c_hi, c_lo)
    own, c_hi = lax.optimization_barrier((own, c_hi))
    solved, spread = gradients(own, parts, prev_items, devices)
    returned = lax.all_to_all(spread, AXES, 0, 0, tiled=True).reshape(num_items, rank)
    return solved, user_side(me, returned, c_hi, c_lo, item_dev, n_grp, n_user)


def solution(mesh):
    return jax.shard_map(
        shards,
        mesh=mesh,
        in_specs=(
            P(AXES, None),
            P(AXES, None, None),
            P(AXES, None, None),
            P(AXES, None),
            P(AXES, None),
            P(AXES, None),
        ),
        out_specs=(P(AXES, None), P(AXES, None)),
        check_vma=False,
    )
```

```python
import functools

import jax
import jax.numpy as jnp
from jax import lax
from jax.experimental import pallas as pl
from jax.experimental.pallas import tpu as pltpu
from jax.sharding import PartitionSpec as P

CG_STEPS = 4
bf16, f32, i32 = jnp.bfloat16, jnp.float32, jnp.int32
AXES = ("user", "grp")
VMEM = pl.BlockSpec(memory_space=pltpu.VMEM)
SMEM = pl.BlockSpec(memory_space=pltpu.SMEM)
struct = jax.ShapeDtypeStruct

confidence_rate = 0.5
ridge_weight = 1.0


def log2(n):
    k = n.bit_length() - 1
    assert 1 << k == n
    return k


def cost(us):
    return pl.CostEstimate(flops=int(us * 1e9), bytes_accessed=int(us * 3e6), transcendentals=0)


def params(mib):
    return pltpu.CompilerParams(vmem_limit_bytes=mib << 20)


def slot_of(item, me, item_dev, n_grp, n_user):
    rel = (item >> log2(item_dev)) ^ me
    slot = item & (item_dev - 1)
    w = rel >> log2(n_grp)
    per, left = n_user * item_dev, n_user
    k = (rel & (n_grp - 1)) * per
    while left > 4:
        per, left = per // 2, left // 2
        k = k + (w & 1) * per
        w = w >> 1
    return k + w * item_dev + slot


def owner_of(group, item_dev, n_grp, n_user):
    k, w = divmod(group, n_user)
    bits, left, at = 0, n_user, 0
    while left > 4:
        left //= 2
        bits |= (w // left) << at
        w %= left
        at += 1
    return (bits | (w << at)) * n_grp + k


def histogram_kernel(step, low_part, item_dev, n_grp, n_user, me_s, *refs):
    sources, rest = refs[:6], refs[6:]
    eouts = rest[:n_grp]
    c_hi, c_lo, prev_here, acc, *here, sem = rest[n_grp:]
    here.append(prev_here)
    copies = [pltpu.make_async_copy(a, b, sem.at[n]) for n, (a, b) in enumerate(zip(sources, here))]
    for copy in copies:
        copy.start()
    valid_s, item_s, users, counts, u, _ = here
    tiles, rows = users.shape[1:]
    num_items = c_hi.shape[0]
    block_users = u.shape[0]
    his = block_users // low_part
    kinds = 2 * his
    pitch = kinds + 8
    me = me_s[0]
    for copy in copies[:4]:
        copy.wait()
    lane = lax.broadcasted_iota(i32, (his, rows), 1)
    sub = lax.broadcasted_iota(i32, (his, rows), 0)
    iota = lax.broadcasted_iota(i32, (low_part, rows), 0).astype(f32).astype(bf16)
    zero = jnp.zeros((kinds, rows), bf16)
    one, nil = jnp.ones((low_part, rows), bf16), jnp.zeros((low_part, rows), bf16)

    def body(b, run):
        base = pl.multiple_of(b * step, step)
        blk = users[0, pl.ds(base, step), :]
        cnt = counts[0, pl.ds(base, step), :].astype(f32) * confidence_rate
        lo = (blk & (low_part - 1)).astype(f32)
        hi = blk >> log2(low_part)
        for t in range(0, step, 2):
            oh, lhs = [], []
            for j in (t, t + 1):
                lob = jnp.broadcast_to(lo[j : j + 1], (16, rows)).astype(bf16)
                oh.append(jnp.where(jnp.concatenate([lob] * (low_part // 16), 0) == iota, one, nil))
                on = (lane < valid_s[0, base + j]) & (jnp.broadcast_to(hi[j : j + 1], (his, rows)) == sub)
                ex = jnp.broadcast_to(cnt[j : j + 1], (his, rows))
                lhs.append(
                    jnp.concatenate([jnp.where(on, ex, 0.0), jnp.where(on, 1.0 + ex, 0.0)], 0).astype(bf16)
                )
            left = jnp.concatenate(
                [jnp.concatenate([lhs[0], zero], 1), jnp.concatenate([zero, lhs[1]], 1)], 0
            )
            out = lax.dot_general(
                left, jnp.concatenate(oh, 1), (((1,), (1,)), ((), ())), preferred_element_type=f32
            )
            for q, j in enumerate((t, t + 1)):
                item, before = item_s[0, base + j], item_s[0, jnp.maximum(base + j - 1, 0)]
                run = jnp.where(item == before, 1.0, 0.0) * run + out[kinds * q : kinds * (q + 1)]
                p = slot_of(item, me, item_dev, n_grp, n_user)
                acc[pl.ds(pl.multiple_of(p * pitch, 8), kinds), :] = run
        return run

    lax.fori_loop(0, tiles // step, body, jnp.zeros((kinds, low_part), f32))
    copies[4].wait()
    copies[5].wait()
    per = num_items // n_grp
    wide = 128 // low_part

    def row(h):
        parts = [acc[pl.ds(h * wide + n, num_items, stride=pitch), :] for n in range(wide)]
        return jnp.concatenate(parts, 1)

    for h in range(block_users // 128):
        e = (row(h) + 1.0).astype(bf16)
        for k in range(n_grp):
            eouts[k][:, h * 128 : (h + 1) * 128] = e[k * per : (k + 1) * per]
        c = row(his // wide + h)
        ch = c.astype(bf16)
        c_hi[:, h * 128 : (h + 1) * 128] = ch
        c_lo[:, h * 128 : (h + 1) * 128] = (c - ch.astype(f32)).astype(bf16)
    uu = u[...]
    r = jnp.dot(c_hi[...], uu, preferred_element_type=f32) + jnp.dot(c_lo[...], uu, preferred_element_type=f32)
    rh = r.astype(bf16)
    rl = (r - rh.astype(f32)).astype(bf16)
    for k in range(n_grp):
        eouts[k][:, block_users : block_users + 128] = rh[k * per : (k + 1) * per]
        eouts[k][:, block_users + 128 :] = rl[k * per : (k + 1) * per]


def histogram(me, valid, item, users, counts, u, prev, num_items, item_dev, n_grp, n_user):
    block_users, rank = u.shape
    step, low_part = 192, 64
    assert users.shape[1] % step == 0
    return pl.pallas_call(
        functools.partial(histogram_kernel, step, low_part, item_dev, n_grp, n_user),
        in_specs=[SMEM] + [pl.BlockSpec(memory_space=pltpu.HBM)] * 6,
        out_specs=[VMEM] * (n_grp + 3),
        out_shape=[struct((num_items // n_grp, block_users + 2 * rank), bf16)] * n_grp
        + [struct((num_items, block_users), bf16)] * 2
        + [struct(prev.shape, f32)],
        scratch_shapes=[
            pltpu.VMEM((num_items * (2 * block_users // low_part + 8), low_part), f32),
            pltpu.SMEM(valid.shape, i32),
            pltpu.SMEM(item.shape, i32),
            pltpu.VMEM(users.shape, i32),
            pltpu.VMEM(counts.shape, i32),
            pltpu.VMEM(u.shape, bf16),
            pltpu.SemaphoreType.DMA((6,)),
        ],
        compiler_params=params(32),
        cost_estimate=cost(7),
        name="histogram",
    )(me, *[pltpu.with_memory_space_constraint(v, pltpu.HBM) for v in (valid, item, users, counts, u, prev)])


def transpose_kernel(*refs):
    *us, ut = refs
    block_users = us[0].shape[0]
    for b, u in enumerate(us):
        for c in range(block_users // 128):
            at = b * block_users + c * 128
            ut[:, at : at + 128] = u[c * 128 : (c + 1) * 128, :].T


def transposed(us):
    block_users, rank = us[0].shape
    return pl.pallas_call(
        transpose_kernel,
        in_specs=[VMEM] * len(us),
        out_specs=VMEM,
        out_shape=struct((rank, block_users * len(us)), bf16),
        compiler_params=params(16),
        cost_estimate=cost(0.2),
        name="transpose",
    )(*us)


def chunk_rows(item_dev):
    return 64 * item_dev + -(-4 * item_dev // 16) * 16


def partial_systems(rows, ut, us, c, item_dev, at):
    rank = ut.shape[0]
    w = []
    for j in range(item_dev):
        one = c * item_dev + j
        e = jnp.concatenate([r[one : one + 1] for r in rows], 1)
        e = jnp.broadcast_to(e, (16, e.shape[1])).astype(bf16)
        w.append(jnp.concatenate([e] * (rank // 16), 0) * ut[:, at : at + e.shape[1]])
    return jnp.dot(jnp.concatenate(w, 0), jnp.concatenate([u[...] for u in us], 0), preferred_element_type=f32)


def some_rows(ref, first, n, cols):
    low, high = first // 16 * 16, -(-(first + n) // 16) * 16
    return ref[low:high, cols].astype(f32)[first - low : first - low + n]


def begun_kernel(first, n_items, item_dev, n, *refs):
    es, us, ut, out = refs[:n], refs[n : 2 * n], refs[2 * n], refs[2 * n + 1]
    rows = [some_rows(e, first, n_items, slice(0, us[0].shape[0])) for e in es]
    for c in range(n_items // item_dev):
        out[c] = partial_systems(rows, ut, us, c, item_dev, 0)


def begun(es, us, ut, first, n_items, item_dev):
    n = len(es)
    block_users, rank = us[0].shape
    return pl.pallas_call(
        functools.partial(begun_kernel, first, n_items, item_dev, n),
        in_specs=[VMEM] * (2 * n + 1),
        out_specs=VMEM,
        out_shape=struct((n_items // item_dev, item_dev * rank, rank), f32),
        compiler_params=params(32),
        cost_estimate=cost(2.6),
        name="begun",
    )(*es, *us, ut)


def systems_kernel(first, n_items, item_dev, keep, n, done, at, *refs):
    es, us, ut = refs[:n], refs[n : 2 * n - done], refs[2 * n - done]
    start = refs[2 * n - done + 1] if done else None
    out = refs[-1]
    block_users, rank = us[0].shape
    rows = [some_rows(e, first, n_items, slice(0, block_users)) for e in es[done:]]
    rhs = jnp.zeros((n_items, rank), f32)
    for e in es:
        rhs = rhs + some_rows(e, first, n_items, slice(block_users, block_users + rank))
        rhs = rhs + some_rows(e, first, n_items, slice(block_users + rank, block_users + 2 * rank))
    row = lax.broadcasted_iota(i32, (64, rank), 0)
    lane = lax.broadcasted_iota(i32, (64, rank), 1)
    eye = lax.broadcasted_iota(i32, (rank, rank), 0) == lax.broadcasted_iota(i32, (rank, rank), 1)
    above = (lane < 64) & (lane > row)
    base = 64 * item_dev

    for c in range(n_items // item_dev):
        total = partial_systems(rows, ut, us, c, item_dev, done * block_users)
        if done:
            total = total + start[at + c]
        diag = []
        for j in range(item_dev):
            g = total[j * rank : (j + 1) * rank]
            packed = jnp.where(above, pltpu.roll(g[64:], 64, 1), g[:64])
            out[c, 64 * j : 64 * j + 64, :] = packed.astype(out.dtype)
            diag.append(jnp.sum(jnp.where(eye, g, 0.0), axis=0, keepdims=True))
        diag = jnp.concatenate(diag, 0)
        side = rhs[c * item_dev : (c + 1) * item_dev]
        put_extras(
            lambda a, n, v, c=c: out.__setitem__((c, slice(base + a, base + a + n)), v), diag, side, keep, item_dev
        )


def put_extras(put, diag, side, keep, item_dev):
    if keep:
        nil = jnp.zeros_like(diag)
        rows = [diag, nil, side, nil]
    else:
        rows = []
        for v in (diag, side):
            high = v.astype(bf16).astype(f32)
            rows += [high, v - high]
    pad = -4 * item_dev % 16
    if pad:
        rows.append(jnp.zeros((pad, diag.shape[1]), f32))
    value = jnp.concatenate(rows, 0)
    put(0, value.shape[0], value if keep else value.astype(bf16))


def systems(es, us, ut, first, n_items, item_dev, keep, start=None, done=0, at=0, us_cost=None):
    n = len(es)
    block_users, rank = us[0].shape
    more = [] if start is None else [start]
    return pl.pallas_call(
        functools.partial(systems_kernel, first, n_items, item_dev, keep, n, done, at),
        in_specs=[VMEM] * (2 * n - done + 1 + len(more)),
        out_specs=VMEM,
        out_shape=struct((n_items // item_dev, chunk_rows(item_dev), rank), f32 if keep else bf16),
        compiler_params=params(40),
        cost_estimate=cost(0.082 * (n - done) * n_items if us_cost is None else us_cost),
        name="systems",
    )(*es, *us[done:], ut, *more)


def extras(value, item_dev):
    base = 64 * item_dev
    part = [value[base + n * item_dev : base + (n + 1) * item_dev] for n in range(4)]
    return part[0] + part[1], part[2] + part[3]


def merge_kernel(item_dev, n_keep, apart, skip, own, got, *outs):
    kept, sent = outs[0], outs[bool(n_keep) :]
    base = 64 * item_dev
    for c in range(own.shape[0]):
        value = own[c] + got[c + skip].astype(f32)
        diag, side = extras(value, item_dev)
        if c < n_keep:
            kept[c, :base, :] = value[:base]
            put_extras(lambda a, n, v, c=c: kept.__setitem__((c, slice(base + a, base + a + n)), v), diag, side, True, item_dev)
        else:
            ref = sent[c - n_keep] if apart else sent[0]
            lead = () if apart else (c - n_keep,)
            ref[lead + (slice(0, base),)] = value[:base].astype(bf16)
            put_extras(
                lambda a, n, v, ref=ref, lead=lead: ref.__setitem__(lead + (slice(base + a, base + a + n),), v),
                diag, side, False, item_dev,
            )


def merged(own, got, item_dev, n_keep, apart, skip=0):
    chunks, rows, rank = own.shape
    n_sent = chunks - n_keep
    shapes = [struct((rows, rank), bf16)] * n_sent if apart else [struct((n_sent, rows, rank), bf16)]
    shapes = ([struct((n_keep, rows, rank), f32)] if n_keep else []) + shapes
    return pl.pallas_call(
        functools.partial(merge_kernel, item_dev, n_keep, apart, skip),
        in_specs=[VMEM] * 2,
        out_specs=[VMEM] * len(shapes),
        out_shape=shapes,
        compiler_params=params(16),
        name="merge",
    )(own, got)


def gradients_kernel(item_dev, own, *refs):
    *got, prev, out, half = refs
    value = own[0]
    for g in got:
        value = value + (g[...] if len(g.shape) == 2 else g[0]).astype(f32)
    rank = value.shape[1]
    diag, side = extras(value, item_dev)
    row = lax.broadcasted_iota(i32, (64, 64), 0)
    col = lax.broadcasted_iota(i32, (64, 64), 1)
    eye = lax.broadcasted_iota(i32, (rank, rank), 0) == lax.broadcasted_iota(i32, (rank, rank), 1)
    matrices = []
    for j in range(item_dev):
        m = value[64 * j : 64 * j + 64]
        t = m.T
        mix, mix_t = m[:, :64], t[:64]
        a = jnp.where(col < row, mix, mix_t)
        c = jnp.where(col > row, mix, mix_t)
        full = jnp.concatenate(
            [jnp.concatenate([a, m[:, 64:]], 1), jnp.concatenate([t[64:], c], 1)], 0
        )
        matrices.append(jnp.where(eye, diag[j : j + 1] + ridge_weight, full))

    def apply(vector):
        rows = []
        for j in range(item_dev):
            s = jnp.sum(matrices[j] * vector[j : j + 1], axis=1, keepdims=True)
            rows.append(jnp.sum(jnp.where(eye, s, 0.0), axis=0, keepdims=True))
        return jnp.concatenate(rows, 0)

    solution = prev[...]
    residual = side - apply(solution)
    direction = residual
    norm_now = jnp.sum(residual * residual, axis=1, keepdims=True)
    for _ in range(CG_STEPS):
        image = apply(direction)
        step = norm_now / jnp.sum(direction * image, axis=1, keepdims=True)
        solution = solution + step * direction
        residual = residual - step * image
        norm_next = jnp.sum(residual * residual, axis=1, keepdims=True)
        direction = residual + norm_next / norm_now * direction
        norm_now = norm_next
    out[...] = solution
    short = solution.astype(bf16)
    for d in range(half.shape[0]):
        half[d] = short


def gradients(own, got, prev, devices):
    item_dev, rank = prev.shape
    return pl.pallas_call(
        functools.partial(gradients_kernel, item_dev),
        in_specs=[VMEM] * (2 + len(got)),
        out_specs=[VMEM] * 2,
        out_shape=[struct(prev.shape, f32), struct((devices,) + prev.shape, bf16)],
        compiler_params=params(16),
        cost_estimate=cost(2),
        name="gradients",
    )(own, *got, prev)


def user_side_kernel(item_dev, n_grp, n_user, me_s, returned, c_hi, c_lo, out, rows, order, made, sem):
    num_items = returned.shape[0]
    rows[...] = returned[...].astype(f32)
    me = me_s[0]
    for group in range(num_items // item_dev):
        owner = owner_of(group, item_dev, n_grp, n_user) ^ me
        order[group * item_dev : (group + 1) * item_dev, :] = rows[pl.ds(owner * item_dev, item_dev), :]
    ret = order[...].astype(bf16)
    copies = []
    for c in range(made.shape[0]):
        rows_c = slice(c * made.shape[1], (c + 1) * made.shape[1])
        made[c] = jnp.dot(c_hi[rows_c], ret, preferred_element_type=f32) + jnp.dot(
            c_lo[rows_c], ret, preferred_element_type=f32
        )
        copies.append(pltpu.make_async_copy(made.at[c], out.at[rows_c], sem.at[c]))
        copies[-1].start()
    for copy in copies:
        copy.wait()


def user_side(me, returned, c_hi, c_lo, item_dev, n_grp, n_user):
    num_items, rank = returned.shape
    pieces = 4
    return pl.pallas_call(
        functools.partial(user_side_kernel, item_dev, n_grp, n_user),
        in_specs=[SMEM, VMEM, VMEM, VMEM],
        out_specs=pl.BlockSpec(memory_space=pltpu.HBM),
        out_shape=struct((c_hi.shape[0], rank), f32),
        scratch_shapes=[pltpu.VMEM((num_items, rank), f32)] * 2
        + [pltpu.VMEM((pieces, c_hi.shape[0] // pieces, rank), f32), pltpu.SemaphoreType.DMA((pieces,))],
        compiler_params=params(16),
        cost_estimate=cost(1),
        name="user_side",
    )(me, returned, c_hi, c_lo)


def flip_kernel(*refs):
    n = len(refs) // 2
    for a, b in zip(refs[:n], refs[n:]):
        for c in range(a.shape[1] // 128):
            b[c * 128 : (c + 1) * 128, :] = a[:, c * 128 : (c + 1) * 128].T


def flipped(*values):
    return pl.pallas_call(
        flip_kernel,
        in_specs=[VMEM] * len(values),
        out_specs=[VMEM] * len(values),
        out_shape=[struct(v.shape[::-1], v.dtype) for v in values],
        compiler_params=params(16),
        cost_estimate=cost(8),
        name="flip",
    )(*values)


def shards(user_factors, tile_user, tile_count, tile_valid, tile_item, prev_items):
    n_user = lax.axis_size("user")
    n_grp = lax.axis_size("grp")
    devices = n_user * n_grp
    item_dev, rank = prev_items.shape
    num_items = item_dev * devices
    assert n_grp == 4 and n_user >= 4 and rank == 128 and user_factors.shape[0] == 1024
    me = lax.axis_index(AXES).astype(i32).reshape(1)

    def swap(value, bit):
        return lax.ppermute(value, AXES, [(d, d ^ bit) for d in range(devices)])

    u0 = user_factors
    u2 = swap(u0, 2)
    u1 = swap(u0, 1)
    *es, c_hi, c_lo, prev = histogram(
        me, tile_valid, tile_item, tile_user, tile_count, u0, prev_items, num_items, item_dev, n_grp, n_user
    )
    u2, es[0] = lax.optimization_barrier((u2, es[0]))
    u3 = swap(u2, 1)
    got = [es[0], swap(es[1], 1), swap(es[2], 2), swap(es[3], 3)]
    us = [u0, u1, u2, u3]
    ut = transposed(us)
    n_items = num_items // n_grp
    n_half = n_items // 2
    start = begun(got[:2], us[:2], transposed(us[:2]), n_half, n_half, item_dev)
    if n_user == 8:
        n_far = n_half // 2
        chunks = n_far // item_dev
        sent = systems(got, us, ut, n_half + n_far, n_far, item_dev, False, start, 2, chunks)
        far_other = swap(sent, n_grp)
        ut, _ = lax.optimization_barrier((ut, sent))
        sent = systems(got, us, ut, n_half, n_far, item_dev, False, start, 2, 0)
        near_other = swap(sent, n_grp)
        ut, _ = lax.optimization_barrier((ut, sent))
        own = systems(got, us, ut, n_far, n_far, item_dev, True, us_cost=0.01)
        far = merged(own, far_other, item_dev, 0, True)
        parts = [swap(value, n_grp * 2 * (chunks + n)) for n, value in reversed(list(enumerate(far)))]
        ut, _ = lax.optimization_barrier((ut, far[0]))
        own = systems(got, us, ut, item_dev, n_far - item_dev, item_dev, True)
        near = merged(own, near_other, item_dev, 0, True, 1)
        parts += [swap(value, n_grp * 2 * (n + 1)) for n, value in enumerate(near)]
        ut, _ = lax.optimization_barrier((ut, own))
        own = systems(got, us, ut, 0, item_dev, item_dev, True)
        parts.append(near_other)
    else:
        left, bit = n_user, n_grp
        sent = systems(got, us, ut, n_half, n_half, item_dev, False, start, 2)
        other = swap(sent, bit)
        own = systems(got, us, ut, 0, n_half, item_dev, True)
        left, bit = left // 2, bit * 2
        while left > 4:
            own, sent = merged(own, other, item_dev, left // 2, False)
            other = swap(sent, bit)
            left, bit = left // 2, bit * 2
        own, *sent = merged(own, other, item_dev, 1, True)
        parts = [swap(value, bit * (n + 1)) for n, value in enumerate(sent)]
    c_hi, c_lo, own, *parts[:2] = lax.optimization_barrier((c_hi, c_lo, own, *parts[:2]))
    c_hi, c_lo = flipped(c_hi, c_lo)
    own, c_hi = lax.optimization_barrier((own, c_hi))
    solved, spread = gradients(own, parts, prev, devices)
    returned = lax.all_to_all(spread, AXES, 0, 0, tiled=True).reshape(num_items, rank)
    return solved, user_side(me, returned, c_hi, c_lo, item_dev, n_grp, n_user)


def solution(mesh):
    return jax.shard_map(
        shards,
        mesh=mesh,
        in_specs=(
            P(AXES, None),
            P(AXES, None, None),
            P(AXES, None, None),
            P(AXES, None),
            P(AXES, None),
            P(AXES, None),
        ),
        out_specs=(P(AXES, None), P(AXES, None)),
        check_vma=False,
    )
```

```python
import functools

import jax
import jax.numpy as jnp
from jax import lax
from jax.experimental import pallas as pl
from jax.experimental.pallas import tpu as pltpu
from jax.sharding import PartitionSpec as P

CG_STEPS = 4
bf16, f32, i32 = jnp.bfloat16, jnp.float32, jnp.int32
AXES = ("user", "grp")
VMEM = pl.BlockSpec(memory_space=pltpu.VMEM)
SMEM = pl.BlockSpec(memory_space=pltpu.SMEM)
struct = jax.ShapeDtypeStruct

confidence_rate = 0.5
ridge_weight = 1.0


def log2(n):
    k = n.bit_length() - 1
    assert 1 << k == n
    return k


def cost(us):
    return pl.CostEstimate(flops=int(us * 1e9), bytes_accessed=int(us * 3e6), transcendentals=0)


def params(mib):
    return pltpu.CompilerParams(vmem_limit_bytes=mib << 20)


def slot_of(item, me, item_dev, n_grp, n_user):
    rel = (item >> log2(item_dev)) ^ me
    slot = item & (item_dev - 1)
    w = rel >> log2(n_grp)
    per, left = n_user * item_dev, n_user
    k = (rel & (n_grp - 1)) * per
    while left > 4:
        per, left = per // 2, left // 2
        k = k + (w & 1) * per
        w = w >> 1
    return k + w * item_dev + slot


def owner_of(group, item_dev, n_grp, n_user):
    k, w = divmod(group, n_user)
    bits, left, at = 0, n_user, 0
    while left > 4:
        left //= 2
        bits |= (w // left) << at
        w %= left
        at += 1
    return (bits | (w << at)) * n_grp + k


def histogram_kernel(step, low_part, item_dev, n_grp, n_user, me_s, *refs):
    sources, rest = refs[:6], refs[6:]
    eouts = rest[:n_grp]
    c_hi, c_lo, prev_here, acc, *here, sem = rest[n_grp:]
    here.append(prev_here)
    copies = [pltpu.make_async_copy(a, b, sem.at[n]) for n, (a, b) in enumerate(zip(sources, here))]
    for copy in copies:
        copy.start()
    valid_s, item_s, users, counts, u, _ = here
    tiles, rows = users.shape[1:]
    num_items = c_hi.shape[0]
    block_users = u.shape[0]
    his = block_users // low_part
    kinds = 2 * his
    pitch = kinds + 8
    me = me_s[0]
    for copy in copies[:4]:
        copy.wait()
    lane = lax.broadcasted_iota(i32, (his, rows), 1)
    sub = lax.broadcasted_iota(i32, (his, rows), 0)
    iota = lax.broadcasted_iota(i32, (low_part, rows), 0).astype(f32).astype(bf16)
    zero = jnp.zeros((kinds, rows), bf16)
    one, nil = jnp.ones((low_part, rows), bf16), jnp.zeros((low_part, rows), bf16)

    def body(b, run):
        base = pl.multiple_of(b * step, step)
        blk = users[0, pl.ds(base, step), :]
        cnt = counts[0, pl.ds(base, step), :].astype(f32) * confidence_rate
        lo = (blk & (low_part - 1)).astype(f32)
        hi = blk >> log2(low_part)
        for t in range(0, step, 2):
            oh, lhs = [], []
            for j in (t, t + 1):
                lob = jnp.broadcast_to(lo[j : j + 1], (16, rows)).astype(bf16)
                oh.append(jnp.where(jnp.concatenate([lob] * (low_part // 16), 0) == iota, one, nil))
                on = (lane < valid_s[0, base + j]) & (jnp.broadcast_to(hi[j : j + 1], (his, rows)) == sub)
                ex = jnp.broadcast_to(cnt[j : j + 1], (his, rows))
                lhs.append(
                    jnp.concatenate([jnp.where(on, ex, 0.0), jnp.where(on, 1.0 + ex, 0.0)], 0).astype(bf16)
                )
            left = jnp.concatenate(
                [jnp.concatenate([lhs[0], zero], 1), jnp.concatenate([zero, lhs[1]], 1)], 0
            )
            out = lax.dot_general(
                left, jnp.concatenate(oh, 1), (((1,), (1,)), ((), ())), preferred_element_type=f32
            )
            for q, j in enumerate((t, t + 1)):
                item, before = item_s[0, base + j], item_s[0, jnp.maximum(base + j - 1, 0)]
                run = jnp.where(item == before, 1.0, 0.0) * run + out[kinds * q : kinds * (q + 1)]
                p = slot_of(item, me, item_dev, n_grp, n_user)
                acc[pl.ds(pl.multiple_of(p * pitch, 8), kinds), :] = run
        return run

    lax.fori_loop(0, tiles // step, body, jnp.zeros((kinds, low_part), f32))
    copies[4].wait()
    copies[5].wait()
    per = num_items // n_grp
    wide = 128 // low_part

    def row(h):
        parts = [acc[pl.ds(h * wide + n, num_items, stride=pitch), :] for n in range(wide)]
        return jnp.concatenate(parts, 1)

    for h in range(block_users // 128):
        e = (row(h) + 1.0).astype(bf16)
        for k in range(n_grp):
            eouts[k][:, h * 128 : (h + 1) * 128] = e[k * per : (k + 1) * per]
        c = row(his // wide + h)
        ch = c.astype(bf16)
        c_hi[:, h * 128 : (h + 1) * 128] = ch
        c_lo[:, h * 128 : (h + 1) * 128] = (c - ch.astype(f32)).astype(bf16)
    uu = u[...]
    r = jnp.dot(c_hi[...], uu, preferred_element_type=f32) + jnp.dot(c_lo[...], uu, preferred_element_type=f32)
    rh = r.astype(bf16)
    rl = (r - rh.astype(f32)).astype(bf16)
    for k in range(n_grp):
        eouts[k][:, block_users : block_users + 128] = rh[k * per : (k + 1) * per]
        eouts[k][:, block_users + 128 :] = rl[k * per : (k + 1) * per]


def histogram(me, valid, item, users, counts, u, prev, num_items, item_dev, n_grp, n_user):
    block_users, rank = u.shape
    step, low_part = 192, 64
    assert users.shape[1] % step == 0
    return pl.pallas_call(
        functools.partial(histogram_kernel, step, low_part, item_dev, n_grp, n_user),
        in_specs=[SMEM] + [pl.BlockSpec(memory_space=pltpu.HBM)] * 6,
        out_specs=[VMEM] * (n_grp + 3),
        out_shape=[struct((num_items // n_grp, block_users + 2 * rank), bf16)] * n_grp
        + [struct((num_items, block_users), bf16)] * 2
        + [struct(prev.shape, f32)],
        scratch_shapes=[
            pltpu.VMEM((num_items * (2 * block_users // low_part + 8), low_part), f32),
            pltpu.SMEM(valid.shape, i32),
            pltpu.SMEM(item.shape, i32),
            pltpu.VMEM(users.shape, i32),
            pltpu.VMEM(counts.shape, i32),
            pltpu.VMEM(u.shape, bf16),
            pltpu.SemaphoreType.DMA((6,)),
        ],
        compiler_params=params(32),
        cost_estimate=cost(7),
        name="histogram",
    )(me, *[pltpu.with_memory_space_constraint(v, pltpu.HBM) for v in (valid, item, users, counts, u, prev)])


def transpose_kernel(*refs):
    *us, ut = refs
    block_users = us[0].shape[0]
    for b, u in enumerate(us):
        for c in range(block_users // 128):
            at = b * block_users + c * 128
            ut[:, at : at + 128] = u[c * 128 : (c + 1) * 128, :].T


def transposed(us):
    block_users, rank = us[0].shape
    return pl.pallas_call(
        transpose_kernel,
        in_specs=[VMEM] * len(us),
        out_specs=VMEM,
        out_shape=struct((rank, block_users * len(us)), bf16),
        compiler_params=params(16),
        cost_estimate=cost(0.2),
        name="transpose",
    )(*us)


def chunk_rows(item_dev):
    return 64 * item_dev + -(-4 * item_dev // 16) * 16


def partial_systems(rows, ut, us, c, item_dev, at):
    rank = ut.shape[0]
    w = []
    for j in range(item_dev):
        one = c * item_dev + j
        e = jnp.concatenate([r[one : one + 1] for r in rows], 1)
        e = jnp.broadcast_to(e, (16, e.shape[1])).astype(bf16)
        w.append(jnp.concatenate([e] * (rank // 16), 0) * ut[:, at : at + e.shape[1]])
    return jnp.dot(jnp.concatenate(w, 0), jnp.concatenate([u[...] for u in us], 0), preferred_element_type=f32)


def some_rows(ref, first, n, cols):
    low, high = first // 16 * 16, -(-(first + n) // 16) * 16
    return ref[low:high, cols].astype(f32)[first - low : first - low + n]


def begun_kernel(first, n_items, item_dev, n, skip, at, *refs):
    es, us, ut, out = refs[:n], refs[n : 2 * n], refs[2 * n], refs[-1]
    more = refs[2 * n + 1 : -1]
    rows = [some_rows(e, first, n_items, slice(0, us[0].shape[0])) for e in es]
    for c in range(n_items // item_dev):
        total = partial_systems(rows, ut, us, c, item_dev, skip * us[0].shape[0])
        out[c] = total + more[0][at + c] if more else total


def begun(es, us, ut, first, n_items, item_dev, start=None, skip=0, at=0):
    more = [] if start is None else [start]
    n = len(es)
    block_users, rank = us[0].shape
    return pl.pallas_call(
        functools.partial(begun_kernel, first, n_items, item_dev, n, skip, at),
        in_specs=[VMEM] * (2 * n + 1 + len(more)),
        out_specs=VMEM,
        out_shape=struct((n_items // item_dev, item_dev * rank, rank), f32),
        compiler_params=params(32),
        cost_estimate=cost(0.082 * n * n_items),
        name="begun",
    )(*es, *us, ut, *more)


def systems_kernel(first, n_items, item_dev, keep, n, done, at, *refs):
    es, us, ut = refs[:n], refs[n : 2 * n - done], refs[2 * n - done]
    start = refs[2 * n - done + 1] if done else None
    out = refs[-1]
    block_users, rank = us[0].shape
    rows = [some_rows(e, first, n_items, slice(0, block_users)) for e in es[done:]]
    rhs = jnp.zeros((n_items, rank), f32)
    for e in es:
        rhs = rhs + some_rows(e, first, n_items, slice(block_users, block_users + rank))
        rhs = rhs + some_rows(e, first, n_items, slice(block_users + rank, block_users + 2 * rank))
    row = lax.broadcasted_iota(i32, (64, rank), 0)
    lane = lax.broadcasted_iota(i32, (64, rank), 1)
    eye = lax.broadcasted_iota(i32, (rank, rank), 0) == lax.broadcasted_iota(i32, (rank, rank), 1)
    above = (lane < 64) & (lane > row)
    base = 64 * item_dev

    for c in range(n_items // item_dev):
        total = partial_systems(rows, ut, us, c, item_dev, done * block_users)
        if done:
            total = total + start[at + c]
        diag = []
        for j in range(item_dev):
            g = total[j * rank : (j + 1) * rank]
            packed = jnp.where(above, pltpu.roll(g[64:], 64, 1), g[:64])
            out[c, 64 * j : 64 * j + 64, :] = packed.astype(out.dtype)
            diag.append(jnp.sum(jnp.where(eye, g, 0.0), axis=0, keepdims=True))
        diag = jnp.concatenate(diag, 0)
        side = rhs[c * item_dev : (c + 1) * item_dev]
        put_extras(
            lambda a, n, v, c=c: out.__setitem__((c, slice(base + a, base + a + n)), v), diag, side, keep, item_dev
        )


def put_extras(put, diag, side, keep, item_dev):
    if keep:
        nil = jnp.zeros_like(diag)
        rows = [diag, nil, side, nil]
    else:
        rows = []
        for v in (diag, side):
            high = v.astype(bf16).astype(f32)
            rows += [high, v - high]
    pad = -4 * item_dev % 16
    if pad:
        rows.append(jnp.zeros((pad, diag.shape[1]), f32))
    value = jnp.concatenate(rows, 0)
    put(0, value.shape[0], value if keep else value.astype(bf16))


def systems(es, us, ut, first, n_items, item_dev, keep, start=None, done=0, at=0, us_cost=None):
    n = len(es)
    block_users, rank = us[0].shape
    more = [] if start is None else [start]
    return pl.pallas_call(
        functools.partial(systems_kernel, first, n_items, item_dev, keep, n, done, at),
        in_specs=[VMEM] * (2 * n - done + 1 + len(more)),
        out_specs=VMEM,
        out_shape=struct((n_items // item_dev, chunk_rows(item_dev), rank), f32 if keep else bf16),
        compiler_params=params(40),
        cost_estimate=cost(0.082 * (n - done) * n_items if us_cost is None else us_cost),
        name="systems",
    )(*es, *us[done:], ut, *more)


def extras(value, item_dev):
    base = 64 * item_dev
    part = [value[base + n * item_dev : base + (n + 1) * item_dev] for n in range(4)]
    return part[0] + part[1], part[2] + part[3]


def merge_kernel(item_dev, n_keep, apart, skip, own, got, *outs):
    kept, sent = outs[0], outs[bool(n_keep) :]
    base = 64 * item_dev
    for c in range(own.shape[0]):
        value = own[c] + got[c + skip].astype(f32)
        diag, side = extras(value, item_dev)
        if c < n_keep:
            kept[c, :base, :] = value[:base]
            put_extras(lambda a, n, v, c=c: kept.__setitem__((c, slice(base + a, base + a + n)), v), diag, side, True, item_dev)
        else:
            ref = sent[c - n_keep] if apart else sent[0]
            lead = () if apart else (c - n_keep,)
            ref[lead + (slice(0, base),)] = value[:base].astype(bf16)
            put_extras(
                lambda a, n, v, ref=ref, lead=lead: ref.__setitem__(lead + (slice(base + a, base + a + n),), v),
                diag, side, False, item_dev,
            )


def merged(own, got, item_dev, n_keep, apart, skip=0):
    chunks, rows, rank = own.shape
    n_sent = chunks - n_keep
    shapes = [struct((rows, rank), bf16)] * n_sent if apart else [struct((n_sent, rows, rank), bf16)]
    shapes = ([struct((n_keep, rows, rank), f32)] if n_keep else []) + shapes
    return pl.pallas_call(
        functools.partial(merge_kernel, item_dev, n_keep, apart, skip),
        in_specs=[VMEM] * 2,
        out_specs=[VMEM] * len(shapes),
        out_shape=shapes,
        compiler_params=params(16),
        name="merge",
    )(own, got)


def gradients_kernel(item_dev, own, *refs):
    *got, prev, out, half = refs
    value = own[0]
    for g in got:
        value = value + (g[...] if len(g.shape) == 2 else g[0]).astype(f32)
    rank = value.shape[1]
    diag, side = extras(value, item_dev)
    row = lax.broadcasted_iota(i32, (64, 64), 0)
    col = lax.broadcasted_iota(i32, (64, 64), 1)
    eye = lax.broadcasted_iota(i32, (rank, rank), 0) == lax.broadcasted_iota(i32, (rank, rank), 1)
    matrices = []
    for j in range(item_dev):
        m = value[64 * j : 64 * j + 64]
        t = m.T
        mix, mix_t = m[:, :64], t[:64]
        a = jnp.where(col < row, mix, mix_t)
        c = jnp.where(col > row, mix, mix_t)
        full = jnp.concatenate(
            [jnp.concatenate([a, m[:, 64:]], 1), jnp.concatenate([t[64:], c], 1)], 0
        )
        matrices.append(jnp.where(eye, diag[j : j + 1] + ridge_weight, full))

    solution = prev[...]
    residual_c = [
        jnp.sum(jnp.where(eye, side[j : j + 1], 0.0) - matrices[j] * solution[j : j + 1], axis=1, keepdims=True)
        for j in range(item_dev)
    ]
    residual = jnp.concatenate(
        [jnp.sum(jnp.where(eye, c, 0.0), axis=0, keepdims=True) for c in residual_c], 0
    )
    direction, direction_c = residual, residual_c
    norm_now = jnp.sum(residual * residual, axis=1, keepdims=True)
    for turn in range(CG_STEPS):
        image = jnp.concatenate(
            [jnp.sum(m * c, axis=0, keepdims=True) for m, c in zip(matrices, direction_c)], 0
        )
        step = norm_now / jnp.sum(direction * image, axis=1, keepdims=True)
        solution = solution + step * direction
        if turn == CG_STEPS - 1:
            break
        residual = residual - step * image
        norm_next = jnp.sum(residual * residual, axis=1, keepdims=True)
        again = norm_next / norm_now
        image_c = [
            jnp.sum(matrices[j] * direction[j : j + 1], axis=1, keepdims=True) for j in range(item_dev)
        ]
        residual_c = [c - step[j : j + 1] * i for j, (c, i) in enumerate(zip(residual_c, image_c))]
        direction_c = [c + again[j : j + 1] * d for j, (c, d) in enumerate(zip(residual_c, direction_c))]
        direction = residual + again * direction
        norm_now = norm_next
    out[...] = solution
    short = solution.astype(bf16)
    for d in range(half.shape[0]):
        half[d] = short


def gradients(own, got, prev, devices):
    item_dev, rank = prev.shape
    return pl.pallas_call(
        functools.partial(gradients_kernel, item_dev),
        in_specs=[VMEM] * (2 + len(got)),
        out_specs=[VMEM] * 2,
        out_shape=[struct(prev.shape, f32), struct((devices,) + prev.shape, bf16)],
        compiler_params=params(16),
        cost_estimate=cost(2),
        name="gradients",
    )(own, *got, prev)


def user_side_kernel(item_dev, n_grp, n_user, me_s, returned, c_hi, c_lo, out, rows, order, made, sem):
    num_items = returned.shape[0]
    rows[...] = returned[...].astype(f32)
    me = me_s[0]
    for group in range(num_items // item_dev):
        owner = owner_of(group, item_dev, n_grp, n_user) ^ me
        order[group * item_dev : (group + 1) * item_dev, :] = rows[pl.ds(owner * item_dev, item_dev), :]
    ret = order[...].astype(bf16)
    copies = []
    for c in range(made.shape[0]):
        rows_c = slice(c * made.shape[1], (c + 1) * made.shape[1])
        made[c] = jnp.dot(c_hi[rows_c], ret, preferred_element_type=f32) + jnp.dot(
            c_lo[rows_c], ret, preferred_element_type=f32
        )
        copies.append(pltpu.make_async_copy(made.at[c], out.at[rows_c], sem.at[c]))
        copies[-1].start()
    for copy in copies:
        copy.wait()


def user_side(me, returned, c_hi, c_lo, item_dev, n_grp, n_user):
    num_items, rank = returned.shape
    pieces = 4
    return pl.pallas_call(
        functools.partial(user_side_kernel, item_dev, n_grp, n_user),
        in_specs=[SMEM, VMEM, VMEM, VMEM],
        out_specs=pl.BlockSpec(memory_space=pltpu.HBM),
        out_shape=struct((c_hi.shape[0], rank), f32),
        scratch_shapes=[pltpu.VMEM((num_items, rank), f32)] * 2
        + [pltpu.VMEM((pieces, c_hi.shape[0] // pieces, rank), f32), pltpu.SemaphoreType.DMA((pieces,))],
        compiler_params=params(16),
        cost_estimate=cost(1),
        name="user_side",
    )(me, returned, c_hi, c_lo)


def flip_kernel(*refs):
    n = len(refs) // 2
    for a, b in zip(refs[:n], refs[n:]):
        for c in range(a.shape[1] // 128):
            b[c * 128 : (c + 1) * 128, :] = a[:, c * 128 : (c + 1) * 128].T


def flipped(*values):
    return pl.pallas_call(
        flip_kernel,
        in_specs=[VMEM] * len(values),
        out_specs=[VMEM] * len(values),
        out_shape=[struct(v.shape[::-1], v.dtype) for v in values],
        compiler_params=params(16),
        cost_estimate=cost(8),
        name="flip",
    )(*values)


def shards(user_factors, tile_user, tile_count, tile_valid, tile_item, prev_items):
    n_user = lax.axis_size("user")
    n_grp = lax.axis_size("grp")
    devices = n_user * n_grp
    item_dev, rank = prev_items.shape
    num_items = item_dev * devices
    assert n_grp == 4 and n_user >= 4 and rank == 128 and user_factors.shape[0] == 1024
    me = lax.axis_index(AXES).astype(i32).reshape(1)

    def swap(value, bit):
        return lax.ppermute(value, AXES, [(d, d ^ bit) for d in range(devices)])

    u0 = user_factors
    u2 = swap(u0, 2)
    u1 = swap(u0, 1)
    *es, c_hi, c_lo, prev = histogram(
        me, tile_valid, tile_item, tile_user, tile_count, u0, prev_items, num_items, item_dev, n_grp, n_user
    )
    u2, es[0] = lax.optimization_barrier((u2, es[0]))
    u3 = swap(u2, 1)
    got = [es[0], swap(es[1], 1), swap(es[2], 2), swap(es[3], 3)]
    us = [u0, u1, u2, u3]
    ut = transposed(us)
    n_items = num_items // n_grp
    n_half = n_items // 2
    start = begun(got[:2], us[:2], transposed(us[:2]), n_half, n_half, item_dev)
    if n_user == 8:
        n_far = n_half // 2
        chunks = n_far // item_dev
        first = begun(got[2:3], us[2:3], ut, n_half + n_far, n_far, item_dev, start, 2, chunks)
        sent = systems(got, us, ut, n_half + n_far, n_far, item_dev, False, first, 3, 0)
        far_other = swap(sent, n_grp)
        ut, _ = lax.optimization_barrier((ut, sent))
        sent = systems(got, us, ut, n_half, n_far, item_dev, False, start, 2, 0)
        near_other = swap(sent, n_grp)
        ut, _ = lax.optimization_barrier((ut, sent))
        own = systems(got, us, ut, n_far, n_far, item_dev, True, us_cost=0.01)
        far = merged(own, far_other, item_dev, 0, True)
        parts = [swap(value, n_grp * 2 * (chunks + n)) for n, value in reversed(list(enumerate(far)))]
        ut, _ = lax.optimization_barrier((ut, far[0]))
        own = systems(got, us, ut, item_dev, n_far - item_dev, item_dev, True)
        near = merged(own, near_other, item_dev, 0, True, 1)
        parts += [swap(value, n_grp * 2 * (n + 1)) for n, value in enumerate(near)]
        ut, _ = lax.optimization_barrier((ut, own))
        own = systems(got, us, ut, 0, item_dev, item_dev, True)
        parts.append(near_other)
    else:
        left, bit = n_user, n_grp
        sent = systems(got, us, ut, n_half, n_half, item_dev, False, start, 2)
        other = swap(sent, bit)
        own = systems(got, us, ut, 0, n_half, item_dev, True)
        left, bit = left // 2, bit * 2
        while left > 4:
            own, sent = merged(own, other, item_dev, left // 2, False)
            other = swap(sent, bit)
            left, bit = left // 2, bit * 2
        own, *sent = merged(own, other, item_dev, 1, True)
        parts = [swap(value, bit * (n + 1)) for n, value in enumerate(sent)]
    c_hi, c_lo, own, *parts[:2] = lax.optimization_barrier((c_hi, c_lo, own, *parts[:2]))
    c_hi, c_lo = flipped(c_hi, c_lo)
    own, c_hi = lax.optimization_barrier((own, c_hi))
    solved, spread = gradients(own, parts, prev, devices)
    returned = lax.all_to_all(spread, AXES, 0, 0, tiled=True).reshape(num_items, rank)
    return solved, user_side(me, returned, c_hi, c_lo, item_dev, n_grp, n_user)


def solution(mesh):
    return jax.shard_map(
        shards,
        mesh=mesh,
        in_specs=(
            P(AXES, None),
            P(AXES, None, None),
            P(AXES, None, None),
            P(AXES, None),
            P(AXES, None),
            P(AXES, None),
        ),
        out_specs=(P(AXES, None), P(AXES, None)),
        check_vma=False,
    )
```

```python
import functools

import jax
import jax.numpy as jnp
from jax import lax
from jax.experimental import pallas as pl
from jax.experimental.pallas import tpu as pltpu
from jax.sharding import PartitionSpec as P

CG_STEPS = 4
bf16, f32, i32 = jnp.bfloat16, jnp.float32, jnp.int32
AXES = ("user", "grp")
VMEM = pl.BlockSpec(memory_space=pltpu.VMEM)
SMEM = pl.BlockSpec(memory_space=pltpu.SMEM)
struct = jax.ShapeDtypeStruct

confidence_rate = 0.5
ridge_weight = 1.0


def log2(n):
    k = n.bit_length() - 1
    assert 1 << k == n
    return k


def cost(us):
    return pl.CostEstimate(flops=int(us * 1e9), bytes_accessed=int(us * 3e6), transcendentals=0)


def params(mib):
    return pltpu.CompilerParams(vmem_limit_bytes=mib << 20)


def slot_of(item, me, item_dev, n_grp, n_user):
    rel = (item >> log2(item_dev)) ^ me
    slot = item & (item_dev - 1)
    w = rel >> log2(n_grp)
    per, left = n_user * item_dev, n_user
    k = (rel & (n_grp - 1)) * per
    while left > 4:
        per, left = per // 2, left // 2
        k = k + (w & 1) * per
        w = w >> 1
    return k + w * item_dev + slot


def owner_of(group, item_dev, n_grp, n_user):
    k, w = divmod(group, n_user)
    bits, left, at = 0, n_user, 0
    while left > 4:
        left //= 2
        bits |= (w // left) << at
        w %= left
        at += 1
    return (bits | (w << at)) * n_grp + k


def histogram_kernel(step, low_part, item_dev, n_grp, n_user, me_s, *refs):
    sources, rest = refs[:6], refs[6:]
    eouts = rest[:n_grp]
    c_hi, c_lo, prev_here, acc, *here, sem = rest[n_grp:]
    here.append(prev_here)
    copies = [pltpu.make_async_copy(a, b, sem.at[n]) for n, (a, b) in enumerate(zip(sources, here))]
    for copy in copies:
        copy.start()
    valid_s, item_s, users, counts, u, _ = here
    tiles, rows = users.shape[1:]
    num_items = c_hi.shape[0]
    block_users = u.shape[0]
    his = block_users // low_part
    kinds = 2 * his
    pitch = kinds + 8
    me = me_s[0]
    for copy in copies[:4]:
        copy.wait()
    lane = lax.broadcasted_iota(i32, (his, rows), 1)
    sub = lax.broadcasted_iota(i32, (his, rows), 0)
    iota = lax.broadcasted_iota(i32, (low_part, rows), 0).astype(f32).astype(bf16)
    zero = jnp.zeros((kinds, rows), bf16)
    one, nil = jnp.ones((low_part, rows), bf16), jnp.zeros((low_part, rows), bf16)

    def body(b, run):
        base = pl.multiple_of(b * step, step)
        blk = users[0, pl.ds(base, step), :]
        cnt = counts[0, pl.ds(base, step), :].astype(f32) * confidence_rate
        lo = (blk & (low_part - 1)).astype(f32)
        hi = blk >> log2(low_part)
        for t in range(0, step, 2):
            oh, lhs = [], []
            for j in (t, t + 1):
                lob = jnp.broadcast_to(lo[j : j + 1], (16, rows)).astype(bf16)
                oh.append(jnp.where(jnp.concatenate([lob] * (low_part // 16), 0) == iota, one, nil))
                on = (lane < valid_s[0, base + j]) & (jnp.broadcast_to(hi[j : j + 1], (his, rows)) == sub)
                ex = jnp.broadcast_to(cnt[j : j + 1], (his, rows))
                lhs.append(
                    jnp.concatenate([jnp.where(on, ex, 0.0), jnp.where(on, 1.0 + ex, 0.0)], 0).astype(bf16)
                )
            left = jnp.concatenate(
                [jnp.concatenate([lhs[0], zero], 1), jnp.concatenate([zero, lhs[1]], 1)], 0
            )
            out = lax.dot_general(
                left, jnp.concatenate(oh, 1), (((1,), (1,)), ((), ())), preferred_element_type=f32
            )
            for q, j in enumerate((t, t + 1)):
                item, before = item_s[0, base + j], item_s[0, jnp.maximum(base + j - 1, 0)]
                run = jnp.where(item == before, 1.0, 0.0) * run + out[kinds * q : kinds * (q + 1)]
                p = slot_of(item, me, item_dev, n_grp, n_user)
                acc[pl.ds(pl.multiple_of(p * pitch, 8), kinds), :] = run
        return run

    lax.fori_loop(0, tiles // step, body, jnp.zeros((kinds, low_part), f32))
    copies[4].wait()
    copies[5].wait()
    per = num_items // n_grp
    wide = 128 // low_part

    def row(h):
        parts = [acc[pl.ds(h * wide + n, num_items, stride=pitch), :] for n in range(wide)]
        return jnp.concatenate(parts, 1)

    for h in range(block_users // 128):
        e = (row(h) + 1.0).astype(bf16)
        for k in range(n_grp):
            eouts[k][:, h * 128 : (h + 1) * 128] = e[k * per : (k + 1) * per]
        c = row(his // wide + h)
        ch = c.astype(bf16)
        c_hi[:, h * 128 : (h + 1) * 128] = ch
        c_lo[:, h * 128 : (h + 1) * 128] = (c - ch.astype(f32)).astype(bf16)
    uu = u[...]
    r = jnp.dot(c_hi[...], uu, preferred_element_type=f32) + jnp.dot(c_lo[...], uu, preferred_element_type=f32)
    rh = r.astype(bf16)
    rl = (r - rh.astype(f32)).astype(bf16)
    for k in range(n_grp):
        eouts[k][:, block_users : block_users + 128] = rh[k * per : (k + 1) * per]
        eouts[k][:, block_users + 128 :] = rl[k * per : (k + 1) * per]


def histogram(me, valid, item, users, counts, u, prev, num_items, item_dev, n_grp, n_user):
    block_users, rank = u.shape
    step, low_part = 192, 64
    assert users.shape[1] % step == 0
    return pl.pallas_call(
        functools.partial(histogram_kernel, step, low_part, item_dev, n_grp, n_user),
        in_specs=[SMEM] + [pl.BlockSpec(memory_space=pltpu.HBM)] * 6,
        out_specs=[VMEM] * (n_grp + 3),
        out_shape=[struct((num_items // n_grp, block_users + 2 * rank), bf16)] * n_grp
        + [struct((num_items, block_users), bf16)] * 2
        + [struct(prev.shape, f32)],
        scratch_shapes=[
            pltpu.VMEM((num_items * (2 * block_users // low_part + 8), low_part), f32),
            pltpu.SMEM(valid.shape, i32),
            pltpu.SMEM(item.shape, i32),
            pltpu.VMEM(users.shape, i32),
            pltpu.VMEM(counts.shape, i32),
            pltpu.VMEM(u.shape, bf16),
            pltpu.SemaphoreType.DMA((6,)),
        ],
        compiler_params=params(32),
        cost_estimate=cost(7),
        name="histogram",
    )(me, *[pltpu.with_memory_space_constraint(v, pltpu.HBM) for v in (valid, item, users, counts, u, prev)])


def transpose_kernel(*refs):
    *us, ut = refs
    block_users = us[0].shape[0]
    for b, u in enumerate(us):
        for c in range(block_users // 128):
            at = b * block_users + c * 128
            ut[:, at : at + 128] = u[c * 128 : (c + 1) * 128, :].T


def transposed(us):
    block_users, rank = us[0].shape
    return pl.pallas_call(
        transpose_kernel,
        in_specs=[VMEM] * len(us),
        out_specs=VMEM,
        out_shape=struct((rank, block_users * len(us)), bf16),
        compiler_params=params(16),
        cost_estimate=cost(0.2),
        name="transpose",
    )(*us)


def chunk_rows(item_dev):
    return 64 * item_dev + -(-4 * item_dev // 16) * 16


def partial_systems(rows, ut, us, c, item_dev, at):
    rank = ut.shape[0]
    w = []
    for j in range(item_dev):
        one = c * item_dev + j
        e = jnp.concatenate([r[one : one + 1] for r in rows], 1)
        e = jnp.broadcast_to(e, (16, e.shape[1])).astype(bf16)
        w.append(jnp.concatenate([e] * (rank // 16), 0) * ut[:, at : at + e.shape[1]])
    return jnp.dot(jnp.concatenate(w, 0), jnp.concatenate([u[...] for u in us], 0), preferred_element_type=f32)


def some_rows(ref, first, n, cols):
    low, high = first // 16 * 16, -(-(first + n) // 16) * 16
    return ref[low:high, cols].astype(f32)[first - low : first - low + n]


def begun_kernel(first, n_items, item_dev, n, skip, at, *refs):
    es, us, ut, out = refs[:n], refs[n : 2 * n], refs[2 * n], refs[-1]
    more = refs[2 * n + 1 : -1]
    rows = [some_rows(e, first, n_items, slice(0, us[0].shape[0])) for e in es]
    for c in range(n_items // item_dev):
        total = partial_systems(rows, ut, us, c, item_dev, skip * us[0].shape[0])
        out[c] = total + more[0][at + c] if more else total


def begun(es, us, ut, first, n_items, item_dev, start=None, skip=0, at=0):
    more = [] if start is None else [start]
    n = len(es)
    block_users, rank = us[0].shape
    return pl.pallas_call(
        functools.partial(begun_kernel, first, n_items, item_dev, n, skip, at),
        in_specs=[VMEM] * (2 * n + 1 + len(more)),
        out_specs=VMEM,
        out_shape=struct((n_items // item_dev, item_dev * rank, rank), f32),
        compiler_params=params(32),
        cost_estimate=cost(0.082 * n * n_items),
        name="begun",
    )(*es, *us, ut, *more)


def systems_kernel(first, n_items, item_dev, keep, n, done, at, *refs):
    es, us, ut = refs[:n], refs[n : 2 * n - done], refs[2 * n - done]
    start = refs[2 * n - done + 1] if done else None
    out = refs[-1]
    block_users, rank = us[0].shape
    rows = [some_rows(e, first, n_items, slice(0, block_users)) for e in es[done:]]
    rhs = jnp.zeros((n_items, rank), f32)
    for e in es:
        rhs = rhs + some_rows(e, first, n_items, slice(block_users, block_users + rank))
        rhs = rhs + some_rows(e, first, n_items, slice(block_users + rank, block_users + 2 * rank))
    row = lax.broadcasted_iota(i32, (64, rank), 0)
    lane = lax.broadcasted_iota(i32, (64, rank), 1)
    eye = lax.broadcasted_iota(i32, (rank, rank), 0) == lax.broadcasted_iota(i32, (rank, rank), 1)
    above = (lane < 64) & (lane > row)
    base = 64 * item_dev

    for c in range(n_items // item_dev):
        total = partial_systems(rows, ut, us, c, item_dev, done * block_users)
        if done:
            total = total + start[at + c]
        diag = []
        for j in range(item_dev):
            g = total[j * rank : (j + 1) * rank]
            packed = jnp.where(above, pltpu.roll(g[64:], 64, 1), g[:64])
            out[c, 64 * j : 64 * j + 64, :] = packed.astype(out.dtype)
            diag.append(jnp.sum(jnp.where(eye, g, 0.0), axis=0, keepdims=True))
        diag = jnp.concatenate(diag, 0)
        side = rhs[c * item_dev : (c + 1) * item_dev]
        put_extras(
            lambda a, n, v, c=c: out.__setitem__((c, slice(base + a, base + a + n)), v), diag, side, keep, item_dev
        )


def put_extras(put, diag, side, keep, item_dev):
    if keep:
        nil = jnp.zeros_like(diag)
        rows = [diag, nil, side, nil]
    else:
        rows = []
        for v in (diag, side):
            high = v.astype(bf16).astype(f32)
            rows += [high, v - high]
    pad = -4 * item_dev % 16
    if pad:
        rows.append(jnp.zeros((pad, diag.shape[1]), f32))
    value = jnp.concatenate(rows, 0)
    put(0, value.shape[0], value if keep else value.astype(bf16))


def systems(es, us, ut, first, n_items, item_dev, keep, start=None, done=0, at=0, us_cost=None):
    n = len(es)
    block_users, rank = us[0].shape
    more = [] if start is None else [start]
    return pl.pallas_call(
        functools.partial(systems_kernel, first, n_items, item_dev, keep, n, done, at),
        in_specs=[VMEM] * (2 * n - done + 1 + len(more)),
        out_specs=VMEM,
        out_shape=struct((n_items // item_dev, chunk_rows(item_dev), rank), f32 if keep else bf16),
        compiler_params=params(40),
        cost_estimate=cost(0.082 * (n - done) * n_items if us_cost is None else us_cost),
        name="systems",
    )(*es, *us[done:], ut, *more)


def extras(value, item_dev):
    base = 64 * item_dev
    part = [value[base + n * item_dev : base + (n + 1) * item_dev] for n in range(4)]
    return part[0] + part[1], part[2] + part[3]


def merge_kernel(item_dev, n_keep, apart, skip, own, got, *outs):
    kept, sent = outs[0], outs[bool(n_keep) :]
    base = 64 * item_dev
    for c in range(own.shape[0]):
        value = own[c] + got[c + skip].astype(f32)
        diag, side = extras(value, item_dev)
        if c < n_keep:
            kept[c, :base, :] = value[:base]
            put_extras(lambda a, n, v, c=c: kept.__setitem__((c, slice(base + a, base + a + n)), v), diag, side, True, item_dev)
        else:
            ref = sent[c - n_keep] if apart else sent[0]
            lead = () if apart else (c - n_keep,)
            ref[lead + (slice(0, base),)] = value[:base].astype(bf16)
            put_extras(
                lambda a, n, v, ref=ref, lead=lead: ref.__setitem__(lead + (slice(base + a, base + a + n),), v),
                diag, side, False, item_dev,
            )


def merged(own, got, item_dev, n_keep, apart, skip=0):
    chunks, rows, rank = own.shape
    n_sent = chunks - n_keep
    shapes = [struct((rows, rank), bf16)] * n_sent if apart else [struct((n_sent, rows, rank), bf16)]
    shapes = ([struct((n_keep, rows, rank), f32)] if n_keep else []) + shapes
    return pl.pallas_call(
        functools.partial(merge_kernel, item_dev, n_keep, apart, skip),
        in_specs=[VMEM] * 2,
        out_specs=[VMEM] * len(shapes),
        out_shape=shapes,
        compiler_params=params(16),
        name="merge",
    )(own, got)


def gradients_kernel(item_dev, own, *refs):
    *got, prev, out, half = refs
    value = own[0]
    for g in got:
        value = value + (g[...] if len(g.shape) == 2 else g[0]).astype(f32)
    rank = value.shape[1]
    diag, side = extras(value, item_dev)
    row = lax.broadcasted_iota(i32, (64, 64), 0)
    col = lax.broadcasted_iota(i32, (64, 64), 1)
    eye = lax.broadcasted_iota(i32, (rank, rank), 0) == lax.broadcasted_iota(i32, (rank, rank), 1)
    matrices = []
    for j in range(item_dev):
        m = value[64 * j : 64 * j + 64]
        t = m.T
        mix, mix_t = m[:, :64], t[:64]
        a = jnp.where(col < row, mix, mix_t)
        c = jnp.where(col > row, mix, mix_t)
        full = jnp.concatenate(
            [jnp.concatenate([a, m[:, 64:]], 1), jnp.concatenate([t[64:], c], 1)], 0
        )
        matrices.append(jnp.where(eye, diag[j : j + 1] + ridge_weight, full))

    solution = prev[...]
    residual_c = [
        jnp.sum(jnp.where(eye, side[j : j + 1], 0.0) - matrices[j] * solution[j : j + 1], axis=1, keepdims=True)
        for j in range(item_dev)
    ]
    residual = jnp.concatenate(
        [jnp.sum(jnp.where(eye, c, 0.0), axis=0, keepdims=True) for c in residual_c], 0
    )
    direction, direction_c = residual, residual_c
    norm_now = jnp.sum(residual * residual, axis=1, keepdims=True)
    for turn in range(CG_STEPS):
        image = jnp.concatenate(
            [jnp.sum(m * c, axis=0, keepdims=True) for m, c in zip(matrices, direction_c)], 0
        )
        step = norm_now / jnp.sum(direction * image, axis=1, keepdims=True)
        solution = solution + step * direction
        if turn == CG_STEPS - 1:
            break
        residual = residual - step * image
        norm_next = jnp.sum(residual * residual, axis=1, keepdims=True)
        again = norm_next / norm_now
        image_c = [
            jnp.sum(matrices[j] * direction[j : j + 1], axis=1, keepdims=True) for j in range(item_dev)
        ]
        residual_c = [c - step[j : j + 1] * i for j, (c, i) in enumerate(zip(residual_c, image_c))]
        direction_c = [c + again[j : j + 1] * d for j, (c, d) in enumerate(zip(residual_c, direction_c))]
        direction = residual + again * direction
        norm_now = norm_next
    out[...] = solution
    short = solution.astype(bf16)
    for d in range(half.shape[0]):
        half[d] = short


def gradients(own, got, prev, devices):
    item_dev, rank = prev.shape
    return pl.pallas_call(
        functools.partial(gradients_kernel, item_dev),
        in_specs=[VMEM] * (2 + len(got)),
        out_specs=[VMEM] * 2,
        out_shape=[struct(prev.shape, f32), struct((devices,) + prev.shape, bf16)],
        compiler_params=params(16),
        cost_estimate=cost(2),
        name="gradients",
    )(own, *got, prev)


def summed_kernel(own, *refs):
    *got, out = refs
    value = own[0]
    for g in got:
        value = value + (g[...] if len(g.shape) == 2 else g[0]).astype(f32)
    out[0] = value


def summed(own, got):
    return pl.pallas_call(
        summed_kernel,
        in_specs=[VMEM] * (1 + len(got)),
        out_specs=VMEM,
        out_shape=struct(own.shape, f32),
        compiler_params=params(16),
        cost_estimate=cost(8),
        name="summed",
    )(own, *got)


def user_side_kernel(item_dev, n_grp, n_user, me_s, returned, c_both, out, rows, order, made, sem):
    num_items = returned.shape[0]
    rows[...] = returned[...].astype(f32)
    me = me_s[0]
    for group in range(num_items // item_dev):
        owner = owner_of(group, item_dev, n_grp, n_user) ^ me
        order[group * item_dev : (group + 1) * item_dev, :] = rows[pl.ds(owner * item_dev, item_dev), :]
    ret = order[...].astype(bf16)
    ret = jnp.concatenate([ret, ret], 0)
    copies = []
    for c in range(made.shape[0]):
        rows_c = slice(c * made.shape[1], (c + 1) * made.shape[1])
        made[c] = jnp.dot(c_both[rows_c], ret, preferred_element_type=f32)
        copies.append(pltpu.make_async_copy(made.at[c], out.at[rows_c], sem.at[c]))
        copies[-1].start()
    for copy in copies:
        copy.wait()


def user_side(me, returned, c_both, item_dev, n_grp, n_user):
    num_items, rank = returned.shape
    pieces = 4
    return pl.pallas_call(
        functools.partial(user_side_kernel, item_dev, n_grp, n_user),
        in_specs=[SMEM, VMEM, VMEM],
        out_specs=pl.BlockSpec(memory_space=pltpu.HBM),
        out_shape=struct((c_both.shape[0], rank), f32),
        scratch_shapes=[pltpu.VMEM((num_items, rank), f32)] * 2
        + [pltpu.VMEM((pieces, c_both.shape[0] // pieces, rank), f32), pltpu.SemaphoreType.DMA((pieces,))],
        compiler_params=params(16),
        cost_estimate=cost(1),
        name="user_side",
    )(me, returned, c_both)


def flip_kernel(a, b, out):
    items = a.shape[0]
    for n, v in enumerate((a, b)):
        for c in range(a.shape[1] // 128):
            out[c * 128 : (c + 1) * 128, n * items : (n + 1) * items] = v[:, c * 128 : (c + 1) * 128].T


def flipped(c_hi, c_lo):
    return pl.pallas_call(
        flip_kernel,
        in_specs=[VMEM] * 2,
        out_specs=VMEM,
        out_shape=struct((c_hi.shape[1], 2 * c_hi.shape[0]), bf16),
        compiler_params=params(16),
        cost_estimate=cost(0.01),
        name="flip",
    )(c_hi, c_lo)


def shards(user_factors, tile_user, tile_count, tile_valid, tile_item, prev_items):
    n_user = lax.axis_size("user")
    n_grp = lax.axis_size("grp")
    devices = n_user * n_grp
    item_dev, rank = prev_items.shape
    num_items = item_dev * devices
    assert n_grp == 4 and n_user >= 4 and rank == 128 and user_factors.shape[0] == 1024
    me = lax.axis_index(AXES).astype(i32).reshape(1)

    def swap(value, bit):
        return lax.ppermute(value, AXES, [(d, d ^ bit) for d in range(devices)])

    u0 = user_factors
    u2 = swap(u0, 2)
    u1 = swap(u0, 1)
    *es, c_hi, c_lo, prev = histogram(
        me, tile_valid, tile_item, tile_user, tile_count, u0, prev_items, num_items, item_dev, n_grp, n_user
    )
    c_both = flipped(c_hi, c_lo)
    u2, c_both = lax.optimization_barrier((u2, c_both))
    u3 = swap(u2, 1)
    got = [es[0], swap(es[1], 1), swap(es[2], 2), swap(es[3], 3)]
    us = [u0, u1, u2, u3]
    ut = transposed(us)
    n_items = num_items // n_grp
    n_half = n_items // 2
    start = begun(got[:2], us[:2], transposed(us[:2]), n_half, n_half, item_dev)
    if n_user == 8:
        n_far = n_half // 2
        chunks = n_far // item_dev
        first = begun(got[2:3], us[2:3], ut, n_half + n_far, n_far, item_dev, start, 2, chunks)
        sent = systems(got, us, ut, n_half + n_far, n_far, item_dev, False, first, 3, 0)
        far_other = swap(sent, n_grp)
        ut, _ = lax.optimization_barrier((ut, sent))
        sent = systems(got, us, ut, n_half, n_far, item_dev, False, start, 2, 0)
        near_other = swap(sent, n_grp)
        ut, _ = lax.optimization_barrier((ut, sent))
        own = systems(got, us, ut, n_far, n_far, item_dev, True, us_cost=0.01)
        far = merged(own, far_other, item_dev, 0, True)
        parts = [swap(value, n_grp * 2 * (chunks + n)) for n, value in reversed(list(enumerate(far)))]
        ut, _ = lax.optimization_barrier((ut, far[0]))
        own = systems(got, us, ut, item_dev, n_far - item_dev, item_dev, True)
        near = merged(own, near_other, item_dev, 0, True, 1)
        parts += [swap(value, n_grp * 2 * (n + 1)) for n, value in enumerate(near)]
        ut, _ = lax.optimization_barrier((ut, own))
        own = systems(got, us, ut, 0, item_dev, item_dev, True)
        own = summed(own, [near_other] + parts[:-1])
        parts = parts[-1:]
    else:
        left, bit = n_user, n_grp
        sent = systems(got, us, ut, n_half, n_half, item_dev, False, start, 2)
        other = swap(sent, bit)
        own = systems(got, us, ut, 0, n_half, item_dev, True)
        left, bit = left // 2, bit * 2
        while left > 4:
            own, sent = merged(own, other, item_dev, left // 2, False)
            other = swap(sent, bit)
            left, bit = left // 2, bit * 2
        own, *sent = merged(own, other, item_dev, 1, True)
        parts = [swap(value, bit * (n + 1)) for n, value in enumerate(sent)]
    solved, spread = gradients(own, parts, prev, devices)
    returned = lax.all_to_all(spread, AXES, 0, 0, tiled=True).reshape(num_items, rank)
    return solved, user_side(me, returned, c_both, item_dev, n_grp, n_user)


def solution(mesh):
    return jax.shard_map(
        shards,
        mesh=mesh,
        in_specs=(
            P(AXES, None),
            P(AXES, None, None),
            P(AXES, None, None),
            P(AXES, None),
            P(AXES, None),
            P(AXES, None),
        ),
        out_specs=(P(AXES, None), P(AXES, None)),
        check_vma=False,
    )
```

```python
import functools

import jax
import jax.numpy as jnp
from jax import lax
from jax.experimental import pallas as pl
from jax.experimental.pallas import tpu as pltpu
from jax.sharding import PartitionSpec as P

CG_STEPS = 4
bf16, f32, i32 = jnp.bfloat16, jnp.float32, jnp.int32
AXES = ("user", "grp")
VMEM = pl.BlockSpec(memory_space=pltpu.VMEM)
SMEM = pl.BlockSpec(memory_space=pltpu.SMEM)
struct = jax.ShapeDtypeStruct

confidence_rate = 0.5
ridge_weight = 1.0


def log2(n):
    k = n.bit_length() - 1
    assert 1 << k == n
    return k


def cost(us):
    return pl.CostEstimate(flops=int(us * 1e9), bytes_accessed=int(us * 3e6), transcendentals=0)


def params(mib):
    return pltpu.CompilerParams(vmem_limit_bytes=mib << 20)


def slot_of(item, me, item_dev, n_grp, n_user):
    rel = (item >> log2(item_dev)) ^ me
    slot = item & (item_dev - 1)
    w = rel >> log2(n_grp)
    per, left = n_user * item_dev, n_user
    k = (rel & (n_grp - 1)) * per
    while left > 4:
        per, left = per // 2, left // 2
        k = k + (w & 1) * per
        w = w >> 1
    return k + w * item_dev + slot


def owner_of(group, item_dev, n_grp, n_user):
    k, w = divmod(group, n_user)
    bits, left, at = 0, n_user, 0
    while left > 4:
        left //= 2
        bits |= (w // left) << at
        w %= left
        at += 1
    return (bits | (w << at)) * n_grp + k


def histogram_kernel(step, low_part, item_dev, n_grp, n_user, me_s, *refs):
    sources, rest = refs[:6], refs[6:]
    eouts = rest[:n_grp]
    c_hi, c_lo, prev_here, ut, acc, *here, sem = rest[n_grp:]
    here.append(prev_here)
    copies = [pltpu.make_async_copy(a, b, sem.at[n]) for n, (a, b) in enumerate(zip(sources, here))]
    for copy in copies:
        copy.start()
    valid_s, item_s, users, counts, u, _ = here
    tiles, rows = users.shape[1:]
    num_items = c_hi.shape[0]
    block_users = u.shape[0]
    his = block_users // low_part
    kinds = 2 * his
    pitch = kinds + 8
    me = me_s[0]
    for copy in copies[:4]:
        copy.wait()
    lane = lax.broadcasted_iota(i32, (his, rows), 1)
    sub = lax.broadcasted_iota(i32, (his, rows), 0)
    iota = lax.broadcasted_iota(i32, (low_part, rows), 0).astype(f32).astype(bf16)
    zero = jnp.zeros((kinds, rows), bf16)
    one, nil = jnp.ones((low_part, rows), bf16), jnp.zeros((low_part, rows), bf16)

    def body(b, run):
        base = pl.multiple_of(b * step, step)
        blk = users[0, pl.ds(base, step), :]
        cnt = counts[0, pl.ds(base, step), :].astype(f32) * confidence_rate
        lo = (blk & (low_part - 1)).astype(f32)
        hi = blk >> log2(low_part)
        for t in range(0, step, 2):
            oh, lhs = [], []
            for j in (t, t + 1):
                lob = jnp.broadcast_to(lo[j : j + 1], (16, rows)).astype(bf16)
                oh.append(jnp.where(jnp.concatenate([lob] * (low_part // 16), 0) == iota, one, nil))
                on = (lane < valid_s[0, base + j]) & (jnp.broadcast_to(hi[j : j + 1], (his, rows)) == sub)
                ex = jnp.broadcast_to(cnt[j : j + 1], (his, rows))
                lhs.append(
                    jnp.concatenate([jnp.where(on, ex, 0.0), jnp.where(on, 1.0 + ex, 0.0)], 0).astype(bf16)
                )
            left = jnp.concatenate(
                [jnp.concatenate([lhs[0], zero], 1), jnp.concatenate([zero, lhs[1]], 1)], 0
            )
            out = lax.dot_general(
                left, jnp.concatenate(oh, 1), (((1,), (1,)), ((), ())), preferred_element_type=f32
            )
            for q, j in enumerate((t, t + 1)):
                item, before = item_s[0, base + j], item_s[0, jnp.maximum(base + j - 1, 0)]
                run = jnp.where(item == before, 1.0, 0.0) * run + out[kinds * q : kinds * (q + 1)]
                p = slot_of(item, me, item_dev, n_grp, n_user)
                acc[pl.ds(pl.multiple_of(p * pitch, 8), kinds), :] = run
        return run

    lax.fori_loop(0, tiles // step, body, jnp.zeros((kinds, low_part), f32))
    copies[4].wait()
    copies[5].wait()
    transpose_kernel(u, ut)
    per = num_items // n_grp
    wide = 128 // low_part

    def row(h):
        parts = [acc[pl.ds(h * wide + n, num_items, stride=pitch), :] for n in range(wide)]
        return jnp.concatenate(parts, 1)

    for h in range(block_users // 128):
        e = (row(h) + 1.0).astype(bf16)
        for k in range(n_grp):
            eouts[k][:, h * 128 : (h + 1) * 128] = e[k * per : (k + 1) * per]
        c = row(his // wide + h)
        ch = c.astype(bf16)
        c_hi[:, h * 128 : (h + 1) * 128] = ch
        c_lo[:, h * 128 : (h + 1) * 128] = (c - ch.astype(f32)).astype(bf16)
    uu = u[...]
    r = jnp.dot(c_hi[...], uu, preferred_element_type=f32) + jnp.dot(c_lo[...], uu, preferred_element_type=f32)
    rh = r.astype(bf16)
    rl = (r - rh.astype(f32)).astype(bf16)
    for k in range(n_grp):
        eouts[k][:, block_users : block_users + 128] = rh[k * per : (k + 1) * per]
        eouts[k][:, block_users + 128 :] = rl[k * per : (k + 1) * per]


def histogram(me, valid, item, users, counts, u, prev, num_items, item_dev, n_grp, n_user):
    block_users, rank = u.shape
    step, low_part = 192, 64
    assert users.shape[1] % step == 0
    return pl.pallas_call(
        functools.partial(histogram_kernel, step, low_part, item_dev, n_grp, n_user),
        in_specs=[SMEM] + [pl.BlockSpec(memory_space=pltpu.HBM)] * 6,
        out_specs=[VMEM] * (n_grp + 4),
        out_shape=[struct((num_items // n_grp, block_users + 2 * rank), bf16)] * n_grp
        + [struct((num_items, block_users), bf16)] * 2
        + [struct(prev.shape, f32), struct((rank, block_users), bf16)],
        scratch_shapes=[
            pltpu.VMEM((num_items * (2 * block_users // low_part + 8), low_part), f32),
            pltpu.SMEM(valid.shape, i32),
            pltpu.SMEM(item.shape, i32),
            pltpu.VMEM(users.shape, i32),
            pltpu.VMEM(counts.shape, i32),
            pltpu.VMEM(u.shape, bf16),
            pltpu.SemaphoreType.DMA((6,)),
        ],
        compiler_params=params(32),
        cost_estimate=cost(7),
        name="histogram",
    )(me, *[pltpu.with_memory_space_constraint(v, pltpu.HBM) for v in (valid, item, users, counts, u, prev)])


def transpose_kernel(u, ut):
    for c in range(u.shape[0] // 128):
        ut[:, c * 128 : (c + 1) * 128] = u[c * 128 : (c + 1) * 128, :].T


def transposed(u):
    return pl.pallas_call(
        transpose_kernel,
        in_specs=[VMEM],
        out_specs=VMEM,
        out_shape=struct(u.shape[::-1], bf16),
        compiler_params=params(16),
        cost_estimate=cost(0.1),
        name="transpose",
    )(u)


def chunk_rows(item_dev):
    return 64 * item_dev + -(-4 * item_dev // 16) * 16


def partial_systems(rows, uts, us, c, item_dev):
    rank = uts[0].shape[0]
    ut = jnp.concatenate([t[...] for t in uts], 1)
    w = []
    for j in range(item_dev):
        one = c * item_dev + j
        e = jnp.concatenate([r[one : one + 1] for r in rows], 1)
        e = jnp.broadcast_to(e, (16, e.shape[1])).astype(bf16)
        w.append(jnp.concatenate([e] * (rank // 16), 0) * ut)
    return jnp.dot(jnp.concatenate(w, 0), jnp.concatenate([u[...] for u in us], 0), preferred_element_type=f32)


def some_rows(ref, first, n, cols):
    low, high = first // 16 * 16, -(-(first + n) // 16) * 16
    return ref[low:high, cols].astype(f32)[first - low : first - low + n]


def begun_kernel(first, n_items, item_dev, n, at, *refs):
    es, us, uts, out = refs[:n], refs[n : 2 * n], refs[2 * n : 3 * n], refs[-1]
    more = refs[3 * n : -1]
    rows = [some_rows(e, first, n_items, slice(0, us[0].shape[0])) for e in es]
    for c in range(n_items // item_dev):
        total = partial_systems(rows, uts, us, c, item_dev)
        out[c] = total + more[0][at + c] if more else total


def begun(es, us, uts, first, n_items, item_dev, start=None, at=0):
    more = [] if start is None else [start]
    n = len(es)
    block_users, rank = us[0].shape
    return pl.pallas_call(
        functools.partial(begun_kernel, first, n_items, item_dev, n, at),
        in_specs=[VMEM] * (3 * n + len(more)),
        out_specs=VMEM,
        out_shape=struct((n_items // item_dev, item_dev * rank, rank), f32),
        compiler_params=params(32),
        cost_estimate=cost(0.082 * n * n_items),
        name="begun",
    )(*es, *us, *uts, *more)


def systems_kernel(first, n_items, item_dev, keep, n, done, at, *refs):
    m = n - done
    es, us, uts = refs[:n], refs[n : n + m], refs[n + m : n + 2 * m]
    start = refs[n + 2 * m] if done else None
    out = refs[-1]
    block_users, rank = us[0].shape
    rows = [some_rows(e, first, n_items, slice(0, block_users)) for e in es[done:]]
    rhs = jnp.zeros((n_items, rank), f32)
    for e in es:
        rhs = rhs + some_rows(e, first, n_items, slice(block_users, block_users + rank))
        rhs = rhs + some_rows(e, first, n_items, slice(block_users + rank, block_users + 2 * rank))
    row = lax.broadcasted_iota(i32, (64, rank), 0)
    lane = lax.broadcasted_iota(i32, (64, rank), 1)
    eye = lax.broadcasted_iota(i32, (rank, rank), 0) == lax.broadcasted_iota(i32, (rank, rank), 1)
    above = (lane < 64) & (lane > row)
    base = 64 * item_dev

    for c in range(n_items // item_dev):
        total = partial_systems(rows, uts, us, c, item_dev)
        if done:
            total = total + start[at + c]
        diag = []
        for j in range(item_dev):
            g = total[j * rank : (j + 1) * rank]
            packed = jnp.where(above, pltpu.roll(g[64:], 64, 1), g[:64])
            out[c, 64 * j : 64 * j + 64, :] = packed.astype(out.dtype)
            diag.append(jnp.sum(jnp.where(eye, g, 0.0), axis=0, keepdims=True))
        diag = jnp.concatenate(diag, 0)
        side = rhs[c * item_dev : (c + 1) * item_dev]
        put_extras(
            lambda a, n, v, c=c: out.__setitem__((c, slice(base + a, base + a + n)), v), diag, side, keep, item_dev
        )


def put_extras(put, diag, side, keep, item_dev):
    if keep:
        nil = jnp.zeros_like(diag)
        rows = [diag, nil, side, nil]
    else:
        rows = []
        for v in (diag, side):
            high = v.astype(bf16).astype(f32)
            rows += [high, v - high]
    pad = -4 * item_dev % 16
    if pad:
        rows.append(jnp.zeros((pad, diag.shape[1]), f32))
    value = jnp.concatenate(rows, 0)
    put(0, value.shape[0], value if keep else value.astype(bf16))


def systems(es, us, ut, first, n_items, item_dev, keep, start=None, done=0, at=0, us_cost=None):
    n = len(es)
    block_users, rank = us[0].shape
    more = [] if start is None else [start]
    return pl.pallas_call(
        functools.partial(systems_kernel, first, n_items, item_dev, keep, n, done, at),
        in_specs=[VMEM] * (3 * n - 2 * done + len(more)),
        out_specs=VMEM,
        out_shape=struct((n_items // item_dev, chunk_rows(item_dev), rank), f32 if keep else bf16),
        compiler_params=params(40),
        cost_estimate=cost(0.082 * (n - done) * n_items if us_cost is None else us_cost),
        name="systems",
    )(*es, *us[done:], *ut[done:], *more)


def extras(value, item_dev):
    base = 64 * item_dev
    part = [value[base + n * item_dev : base + (n + 1) * item_dev] for n in range(4)]
    return part[0] + part[1], part[2] + part[3]


def merge_kernel(item_dev, n_keep, apart, skip, own, got, *outs):
    kept, sent = outs[0], outs[bool(n_keep) :]
    base = 64 * item_dev
    for c in range(own.shape[0]):
        value = own[c] + got[c + skip].astype(f32)
        diag, side = extras(value, item_dev)
        if c < n_keep:
            kept[c, :base, :] = value[:base]
            put_extras(lambda a, n, v, c=c: kept.__setitem__((c, slice(base + a, base + a + n)), v), diag, side, True, item_dev)
        else:
            ref = sent[c - n_keep] if apart else sent[0]
            lead = () if apart else (c - n_keep,)
            ref[lead + (slice(0, base),)] = value[:base].astype(bf16)
            put_extras(
                lambda a, n, v, ref=ref, lead=lead: ref.__setitem__(lead + (slice(base + a, base + a + n),), v),
                diag, side, False, item_dev,
            )


def merged(own, got, item_dev, n_keep, apart, skip=0):
    chunks, rows, rank = own.shape
    n_sent = chunks - n_keep
    shapes = [struct((rows, rank), bf16)] * n_sent if apart else [struct((n_sent, rows, rank), bf16)]
    shapes = ([struct((n_keep, rows, rank), f32)] if n_keep else []) + shapes
    return pl.pallas_call(
        functools.partial(merge_kernel, item_dev, n_keep, apart, skip),
        in_specs=[VMEM] * 2,
        out_specs=[VMEM] * len(shapes),
        out_shape=shapes,
        compiler_params=params(16),
        name="merge",
    )(own, got)


def gradients_kernel(item_dev, own, *refs):
    *got, prev, out, half = refs
    value = own[0]
    for g in got:
        value = value + (g[...] if len(g.shape) == 2 else g[0]).astype(f32)
    rank = value.shape[1]
    diag, side = extras(value, item_dev)
    row = lax.broadcasted_iota(i32, (64, 64), 0)
    col = lax.broadcasted_iota(i32, (64, 64), 1)
    eye = lax.broadcasted_iota(i32, (rank, rank), 0) == lax.broadcasted_iota(i32, (rank, rank), 1)
    matrices = []
    for j in range(item_dev):
        m = value[64 * j : 64 * j + 64]
        t = m.T
        mix, mix_t = m[:, :64], t[:64]
        a = jnp.where(col < row, mix, mix_t)
        c = jnp.where(col > row, mix, mix_t)
        full = jnp.concatenate(
            [jnp.concatenate([a, m[:, 64:]], 1), jnp.concatenate([t[64:], c], 1)], 0
        )
        matrices.append(jnp.where(eye, diag[j : j + 1] + ridge_weight, full))

    solution = prev[...]
    residual_c = [
        jnp.sum(jnp.where(eye, side[j : j + 1], 0.0) - matrices[j] * solution[j : j + 1], axis=1, keepdims=True)
        for j in range(item_dev)
    ]
    residual = jnp.concatenate(
        [jnp.sum(jnp.where(eye, c, 0.0), axis=0, keepdims=True) for c in residual_c], 0
    )
    direction, direction_c = residual, residual_c
    norm_now = jnp.sum(residual * residual, axis=1, keepdims=True)
    for turn in range(CG_STEPS):
        image = jnp.concatenate(
            [jnp.sum(m * c, axis=0, keepdims=True) for m, c in zip(matrices, direction_c)], 0
        )
        step = norm_now / jnp.sum(direction * image, axis=1, keepdims=True)
        solution = solution + step * direction
        if turn == CG_STEPS - 1:
            break
        residual = residual - step * image
        norm_next = jnp.sum(residual * residual, axis=1, keepdims=True)
        again = norm_next / norm_now
        image_c = [
            jnp.sum(matrices[j] * direction[j : j + 1], axis=1, keepdims=True) for j in range(item_dev)
        ]
        residual_c = [c - step[j : j + 1] * i for j, (c, i) in enumerate(zip(residual_c, image_c))]
        direction_c = [c + again[j : j + 1] * d for j, (c, d) in enumerate(zip(residual_c, direction_c))]
        direction = residual + again * direction
        norm_now = norm_next
    out[...] = solution
    short = solution.astype(bf16)
    for d in range(half.shape[0]):
        half[d] = short


def gradients(own, got, prev, devices):
    item_dev, rank = prev.shape
    return pl.pallas_call(
        functools.partial(gradients_kernel, item_dev),
        in_specs=[VMEM] * (2 + len(got)),
        out_specs=[VMEM] * 2,
        out_shape=[struct(prev.shape, f32), struct((devices,) + prev.shape, bf16)],
        compiler_params=params(16),
        cost_estimate=cost(2),
        name="gradients",
    )(own, *got, prev)


def summed_kernel(own, *refs):
    *got, out = refs
    value = own[0]
    for g in got:
        value = value + (g[...] if len(g.shape) == 2 else g[0]).astype(f32)
    out[0] = value


def summed(own, got):
    return pl.pallas_call(
        summed_kernel,
        in_specs=[VMEM] * (1 + len(got)),
        out_specs=VMEM,
        out_shape=struct(own.shape, f32),
        compiler_params=params(16),
        cost_estimate=cost(8),
        name="summed",
    )(own, *got)


def user_side_kernel(item_dev, n_grp, n_user, me_s, returned, c_both, out, rows, order, made, sem):
    num_items = returned.shape[0]
    rows[...] = returned[...].astype(f32)
    me = me_s[0]
    for group in range(num_items // item_dev):
        owner = owner_of(group, item_dev, n_grp, n_user) ^ me
        order[group * item_dev : (group + 1) * item_dev, :] = rows[pl.ds(owner * item_dev, item_dev), :]
    ret = order[...].astype(bf16)
    ret = jnp.concatenate([ret, ret], 0)
    copies = []
    for c in range(made.shape[0]):
        rows_c = slice(c * made.shape[1], (c + 1) * made.shape[1])
        made[c] = jnp.dot(c_both[rows_c], ret, preferred_element_type=f32)
        copies.append(pltpu.make_async_copy(made.at[c], out.at[rows_c], sem.at[c]))
        copies[-1].start()
    for copy in copies:
        copy.wait()


def user_side(me, returned, c_both, item_dev, n_grp, n_user):
    num_items, rank = returned.shape
    pieces = 4
    return pl.pallas_call(
        functools.partial(user_side_kernel, item_dev, n_grp, n_user),
        in_specs=[SMEM, VMEM, VMEM],
        out_specs=pl.BlockSpec(memory_space=pltpu.HBM),
        out_shape=struct((c_both.shape[0], rank), f32),
        scratch_shapes=[pltpu.VMEM((num_items, rank), f32)] * 2
        + [pltpu.VMEM((pieces, c_both.shape[0] // pieces, rank), f32), pltpu.SemaphoreType.DMA((pieces,))],
        compiler_params=params(16),
        cost_estimate=cost(1),
        name="user_side",
    )(me, returned, c_both)


def flip_kernel(a, b, out):
    items = a.shape[0]
    for n, v in enumerate((a, b)):
        for c in range(a.shape[1] // 128):
            out[c * 128 : (c + 1) * 128, n * items : (n + 1) * items] = v[:, c * 128 : (c + 1) * 128].T


def flipped(c_hi, c_lo):
    return pl.pallas_call(
        flip_kernel,
        in_specs=[VMEM] * 2,
        out_specs=VMEM,
        out_shape=struct((c_hi.shape[1], 2 * c_hi.shape[0]), bf16),
        compiler_params=params(16),
        cost_estimate=cost(0.01),
        name="flip",
    )(c_hi, c_lo)


def shards(user_factors, tile_user, tile_count, tile_valid, tile_item, prev_items):
    n_user = lax.axis_size("user")
    n_grp = lax.axis_size("grp")
    devices = n_user * n_grp
    item_dev, rank = prev_items.shape
    num_items = item_dev * devices
    assert n_grp == 4 and n_user >= 4 and rank == 128 and user_factors.shape[0] == 1024
    me = lax.axis_index(AXES).astype(i32).reshape(1)

    def swap(value, bit):
        return lax.ppermute(value, AXES, [(d, d ^ bit) for d in range(devices)])

    u0 = user_factors
    u2 = swap(u0, 2)
    u1 = swap(u0, 1)
    *es, c_hi, c_lo, prev, ut0 = histogram(
        me, tile_valid, tile_item, tile_user, tile_count, u0, prev_items, num_items, item_dev, n_grp, n_user
    )
    c_both = flipped(c_hi, c_lo)
    u2, c_both = lax.optimization_barrier((u2, c_both))
    u3 = swap(u2, 1)
    got = [es[0], swap(es[1], 1), swap(es[2], 2), swap(es[3], 3)]
    us = [u0, u1, u2, u3]
    ut = [ut0] + [transposed(u) for u in us[1:]]
    n_items = num_items // n_grp
    n_half = n_items // 2
    start = begun(got[:2], us[:2], ut[:2], n_half, n_half, item_dev)
    if n_user == 8:
        n_far = n_half // 2
        chunks = n_far // item_dev
        first = begun(got[2:3], us[2:3], ut[2:3], n_half + n_far, n_far, item_dev, start, chunks)
        sent = systems(got, us, ut, n_half + n_far, n_far, item_dev, False, first, 3, 0)
        far_other = swap(sent, n_grp)
        ut[0], _ = lax.optimization_barrier((ut[0], sent))
        sent = systems(got, us, ut, n_half, n_far, item_dev, False, start, 2, 0)
        near_other = swap(sent, n_grp)
        ut[0], _ = lax.optimization_barrier((ut[0], sent))
        own = systems(got, us, ut, n_far, n_far, item_dev, True, us_cost=0.01)
        far = merged(own, far_other, item_dev, 0, True)
        parts = [swap(value, n_grp * 2 * (chunks + n)) for n, value in reversed(list(enumerate(far)))]
        ut[0], _ = lax.optimization_barrier((ut[0], far[0]))
        own = systems(got, us, ut, item_dev, n_far - item_dev, item_dev, True)
        near = merged(own, near_other, item_dev, 0, True, 1)
        parts += [swap(value, n_grp * 2 * (n + 1)) for n, value in enumerate(near)]
        ut[0], _ = lax.optimization_barrier((ut[0], own))
        own = systems(got, us, ut, 0, item_dev, item_dev, True)
        own = summed(own, [near_other] + parts[:-1])
        parts = parts[-1:]
    else:
        left, bit = n_user, n_grp
        sent = systems(got, us, ut, n_half, n_half, item_dev, False, start, 2)
        other = swap(sent, bit)
        own = systems(got, us, ut, 0, n_half, item_dev, True)
        left, bit = left // 2, bit * 2
        while left > 4:
            own, sent = merged(own, other, item_dev, left // 2, False)
            other = swap(sent, bit)
            left, bit = left // 2, bit * 2
        own, *sent = merged(own, other, item_dev, 1, True)
        parts = [swap(value, bit * (n + 1)) for n, value in enumerate(sent)]
    solved, spread = gradients(own, parts, prev, devices)
    returned = lax.all_to_all(spread, AXES, 0, 0, tiled=True).reshape(num_items, rank)
    return solved, user_side(me, returned, c_both, item_dev, n_grp, n_user)


def solution(mesh):
    return jax.shard_map(
        shards,
        mesh=mesh,
        in_specs=(
            P(AXES, None),
            P(AXES, None, None),
            P(AXES, None, None),
            P(AXES, None),
            P(AXES, None),
            P(AXES, None),
        ),
        out_specs=(P(AXES, None), P(AXES, None)),
        check_vma=False,
    )
```

```python
import functools

import jax
import jax.numpy as jnp
from jax import lax
from jax.experimental import pallas as pl
from jax.experimental.pallas import tpu as pltpu
from jax.sharding import PartitionSpec as P

CG_STEPS = 4
bf16, f32, i32 = jnp.bfloat16, jnp.float32, jnp.int32
AXES = ("user", "grp")
VMEM = pl.BlockSpec(memory_space=pltpu.VMEM)
SMEM = pl.BlockSpec(memory_space=pltpu.SMEM)
struct = jax.ShapeDtypeStruct

confidence_rate = 0.5
ridge_weight = 1.0


def log2(n):
    k = n.bit_length() - 1
    assert 1 << k == n
    return k


def cost(us):
    return pl.CostEstimate(flops=int(us * 1e9), bytes_accessed=int(us * 3e6), transcendentals=0)


def params(mib):
    return pltpu.CompilerParams(vmem_limit_bytes=mib << 20)


def slot_of(item, me, item_dev, n_grp, n_user):
    rel = (item >> log2(item_dev)) ^ me
    slot = item & (item_dev - 1)
    w = rel >> log2(n_grp)
    per, left = n_user * item_dev, n_user
    k = (rel & (n_grp - 1)) * per
    while left > 4:
        per, left = per // 2, left // 2
        k = k + (w & 1) * per
        w = w >> 1
    return k + w * item_dev + slot


def owner_of(group, item_dev, n_grp, n_user):
    k, w = divmod(group, n_user)
    bits, left, at = 0, n_user, 0
    while left > 4:
        left //= 2
        bits |= (w // left) << at
        w %= left
        at += 1
    return (bits | (w << at)) * n_grp + k


def histogram_kernel(step, low_part, item_dev, n_grp, n_user, me_s, *refs):
    sources, rest = refs[:6], refs[6:]
    eouts = rest[:n_grp]
    c_hi, c_lo, prev_here, ut, acc, *here, sem = rest[n_grp:]
    here.append(prev_here)
    copies = [pltpu.make_async_copy(a, b, sem.at[n]) for n, (a, b) in enumerate(zip(sources, here))]
    for copy in copies:
        copy.start()
    valid_s, item_s, users, counts, u, _ = here
    tiles, rows = users.shape[1:]
    num_items = c_hi.shape[0]
    block_users = u.shape[0]
    his = block_users // low_part
    kinds = 2 * his
    pitch = kinds + 8
    me = me_s[0]
    for copy in copies[:4]:
        copy.wait()
    lane = lax.broadcasted_iota(i32, (his, rows), 1)
    sub = lax.broadcasted_iota(i32, (his, rows), 0)
    iota = lax.broadcasted_iota(i32, (low_part, rows), 0).astype(f32).astype(bf16)
    zero = jnp.zeros((kinds, rows), bf16)
    one, nil = jnp.ones((low_part, rows), bf16), jnp.zeros((low_part, rows), bf16)

    def body(b, run):
        base = pl.multiple_of(b * step, step)
        blk = users[0, pl.ds(base, step), :]
        cnt = counts[0, pl.ds(base, step), :].astype(f32) * confidence_rate
        lo = (blk & (low_part - 1)).astype(f32)
        hi = blk >> log2(low_part)
        for t in range(0, step, 2):
            oh, lhs = [], []
            for j in (t, t + 1):
                lob = jnp.broadcast_to(lo[j : j + 1], (16, rows)).astype(bf16)
                oh.append(jnp.where(jnp.concatenate([lob] * (low_part // 16), 0) == iota, one, nil))
                on = (lane < valid_s[0, base + j]) & (jnp.broadcast_to(hi[j : j + 1], (his, rows)) == sub)
                ex = jnp.broadcast_to(cnt[j : j + 1], (his, rows))
                lhs.append(
                    jnp.concatenate([jnp.where(on, ex, 0.0), jnp.where(on, 1.0 + ex, 0.0)], 0).astype(bf16)
                )
            left = jnp.concatenate(
                [jnp.concatenate([lhs[0], zero], 1), jnp.concatenate([zero, lhs[1]], 1)], 0
            )
            out = lax.dot_general(
                left, jnp.concatenate(oh, 1), (((1,), (1,)), ((), ())), preferred_element_type=f32
            )
            for q, j in enumerate((t, t + 1)):
                item, before = item_s[0, base + j], item_s[0, jnp.maximum(base + j - 1, 0)]
                run = jnp.where(item == before, 1.0, 0.0) * run + out[kinds * q : kinds * (q + 1)]
                p = slot_of(item, me, item_dev, n_grp, n_user)
                acc[pl.ds(pl.multiple_of(p * pitch, 8), kinds), :] = run
        return run

    lax.fori_loop(0, tiles // step, body, jnp.zeros((kinds, low_part), f32))
    copies[4].wait()
    copies[5].wait()
    transpose_kernel(u, ut)
    per = num_items // n_grp
    wide = 128 // low_part

    def row(h):
        parts = [acc[pl.ds(h * wide + n, num_items, stride=pitch), :] for n in range(wide)]
        return jnp.concatenate(parts, 1)

    for h in range(block_users // 128):
        e = (row(h) + 1.0).astype(bf16)
        for k in range(n_grp):
            eouts[k][:, h * 128 : (h + 1) * 128] = e[k * per : (k + 1) * per]
        c = row(his // wide + h)
        ch = c.astype(bf16)
        c_hi[:, h * 128 : (h + 1) * 128] = ch
        c_lo[:, h * 128 : (h + 1) * 128] = (c - ch.astype(f32)).astype(bf16)
    uu = u[...]
    r = jnp.dot(c_hi[...], uu, preferred_element_type=f32) + jnp.dot(c_lo[...], uu, preferred_element_type=f32)
    rh = r.astype(bf16)
    rl = (r - rh.astype(f32)).astype(bf16)
    for k in range(n_grp):
        eouts[k][:, block_users : block_users + 128] = rh[k * per : (k + 1) * per]
        eouts[k][:, block_users + 128 :] = rl[k * per : (k + 1) * per]


def histogram(me, valid, item, users, counts, u, prev, num_items, item_dev, n_grp, n_user):
    block_users, rank = u.shape
    step, low_part = 192, 64
    assert users.shape[1] % step == 0
    return pl.pallas_call(
        functools.partial(histogram_kernel, step, low_part, item_dev, n_grp, n_user),
        in_specs=[SMEM] + [pl.BlockSpec(memory_space=pltpu.HBM)] * 6,
        out_specs=[VMEM] * (n_grp + 4),
        out_shape=[struct((num_items // n_grp, block_users + 2 * rank), bf16)] * n_grp
        + [struct((num_items, block_users), bf16)] * 2
        + [struct(prev.shape, f32), struct((rank, block_users), bf16)],
        scratch_shapes=[
            pltpu.VMEM((num_items * (2 * block_users // low_part + 8), low_part), f32),
            pltpu.SMEM(valid.shape, i32),
            pltpu.SMEM(item.shape, i32),
            pltpu.VMEM(users.shape, i32),
            pltpu.VMEM(counts.shape, i32),
            pltpu.VMEM(u.shape, bf16),
            pltpu.SemaphoreType.DMA((6,)),
        ],
        compiler_params=params(32),
        cost_estimate=cost(7),
        name="histogram",
    )(me, *[pltpu.with_memory_space_constraint(v, pltpu.HBM) for v in (valid, item, users, counts, u, prev)])


def transpose_kernel(u, ut):
    for c in range(u.shape[0] // 128):
        ut[:, c * 128 : (c + 1) * 128] = u[c * 128 : (c + 1) * 128, :].T


def transposed(u):
    return pl.pallas_call(
        transpose_kernel,
        in_specs=[VMEM],
        out_specs=VMEM,
        out_shape=struct(u.shape[::-1], bf16),
        compiler_params=params(16),
        cost_estimate=cost(0.1),
        name="transpose",
    )(u)


def chunk_rows(item_dev):
    return 64 * item_dev + -(-4 * item_dev // 16) * 16


def partial_systems(rows, uts, us, c, item_dev):
    rank = uts[0].shape[0]
    ut = jnp.concatenate([t[...] for t in uts], 1)
    w = []
    for j in range(item_dev):
        one = c * item_dev + j
        e = jnp.concatenate([r[one : one + 1] for r in rows], 1)
        e = jnp.broadcast_to(e, (16, e.shape[1])).astype(bf16)
        w.append(jnp.concatenate([e] * (rank // 16), 0) * ut)
    return jnp.dot(jnp.concatenate(w, 0), jnp.concatenate([u[...] for u in us], 0), preferred_element_type=f32)


def some_rows(ref, first, n, cols):
    low, high = first // 16 * 16, -(-(first + n) // 16) * 16
    return ref[low:high, cols].astype(f32)[first - low : first - low + n]


def begun_kernel(first, n_items, item_dev, n, at, *refs):
    es, us, uts, out = refs[:n], refs[n : 2 * n], refs[2 * n : 3 * n], refs[-1]
    more = refs[3 * n : -1]
    rows = [some_rows(e, first, n_items, slice(0, us[0].shape[0])) for e in es]
    for c in range(n_items // item_dev):
        total = partial_systems(rows, uts, us, c, item_dev)
        out[c] = total + more[0][at + c] if more else total


def begun(es, us, uts, first, n_items, item_dev, start=None, at=0):
    more = [] if start is None else [start]
    n = len(es)
    block_users, rank = us[0].shape
    return pl.pallas_call(
        functools.partial(begun_kernel, first, n_items, item_dev, n, at),
        in_specs=[VMEM] * (3 * n + len(more)),
        out_specs=VMEM,
        out_shape=struct((n_items // item_dev, item_dev * rank, rank), f32),
        compiler_params=params(32),
        cost_estimate=cost(0.082 * n * n_items),
        name="begun",
    )(*es, *us, *uts, *more)


def systems_kernel(first, n_items, item_dev, keep, n, done, at, *refs):
    m = n - done
    es, us, uts = refs[:n], refs[n : n + m], refs[n + m : n + 2 * m]
    start = refs[n + 2 * m] if done else None
    out = refs[-1]
    block_users, rank = us[0].shape
    rows = [some_rows(e, first, n_items, slice(0, block_users)) for e in es[done:]]
    rhs = jnp.zeros((n_items, rank), f32)
    for e in es:
        rhs = rhs + some_rows(e, first, n_items, slice(block_users, block_users + rank))
        rhs = rhs + some_rows(e, first, n_items, slice(block_users + rank, block_users + 2 * rank))
    row = lax.broadcasted_iota(i32, (64, rank), 0)
    lane = lax.broadcasted_iota(i32, (64, rank), 1)
    eye = lax.broadcasted_iota(i32, (rank, rank), 0) == lax.broadcasted_iota(i32, (rank, rank), 1)
    above = (lane < 64) & (lane > row)
    base = 64 * item_dev

    for c in range(n_items // item_dev):
        total = partial_systems(rows, uts, us, c, item_dev)
        if done:
            total = total + start[at + c]
        diag = []
        for j in range(item_dev):
            g = total[j * rank : (j + 1) * rank]
            packed = jnp.where(above, pltpu.roll(g[64:], 64, 1), g[:64])
            out[c, 64 * j : 64 * j + 64, :] = packed.astype(out.dtype)
            diag.append(jnp.sum(jnp.where(eye, g, 0.0), axis=0, keepdims=True))
        diag = jnp.concatenate(diag, 0)
        side = rhs[c * item_dev : (c + 1) * item_dev]
        put_extras(
            lambda a, n, v, c=c: out.__setitem__((c, slice(base + a, base + a + n)), v), diag, side, keep, item_dev
        )


def put_extras(put, diag, side, keep, item_dev):
    if keep:
        nil = jnp.zeros_like(diag)
        rows = [diag, nil, side, nil]
    else:
        rows = []
        for v in (diag, side):
            high = v.astype(bf16).astype(f32)
            rows += [high, v - high]
    pad = -4 * item_dev % 16
    if pad:
        rows.append(jnp.zeros((pad, diag.shape[1]), f32))
    value = jnp.concatenate(rows, 0)
    put(0, value.shape[0], value if keep else value.astype(bf16))


def systems(es, us, ut, first, n_items, item_dev, keep, start=None, done=0, at=0, us_cost=None):
    n = len(es)
    block_users, rank = us[0].shape
    more = [] if start is None else [start]
    return pl.pallas_call(
        functools.partial(systems_kernel, first, n_items, item_dev, keep, n, done, at),
        in_specs=[VMEM] * (3 * n - 2 * done + len(more)),
        out_specs=VMEM,
        out_shape=struct((n_items // item_dev, chunk_rows(item_dev), rank), f32 if keep else bf16),
        compiler_params=params(40),
        cost_estimate=cost(0.082 * (n - done) * n_items if us_cost is None else us_cost),
        name="systems",
    )(*es, *us[done:], *ut[done:], *more)


def extras(value, item_dev):
    base = 64 * item_dev
    part = [value[base + n * item_dev : base + (n + 1) * item_dev] for n in range(4)]
    return part[0] + part[1], part[2] + part[3]


def merge_kernel(item_dev, n_keep, apart, skip, own, got, *outs):
    kept, sent = outs[0], outs[bool(n_keep) :]
    base = 64 * item_dev
    for c in range(own.shape[0]):
        value = own[c] + got[c + skip].astype(f32)
        diag, side = extras(value, item_dev)
        if c < n_keep:
            kept[c, :base, :] = value[:base]
            put_extras(lambda a, n, v, c=c: kept.__setitem__((c, slice(base + a, base + a + n)), v), diag, side, True, item_dev)
        else:
            ref = sent[c - n_keep] if apart else sent[0]
            lead = () if apart else (c - n_keep,)
            ref[lead + (slice(0, base),)] = value[:base].astype(bf16)
            put_extras(
                lambda a, n, v, ref=ref, lead=lead: ref.__setitem__(lead + (slice(base + a, base + a + n),), v),
                diag, side, False, item_dev,
            )


def merged(own, got, item_dev, n_keep, apart, skip=0):
    chunks, rows, rank = own.shape
    n_sent = chunks - n_keep
    shapes = [struct((rows, rank), bf16)] * n_sent if apart else [struct((n_sent, rows, rank), bf16)]
    shapes = ([struct((n_keep, rows, rank), f32)] if n_keep else []) + shapes
    return pl.pallas_call(
        functools.partial(merge_kernel, item_dev, n_keep, apart, skip),
        in_specs=[VMEM] * 2,
        out_specs=[VMEM] * len(shapes),
        out_shape=shapes,
        compiler_params=params(16),
        name="merge",
    )(own, got)


def gradients_kernel(item_dev, own, *refs):
    *got, prev, out, half = refs
    value = own[0]
    for g in got:
        value = value + (g[...] if len(g.shape) == 2 else g[0]).astype(f32)
    rank = value.shape[1]
    diag, side = extras(value, item_dev)
    row = lax.broadcasted_iota(i32, (64, 64), 0)
    col = lax.broadcasted_iota(i32, (64, 64), 1)
    eye = lax.broadcasted_iota(i32, (rank, rank), 0) == lax.broadcasted_iota(i32, (rank, rank), 1)
    matrices = []
    for j in range(item_dev):
        m = value[64 * j : 64 * j + 64]
        t = m.T
        mix, mix_t = m[:, :64], t[:64]
        a = jnp.where(col < row, mix, mix_t)
        c = jnp.where(col > row, mix, mix_t)
        full = jnp.concatenate(
            [jnp.concatenate([a, m[:, 64:]], 1), jnp.concatenate([t[64:], c], 1)], 0
        )
        matrices.append(jnp.where(eye, diag[j : j + 1] + ridge_weight, full))

    solution = prev[...]
    residual_c = [
        jnp.sum(jnp.where(eye, side[j : j + 1], 0.0) - matrices[j] * solution[j : j + 1], axis=1, keepdims=True)
        for j in range(item_dev)
    ]
    residual = jnp.concatenate(
        [jnp.sum(jnp.where(eye, c, 0.0), axis=0, keepdims=True) for c in residual_c], 0
    )
    direction, direction_c = residual, residual_c
    norm_now = jnp.sum(residual * residual, axis=1, keepdims=True)
    for turn in range(CG_STEPS):
        image = jnp.concatenate(
            [jnp.sum(m * c, axis=0, keepdims=True) for m, c in zip(matrices, direction_c)], 0
        )
        step = norm_now / jnp.sum(direction * image, axis=1, keepdims=True)
        solution = solution + step * direction
        if turn == CG_STEPS - 1:
            break
        residual = residual - step * image
        norm_next = jnp.sum(residual * residual, axis=1, keepdims=True)
        again = norm_next / norm_now
        image_c = [
            jnp.sum(matrices[j] * direction[j : j + 1], axis=1, keepdims=True) for j in range(item_dev)
        ]
        residual_c = [c - step[j : j + 1] * i for j, (c, i) in enumerate(zip(residual_c, image_c))]
        direction_c = [c + again[j : j + 1] * d for j, (c, d) in enumerate(zip(residual_c, direction_c))]
        direction = residual + again * direction
        norm_now = norm_next
    out[...] = solution
    short = solution.astype(bf16)
    for d in range(half.shape[0]):
        half[d] = short


def gradients(own, got, prev, devices):
    item_dev, rank = prev.shape
    return pl.pallas_call(
        functools.partial(gradients_kernel, item_dev),
        in_specs=[VMEM] * (2 + len(got)),
        out_specs=[VMEM] * 2,
        out_shape=[struct(prev.shape, f32), struct((devices,) + prev.shape, bf16)],
        compiler_params=params(16),
        cost_estimate=cost(2),
        name="gradients",
    )(own, *got, prev)


def summed_kernel(own, *refs):
    *got, out = refs
    value = own[0]
    for g in got:
        value = value + (g[...] if len(g.shape) == 2 else g[0]).astype(f32)
    out[0] = value


def summed(own, got):
    return pl.pallas_call(
        summed_kernel,
        in_specs=[VMEM] * (1 + len(got)),
        out_specs=VMEM,
        out_shape=struct(own.shape, f32),
        compiler_params=params(16),
        cost_estimate=cost(8),
        name="summed",
    )(own, *got)


def user_side_kernel(item_dev, n_grp, n_user, me_s, returned, c_both, out, rows, order, made, sem):
    num_items = returned.shape[0]
    rows[...] = returned[...].astype(f32)
    me = me_s[0]
    for group in range(num_items // item_dev):
        owner = owner_of(group, item_dev, n_grp, n_user) ^ me
        order[group * item_dev : (group + 1) * item_dev, :] = rows[pl.ds(owner * item_dev, item_dev), :]
    ret = order[...].astype(bf16)
    ret = jnp.concatenate([ret, ret], 0)
    copies = []
    for c in range(made.shape[0]):
        rows_c = slice(c * made.shape[1], (c + 1) * made.shape[1])
        made[c] = jnp.dot(c_both[rows_c], ret, preferred_element_type=f32)
        copies.append(pltpu.make_async_copy(made.at[c], out.at[rows_c], sem.at[c]))
        copies[-1].start()
    for copy in copies:
        copy.wait()


def user_side(me, returned, c_both, item_dev, n_grp, n_user):
    num_items, rank = returned.shape
    pieces = 8
    return pl.pallas_call(
        functools.partial(user_side_kernel, item_dev, n_grp, n_user),
        in_specs=[SMEM, VMEM, VMEM],
        out_specs=pl.BlockSpec(memory_space=pltpu.HBM),
        out_shape=struct((c_both.shape[0], rank), f32),
        scratch_shapes=[pltpu.VMEM((num_items, rank), f32)] * 2
        + [pltpu.VMEM((pieces, c_both.shape[0] // pieces, rank), f32), pltpu.SemaphoreType.DMA((pieces,))],
        compiler_params=params(16),
        cost_estimate=cost(1),
        name="user_side",
    )(me, returned, c_both)


def flip_kernel(a, b, out):
    items = a.shape[0]
    for n, v in enumerate((a, b)):
        for c in range(a.shape[1] // 128):
            out[c * 128 : (c + 1) * 128, n * items : (n + 1) * items] = v[:, c * 128 : (c + 1) * 128].T


def flipped(c_hi, c_lo):
    return pl.pallas_call(
        flip_kernel,
        in_specs=[VMEM] * 2,
        out_specs=VMEM,
        out_shape=struct((c_hi.shape[1], 2 * c_hi.shape[0]), bf16),
        compiler_params=params(16),
        cost_estimate=cost(0.01),
        name="flip",
    )(c_hi, c_lo)


def shards(user_factors, tile_user, tile_count, tile_valid, tile_item, prev_items):
    n_user = lax.axis_size("user")
    n_grp = lax.axis_size("grp")
    devices = n_user * n_grp
    item_dev, rank = prev_items.shape
    num_items = item_dev * devices
    assert n_grp == 4 and n_user >= 4 and rank == 128 and user_factors.shape[0] == 1024
    me = lax.axis_index(AXES).astype(i32).reshape(1)

    def swap(value, bit):
        return lax.ppermute(value, AXES, [(d, d ^ bit) for d in range(devices)])

    u0 = user_factors
    u2 = swap(u0, 2)
    u1 = swap(u0, 1)
    *es, c_hi, c_lo, prev, ut0 = histogram(
        me, tile_valid, tile_item, tile_user, tile_count, u0, prev_items, num_items, item_dev, n_grp, n_user
    )
    c_both = flipped(c_hi, c_lo)
    u2, c_both = lax.optimization_barrier((u2, c_both))
    u3 = swap(u2, 1)
    got = [es[0], swap(es[1], 1), swap(es[2], 2), swap(es[3], 3)]
    us = [u0, u1, u2, u3]
    ut = [ut0] + [transposed(u) for u in us[1:]]
    n_items = num_items // n_grp
    n_half = n_items // 2
    start = begun(got[:2], us[:2], ut[:2], n_half, n_half, item_dev)
    if n_user == 8:
        n_far = n_half // 2
        chunks = n_far // item_dev
        first = begun(got[2:3], us[2:3], ut[2:3], n_half + n_far, n_far, item_dev, start, chunks)
        sent = systems(got, us, ut, n_half + n_far, n_far, item_dev, False, first, 3, 0)
        far_other = swap(sent, n_grp)
        ut[0], _ = lax.optimization_barrier((ut[0], sent))
        sent = systems(got, us, ut, n_half, n_far, item_dev, False, start, 2, 0)
        near_other = swap(sent, n_grp)
        ut[0], _ = lax.optimization_barrier((ut[0], sent))
        own = systems(got, us, ut, n_far, n_far, item_dev, True, us_cost=0.01)
        far = merged(own, far_other, item_dev, 0, True)
        parts = [swap(value, n_grp * 2 * (chunks + n)) for n, value in reversed(list(enumerate(far)))]
        ut[0], _ = lax.optimization_barrier((ut[0], far[0]))
        own = systems(got, us, ut, item_dev, n_far - item_dev, item_dev, True)
        near = merged(own, near_other, item_dev, 0, True, 1)
        parts += [swap(value, n_grp * 2 * (n + 1)) for n, value in enumerate(near)]
        ut[0], _ = lax.optimization_barrier((ut[0], own))
        own = systems(got, us, ut, 0, item_dev, item_dev, True)
        own = summed(own, [near_other] + parts[:-1])
        parts = parts[-1:]
    else:
        left, bit = n_user, n_grp
        sent = systems(got, us, ut, n_half, n_half, item_dev, False, start, 2)
        other = swap(sent, bit)
        own = systems(got, us, ut, 0, n_half, item_dev, True)
        left, bit = left // 2, bit * 2
        while left > 4:
            own, sent = merged(own, other, item_dev, left // 2, False)
            other = swap(sent, bit)
            left, bit = left // 2, bit * 2
        own, *sent = merged(own, other, item_dev, 1, True)
        parts = [swap(value, bit * (n + 1)) for n, value in enumerate(sent)]
    solved, spread = gradients(own, parts, prev, devices)
    returned = lax.all_to_all(spread, AXES, 0, 0, tiled=True).reshape(num_items, rank)
    return solved, user_side(me, returned, c_both, item_dev, n_grp, n_user)


def solution(mesh):
    return jax.shard_map(
        shards,
        mesh=mesh,
        in_specs=(
            P(AXES, None),
            P(AXES, None, None),
            P(AXES, None, None),
            P(AXES, None),
            P(AXES, None),
            P(AXES, None),
        ),
        out_specs=(P(AXES, None), P(AXES, None)),
        check_vma=False,
    )
```
